32 devices in a mesh: tm: 16 (over z, y, x), det: 2 (over core).
Axes of the slice: x: 2, y: 2, z: 4, core: 2. Of those that a mesh axis runs over, the one named last changes fastest.
Arguments:
- offset_coeffs: float32 [16, 32], P('det', 'tm'), may hold values from -6 to 6
- leftover_error: float32 [16, 32], P('det', 'tm'), may hold values from -22 to 22
- search_vector: float32 [16, 32], P('det', 'tm'), may hold values from -22 to 22
- node_lattice_offset: int32 [16], P('det'), may hold values from 0 to 1023
- sky_cell_in_patch: int32 [16, 32768], P('det', 'tm'), may hold values from 0 to 127
- analyser_reading_phase: float32 [16, 32768], P('det', 'tm'), may hold values from -3.140625 to 3.140625
- segment_sky_patch: int32 [16, 256], P('det', 'tm'), may hold values from 0 to 16383, as said below
Outputs:
- fresh_offset_coeffs: float32 [16, 32], P('det', 'tm')
- fresh_leftover_error: float32 [16, 32], P('det', 'tm')
- fresh_search_vector: float32 [16, 32], P('det', 'tm')
The draws below stay inside these ranges and needn't reach their ends.
Inputs may be any that keep to these rules, and one draw needn't show every extreme that they name: `segment_sky_patch`: tile t belongs to owner t // 1024. Among the blocks of one device (8 detectors, one time span), at most 16 lie in tiles of one owner, and on every device some owner holds exactly 16 of them.
All inputs are finite; a program needn't handle non-finite values.
Results may differ from the reference program's by a relative error of at most 0.0001.
Values sent between devices are 32-bit elements; how exact they have to be, the bound alone decides.
No kernel may reach another device: no remote copies, remote signals or barrier semaphores. Data moves between devices by JAX's collectives and lax.ppermute only.
A program may use at most 64 MiB of HBM per device.

```python
import jax
import jax.numpy as jnp

DET_DEV = 8
SAMP_DEV = 2048
PIX_OWN = 131072
SENSOR_COUNT = 16
TIME = 32768
NODES_AROUND = 32
NPIX = 2097152
SPACING = 1024


def scaled_field(key, salt):
    key = jax.random.fold_in(key, salt)
    base_key, scale_key = jax.random.split(key, 2)
    ramp = jnp.arange(NODES_AROUND, dtype=jnp.float32)[None, :] / NODES_AROUND
    spread = 10.0 ** (jax.random.uniform(scale_key, (SENSOR_COUNT, 1), jnp.float32) - 0.5)
    scale = spread * 3.0 ** (ramp - 0.5)
    base = jnp.clip(jax.random.normal(base_key, (SENSOR_COUNT, NODES_AROUND), jnp.float32), -4.0, 4.0)
    return base * scale


def draw_leftover_error(key, part):
    return scaled_field(key, 11)


def draw_search_vector(key, part):
    return scaled_field(key, 23)


def draw_segment_sky_patch(key, part):
    ranks = TIME // SAMP_DEV
    groups = SENSOR_COUNT // DET_DEV
    blocks_here = DET_DEV * (SAMP_DEV // 128)
    capacity = max(2, 2 * blocks_here // ranks)
    owner_tiles = PIX_OWN // 128
    slot_total = ranks * capacity
    slot_owner = jnp.arange(slot_total, dtype=jnp.int32) // capacity

    def one_device(device):
        device_key = jax.random.fold_in(jax.random.fold_in(key, 7), device)
        full_key, order_key, shuffle_key, tile_key = jax.random.split(device_key, 4)
        full_owner = jax.random.randint(full_key, (), 0, ranks, dtype=jnp.int32)
        full_owner = jnp.where(device == 0, ranks - 1, jnp.where(device == 1, 0, full_owner))
        order = jax.random.permutation(order_key, slot_total).astype(jnp.int32)
        scores = order - jnp.where(slot_owner == full_owner, slot_total, 0)
        chosen = jnp.argsort(scores, stable=True)[:blocks_here]
        owners = slot_owner[chosen]
        local_tiles = jax.random.randint(tile_key, (blocks_here,), 0, owner_tiles, dtype=jnp.int32)
        edge_tile = jnp.where(device == 0, owner_tiles - 1, jnp.where(device == 1, 0, local_tiles[0]))
        local_tiles = local_tiles.at[0].set(edge_tile)
        shuffle = jax.random.permutation(shuffle_key, blocks_here)
        tiles = owners[shuffle] * owner_tiles + local_tiles[shuffle]
        return tiles.reshape(DET_DEV, blocks_here // DET_DEV)
    every = jax.vmap(one_device)(jnp.arange(groups * ranks, dtype=jnp.int32))
    every = every.reshape(groups, ranks, DET_DEV, SAMP_DEV // 128)
    every = jnp.transpose(every, (0, 2, 1, 3))
    return every.reshape(SENSOR_COUNT, TIME // 128).astype(jnp.int32)


def set_ends(result, rng, low, largest):
    place = [jax.random.randint(jax.random.fold_in(rng, axis), (), 0, length) for axis, length in enumerate(result.shape)]
    widest = result.shape.index(max(result.shape))
    neighbour = place[:widest] + [(place[widest] + 1) % result.shape[widest]] + place[widest + 1:]
    return result.at[tuple(place)].set(low).at[tuple(neighbour)].set(largest)


def steps_of(own_key, shape, shards, least, largest):
    loudness, own = 1.0, jax.random.fold_in(own_key, 6)
    for position, blocks in shards:
        steps = jnp.exp(jax.random.uniform(jax.random.fold_in(own, position), (blocks,), jnp.float32, least / len(shards), largest / len(shards)))
        loudness = loudness * jnp.repeat(steps, shape[position] // blocks).reshape([-1 if axis == position else 1 for axis in range(len(shape))])
    return loudness


def gaussian(own_key, shape, scale, reach, shards=(), held_as=jnp.bfloat16):
    gain = steps_of(own_key, shape, shards, -0.22, 0.18) if shards else 1.0
    result = jax.random.normal(own_key, shape, jnp.float32) * scale * gain
    return jnp.minimum(jnp.maximum(result, -reach), reach).astype(held_as)


def setup_inputs(seed: int = 0) -> dict:
    seeds = jax.random.split(jax.random.key(seed), 8)
    offset_coeffs = gaussian(seeds[0], (SENSOR_COUNT, NODES_AROUND), 1.0, 6.0, ((0, 2), (1, 16)), jnp.float32)
    leftover_error = draw_leftover_error(jax.random.fold_in(seeds[7], 71), 0)
    search_vector = draw_search_vector(jax.random.fold_in(seeds[7], 71), 0)
    node_lattice_offset = set_ends(jax.random.randint(seeds[3], (SENSOR_COUNT,), 0, SPACING), jax.random.fold_in(seeds[3], 1), 0, SPACING - 1).astype(jnp.int32)
    sky_cell_in_patch = set_ends(jax.random.randint(seeds[4], (SENSOR_COUNT, TIME), 0, 128), jax.random.fold_in(seeds[4], 1), 0, 127).astype(jnp.int32)
    analyser_reading_phase = jnp.clip(jax.random.uniform(seeds[5], (SENSOR_COUNT, TIME), jnp.float32, -3.140625, 3.140625), -3.140625, 3.140625)
    segment_sky_patch = draw_segment_sky_patch(jax.random.fold_in(seeds[7], 71), 0)
    return dict(offset_coeffs=offset_coeffs, leftover_error=leftover_error, search_vector=search_vector, node_lattice_offset=node_lattice_offset, sky_cell_in_patch=sky_cell_in_patch, analyser_reading_phase=analyser_reading_phase, segment_sky_patch=segment_sky_patch)


MAP_PRIOR = 1.0
BASE_PRIOR = 0.1


def spline_weights(fraction):
    square = fraction * fraction
    cube = square * fraction
    first = (1.0 - fraction) * (1.0 - fraction) * (1.0 - fraction) / 6.0
    second = (3.0 * cube - 6.0 * square + 4.0) / 6.0
    third = (-3.0 * cube + 3.0 * square + 3.0 * fraction + 1.0) / 6.0
    fourth = cube / 6.0
    return (first, second, third, fourth)


def solve_pixels(sums):
    total_signal, signal_cos, signal_sin, hit_count, cos_sum, sin_sum, cos_cos, cos_sin, sin_sin = sums
    stokes_i = hit_count + MAP_PRIOR
    stokes_q = cos_cos + MAP_PRIOR
    stokes_u = sin_sin + MAP_PRIOR
    minor_one = stokes_q * stokes_u - cos_sin * cos_sin
    minor_two = sin_sum * cos_sin - cos_sum * stokes_u
    minor_three = cos_sum * cos_sin - sin_sum * stokes_q
    minor_four = stokes_i * stokes_u - sin_sum * sin_sum
    minor_five = cos_sum * sin_sum - stokes_i * cos_sin
    minor_six = stokes_i * stokes_q - cos_sum * cos_sum
    determinant = stokes_i * minor_one + cos_sum * minor_two + sin_sum * minor_three
    intensity = (minor_one * total_signal + minor_two * signal_cos + minor_three * signal_sin) / determinant
    polar_q = (minor_two * total_signal + minor_four * signal_cos + minor_five * signal_sin) / determinant
    polar_u = (minor_three * total_signal + minor_five * signal_cos + minor_six * signal_sin) / determinant
    return intensity, polar_q, polar_u


def reference(offset_coeffs, leftover_error, search_vector, node_lattice_offset, sky_cell_in_patch, analyser_reading_phase, segment_sky_patch):
    times = jnp.arange(TIME, dtype=jnp.int32)
    shifted = times[None, :] - node_lattice_offset[:, None]
    interval = jnp.floor_divide(shifted, SPACING)
    fraction = (shifted - interval * SPACING).astype(jnp.float32) / SPACING
    weights = spline_weights(fraction)
    row_ids = jnp.arange(SENSOR_COUNT, dtype=jnp.int32)[:, None]
    stream = jnp.zeros(fraction.shape, jnp.float32)
    knot_ids = []
    for term in range(4):
        knot = jnp.mod(interval + term - 1, NODES_AROUND).astype(jnp.int32)
        knot_ids.append(knot)
        stream = stream + weights[term] * search_vector[row_ids, knot]
    cosine = jnp.cos(2.0 * analyser_reading_phase)
    sine = jnp.sin(2.0 * analyser_reading_phase)
    block_ids = jnp.floor_divide(times, 128).astype(jnp.int32)
    pixel = (segment_sky_patch[:, block_ids] * 128 + sky_cell_in_patch).astype(jnp.int32).reshape(-1)
    ones = jnp.ones(fraction.shape, jnp.float32)
    channels = [stream, stream * cosine, stream * sine, ones, cosine, sine,
                cosine * cosine, cosine * sine, sine * sine]
    sums = tuple(jax.ops.segment_sum(channel.reshape(-1), pixel, num_segments=NPIX) for channel in channels)
    intensity, polar_q, polar_u = solve_pixels(sums)
    projected = (intensity[pixel] + cosine.reshape(-1) * polar_q[pixel]) + sine.reshape(-1) * polar_u[pixel]
    cleaned = stream - projected.reshape(SENSOR_COUNT, TIME)
    image = jnp.zeros((SENSOR_COUNT * NODES_AROUND,), jnp.float32)
    for term in range(4):
        target = (row_ids * NODES_AROUND + knot_ids[term]).astype(jnp.int32).reshape(-1)
        image = image + jax.ops.segment_sum((weights[term] * cleaned).reshape(-1), target,
                                            num_segments=SENSOR_COUNT * NODES_AROUND)
    image = image.reshape(SENSOR_COUNT, NODES_AROUND) / SPACING + BASE_PRIOR * search_vector
    norm_old = jnp.sum(leftover_error * leftover_error)
    stride_factor = norm_old / jnp.sum(search_vector * image)
    fresh_offset_coeffs = offset_coeffs + stride_factor * search_vector
    fresh_leftover_error = leftover_error - stride_factor * image
    beta = jnp.sum(fresh_leftover_error * fresh_leftover_error) / norm_old
    fresh_search_vector = fresh_leftover_error + beta * search_vector
    return (fresh_offset_coeffs, fresh_leftover_error, fresh_search_vector)
```

```python
import functools

import jax
import jax.numpy as jnp
from jax import lax
from jax.experimental import pallas as pl
from jax.experimental.pallas import tpu as pltpu
from jax.sharding import PartitionSpec as P

PIX_OWN = 131072
MAP_PRIOR = 1.0
BASE_PRIOR = 0.1
LANES = 128
OWNER_TILES = PIX_OWN // LANES
CHANNELS = 8
VMEM_BYTES = 32 * 1024 * 1024

SIN_TERMS = (1.0, -1.0 / 6, 1.0 / 120, -1.0 / 5040, 1.0 / 362880, -1.0 / 39916800, 1.0 / 6227020800)
COS_TERMS = (1.0, -0.5, 1.0 / 24, -1.0 / 720, 1.0 / 40320, -1.0 / 3628800, 1.0 / 479001600, -1.0 / 87178291200)
PI_PARTS = (3.140625, 0.0009670257568359375, 6.2771141529083252e-07)


def iota(shape, dim):
    return lax.broadcasted_iota(jnp.int32, shape, dim)


def log2(number):
    assert number & (number - 1) == 0
    return number.bit_length() - 1


def split3(x):
    high = x.astype(jnp.bfloat16)
    rest = x - high.astype(jnp.float32)
    middle = rest.astype(jnp.bfloat16)
    low = (rest - middle.astype(jnp.float32)).astype(jnp.bfloat16)
    return high, middle, low


def dot(a, b):
    return jnp.dot(a, b, preferred_element_type=jnp.float32)


def exact_dot(selector, x):
    high, middle, low = split3(x)
    return (dot(selector, high) + dot(selector, middle)) + dot(selector, low)


def horner(x, terms):
    total = jnp.full_like(x, terms[-1])
    for term in terms[-2::-1]:
        total = total * x + term
    return total


def cos_sin(angle):
    turns = jnp.round(angle * (1.0 / 3.14159265358979))
    rest = angle - turns * PI_PARTS[0]
    rest = rest - turns * PI_PARTS[1]
    rest = rest - turns * PI_PARTS[2]
    half = turns * 0.5
    sign = 1.0 - 4.0 * (half - jnp.floor(half))
    square = rest * rest
    cosine = sign * horner(square, COS_TERMS)
    sine = sign * rest * horner(square, SIN_TERMS)
    return cosine, sine


def spline_weights(fraction):
    square = fraction * fraction
    cube = square * fraction
    rest = 1.0 - fraction
    first = rest * rest * rest * (1.0 / 6.0)
    second = (3.0 * cube - 6.0 * square + 4.0) * (1.0 / 6.0)
    third = (-3.0 * cube + 3.0 * square + 3.0 * fraction + 1.0) * (1.0 / 6.0)
    fourth = cube * (1.0 / 6.0)
    return (first, second, third, fourth)


def lane_gather(table, index):
    return jnp.take_along_axis(table, index, axis=1, mode="promise_in_bounds")


def send_kernel(ranks, cap, offset_ref, patch_ref, cell_ref, phase_ref, search_ref, left_ref, out_ref):
    dets, columns = patch_ref.shape
    blocks = dets * columns
    samples = phase_ref.shape[1]
    nodes = search_ref.shape[1]
    span = lax.axis_index("tm")
    rows = 2 * cap + 1
    square = (blocks, blocks)
    tiles = jnp.concatenate(
        [jnp.broadcast_to(patch_ref[:, c : c + 1], (dets, LANES)) for c in range(columns)], axis=0
    )
    cells = jnp.concatenate([cell_ref[:, c * LANES : (c + 1) * LANES] for c in range(columns)], axis=0)
    phases = jnp.concatenate([phase_ref[:, c * LANES : (c + 1) * LANES] for c in range(columns)], axis=0)
    pixels = (tiles * LANES + cells + 1).astype(jnp.float32)
    owner = (tiles >> log2(OWNER_TILES)).astype(jnp.float32)
    owner_t = owner.T
    same = owner == owner_t
    here, there = iota(square, 0), iota(square, 1)
    rank_row = jnp.sum(jnp.where(same & (here < there), 1.0, 0.0), axis=0, keepdims=True)
    rank_col = jnp.sum(jnp.where(same & (there < here), 1.0, 0.0), axis=1, keepdims=True)
    slot_row = (owner_t[0:1, :] * cap + rank_row).astype(jnp.int32)
    place = (iota((ranks * cap, blocks), 0) == slot_row).astype(jnp.bfloat16)
    slot_phase = exact_dot(place, phases)
    slot_pixel = exact_dot(place, pixels) - 1.0
    lane = iota(square, 1)
    det_lane = iota((dets, LANES), 0)
    shift = jnp.zeros((dets, LANES), jnp.int32)
    for d in range(dets):
        shift = jnp.where(det_lane == d, offset_ref[d], shift)
    start = jnp.concatenate([c * LANES - shift for c in range(columns)], axis=0) + span * samples
    which = (iota(square, 0) & (dets - 1)) + 1
    rank = rank_col.astype(jnp.int32)
    listing = jnp.where(lane == rank, start, 0) + jnp.where(lane == rank + cap, which, 0)
    chosen = (iota((ranks, blocks), 0).astype(jnp.float32) == owner_t[0:1, :]).astype(jnp.bfloat16)
    info = exact_dot(chosen, listing.astype(jnp.float32))
    knots = jnp.zeros((dets, LANES), jnp.float32)
    small = iota((dets, LANES), 1)
    for n in range(nodes):
        base = 2 * cap + det_lane * nodes + n
        knots = knots + jnp.where(small == base, search_ref[:, n : n + 1], 0.0)
        knots = knots + jnp.where(small == base + dets * nodes, left_ref[:, n : n + 1], 0.0)
    info = info + jnp.sum(knots, axis=0, keepdims=True)
    for o in range(ranks):
        out_ref[o * rows : o * rows + cap, :] = slot_phase[o * cap : (o + 1) * cap, :]
        out_ref[o * rows + cap : o * rows + 2 * cap, :] = slot_pixel[o * cap : (o + 1) * cap, :]
        out_ref[o * rows + 2 * cap : (o + 1) * rows, :] = info[o : o + 1, :]


def main_kernel(
    ranks, cap, dets, nodes, spacing, own_ref, other_ref, out_ref, packs_ref,
    phase_ref, cell_ref, label_ref, info_ref, meta_ref, flip_ref, table_ref,
    wave_ref, stream_ref, entry_ref, bin_ref,
):
    slots = ranks * cap
    rows = 2 * cap + 1
    knots = ranks * nodes
    pages = max(1, knots // LANES)
    group = lax.axis_index("det")
    packed = knots * dets // LANES
    chunk = 32

    meta_ref[...] = jnp.zeros_like(meta_ref)
    for half, ref in enumerate((own_ref, other_ref)):
        for o in range(ranks):
            here = half * slots + o * cap
            phase_ref[here : here + cap, :] = ref[o * rows : o * rows + cap, :]
            pixel = ref[o * rows + cap : o * rows + 2 * cap, :]
            label = jnp.floor(pixel * (1.0 / LANES))
            label_ref[here : here + cap, :] = label
            cell_ref[here : here + cap, :] = pixel - label * LANES
            info = ref[o * rows + 2 * cap : (o + 1) * rows, :]
            info_ref[here : here + cap, :] = jnp.broadcast_to(info, (cap, LANES))
            meta_ref[half, o : o + 1, :] = info

    small = iota((dets, LANES), 1)
    per_row = LANES // (dets * nodes)
    for half in range(2):
        flip_ref[...] = meta_ref[half].T
        for page in range(pages):
            table = jnp.zeros((dets, LANES), jnp.float32)
            place = small + page * LANES
            for n in range(nodes):
                column = flip_ref[pl.ds(2 * cap + n, dets, stride=nodes), :]
                values = lane_gather(column, (place >> log2(nodes)) & (LANES - 1))
                table = jnp.where((place & (nodes - 1)) == n, values, table)
            table = jnp.concatenate([table, jnp.zeros((LANES - dets, LANES), jnp.float32)], axis=0)
            at = half * slots
            index = (iota((slots, LANES), 0) & (cap - 1)) + cap
            which = lane_gather(info_ref[at : at + slots, :], index)
            chosen = (which == (iota((slots, LANES), 1) + 1).astype(jnp.float32)).astype(jnp.bfloat16)
            table_ref[page, at : at + slots, :] = exact_dot(chosen, table)
        side = group if half == 0 else 1 - group
        for kind in range(2):
            for p in range(packed):
                spans = meta_ref[half, p * per_row : (p + 1) * per_row, :]
                lane = iota((per_row, LANES), 1)
                first = 2 * cap + kind * dets * nodes
                spread = lane_gather(spans, first + (lane & (dets * nodes - 1)))
                mine = (lane >> log2(dets * nodes)) == iota((per_row, LANES), 0)
                line = jnp.sum(jnp.where(mine, spread, 0.0), axis=0, keepdims=True)
                packs_ref[kind, pl.ds(side * packed + p, 1), :] = line

    def spline(at, count):
        info = info_ref[pl.ds(at, count), :]
        slot = (iota((count, LANES), 0) + at) & (cap - 1)
        start = lane_gather(info, slot).astype(jnp.int32)
        time = start + iota((count, LANES), 1)
        interval = time >> log2(spacing)
        fraction = (time & (spacing - 1)).astype(jnp.float32) * (1.0 / spacing)
        return start >> log2(spacing), interval, spline_weights(fraction)

    def prepare(step, carry):
        at = pl.multiple_of(step * chunk, chunk)
        cosine, sine = cos_sin(2.0 * phase_ref[pl.ds(at, chunk), :])
        _, interval, weights = spline(at, chunk)
        stream = jnp.zeros((chunk, LANES), jnp.float32)
        for term in range(4):
            knot = (interval + (term - 1)) & (knots - 1)
            value = lane_gather(table_ref[0, pl.ds(at, chunk), :], knot & (LANES - 1))
            for page in range(1, pages):
                more = lane_gather(table_ref[page, pl.ds(at, chunk), :], knot & (LANES - 1))
                value = jnp.where((knot >> log2(LANES)) == page, more, value)
            stream = stream + weights[term] * value
        wave_ref[0, pl.ds(at, chunk), :] = cosine
        wave_ref[1, pl.ds(at, chunk), :] = sine
        stream_ref[pl.ds(at, chunk), :] = stream
        entries = (
            stream, stream * cosine, stream * sine, jnp.ones_like(cosine), cosine, sine,
            cosine * cosine, cosine * sine,
        )
        for channel, entry in enumerate(entries):
            entry_ref[pl.ds(at * CHANNELS + channel, chunk, stride=CHANNELS), :] = entry
        return carry

    lax.fori_loop(0, 2 * slots // chunk, prepare, 0)

    lanes_down = iota((LANES, LANES), 0).astype(jnp.float32)

    def collect(slot, carry):
        at = pl.multiple_of(slot * CHANNELS, CHANNELS)
        entry = jnp.concatenate(split3(entry_ref[pl.ds(at, CHANNELS), :]), axis=0)
        cell = cell_ref[pl.ds(slot, 1), :]
        hits = (lanes_down == cell).astype(jnp.bfloat16)
        sums = lax.dot_general(
            entry, hits, (((1,), (1,)), ((), ())), preferred_element_type=jnp.float32
        )
        bin_ref[pl.ds(at, CHANNELS), :] = (
            sums[:CHANNELS] + sums[CHANNELS : 2 * CHANNELS]
        ) + sums[2 * CHANNELS :]
        return carry

    lax.fori_loop(0, 2 * slots, collect, 0, unroll=8)

    labels = label_ref[...]
    across = jnp.concatenate(
        [labels[k * LANES : (k + 1) * LANES, :].T[0:1, :] for k in range(2 * slots // LANES)], axis=1
    )
    same = (labels[:slots, 0:1] == across).astype(jnp.bfloat16)
    totals = []
    for channel in range(CHANNELS):
        binned = bin_ref[pl.ds(channel, 2 * slots, stride=CHANNELS), :]
        totals.append(exact_dot(same, binned))
    signal, signal_cos, signal_sin, count, cos_sum, sin_sum, cos_cos, cos_sin_sum = totals
    sin_sin = count - cos_cos
    stokes_i = count + MAP_PRIOR
    stokes_q = cos_cos + MAP_PRIOR
    stokes_u = sin_sin + MAP_PRIOR
    minor_one = stokes_q * stokes_u - cos_sin_sum * cos_sin_sum
    minor_two = sin_sum * cos_sin_sum - cos_sum * stokes_u
    minor_three = cos_sum * cos_sin_sum - sin_sum * stokes_q
    minor_four = stokes_i * stokes_u - sin_sum * sin_sum
    minor_five = cos_sum * sin_sum - stokes_i * cos_sin_sum
    minor_six = stokes_i * stokes_q - cos_sum * cos_sum
    determinant = stokes_i * minor_one + cos_sum * minor_two + sin_sum * minor_three
    scale = 1.0 / determinant
    map_i = (minor_one * signal + minor_two * signal_cos + minor_three * signal_sin) * scale
    map_q = (minor_two * signal + minor_four * signal_cos + minor_five * signal_sin) * scale
    map_u = (minor_three * signal + minor_five * signal_cos + minor_six * signal_sin) * scale

    cell = cell_ref[:slots, :].astype(jnp.int32)
    projected = (
        lane_gather(map_i, cell) + wave_ref[0, :slots, :] * lane_gather(map_q, cell)
    ) + wave_ref[1, :slots, :] * lane_gather(map_u, cell)
    which = lane_gather(info_ref[:slots, :], (iota((slots, LANES), 0) & (cap - 1)) + cap)
    cleaned = jnp.where(which > 0.5, stream_ref[:slots, :] - projected, 0.0)
    base, interval, weights = spline(0, slots)
    base = base[:, 0:1]
    early = interval == base
    det = which.astype(jnp.int32)[:, 0:1] - 1
    lines = [jnp.zeros((slots, LANES), jnp.float32) for _ in range(packed)]
    lane = iota((slots, LANES), 1)
    for term in range(5):
        low = weights[term] if term < 4 else 0.0
        high = weights[term - 1] if term > 0 else 0.0
        value = jnp.sum(jnp.where(early, low, high) * cleaned, axis=1, keepdims=True)
        knot = (base + (term - 1)) & (knots - 1)
        spot = (knot >> log2(nodes)) * (dets * nodes) + det * nodes + (knot & (nodes - 1))
        for p in range(packed):
            lines[p] = lines[p] + jnp.where(lane == spot - p * LANES, value, 0.0)
    partial = jnp.concatenate([jnp.sum(line, axis=0, keepdims=True) for line in lines], axis=0)
    for target in range(out_ref.shape[0] // packed):
        out_ref[target * packed : (target + 1) * packed, :] = partial


def finish_kernel(
    ranks, spacing, arrived_ref, packs_ref, offset_ref, left_ref, search_ref,
    new_offset_ref, new_left_ref, new_search_ref,
):
    dets, nodes = search_ref.shape
    height = packs_ref.shape[1]
    total = arrived_ref[0:height, :]
    for o in range(1, ranks):
        total = total + arrived_ref[o * height : (o + 1) * height, :]
    search, left = packs_ref[0], packs_ref[1]
    image = total * (1.0 / spacing) + BASE_PRIOR * search
    norm_old = jnp.sum(left * left, keepdims=True)
    stride_factor = norm_old / jnp.sum(search * image, keepdims=True)
    fresh = left - stride_factor * image
    beta = jnp.sum(fresh * fresh, keepdims=True) / norm_old
    span, group = lax.axis_index("tm"), lax.axis_index("det")
    per_row = LANES // (dets * nodes)
    row = group * (height // 2) + (span >> log2(per_row))
    mine = jnp.sum(jnp.where(iota((height, LANES), 0) == row, image, 0.0), axis=0, keepdims=True)
    lane = iota((dets, LANES), 1)
    first = (span & (per_row - 1)) * (dets * nodes)
    index = first + iota((dets, LANES), 0) * nodes + (lane & (nodes - 1))
    mine = lane_gather(jnp.broadcast_to(mine, (dets, LANES)), index)[:, :nodes]
    new_offset_ref[...] = offset_ref[...] + stride_factor * search_ref[...]
    new_left = left_ref[...] - stride_factor * mine
    new_left_ref[...] = new_left
    new_search_ref[...] = new_left + beta * search_ref[...]


def body(
    offset_coeffs,
    leftover_error,
    search_vector,
    node_lattice_offset,
    sky_cell_in_patch,
    analyser_reading_phase,
    segment_sky_patch,
):
    ranks, groups = lax.axis_size("tm"), lax.axis_size("det")
    dets, samples = analyser_reading_phase.shape
    nodes = search_vector.shape[1]
    spacing = samples // nodes
    blocks = segment_sky_patch.size
    cap = max(2, 2 * blocks // ranks)
    slots = ranks * cap
    rows = 2 * cap + 1
    packed = ranks * nodes * dets // LANES
    vmem = pl.BlockSpec(memory_space=pltpu.VMEM)
    smem = pl.BlockSpec(memory_space=pltpu.SMEM)
    params = pltpu.CompilerParams(vmem_limit_bytes=VMEM_BYTES)

    outgoing = pl.pallas_call(
        functools.partial(send_kernel, ranks, cap),
        out_shape=jax.ShapeDtypeStruct((ranks * rows, LANES), jnp.float32),
        in_specs=[smem] + [vmem] * 5,
        out_specs=vmem,
        compiler_params=params,
        name="send",
    )(
        node_lattice_offset, segment_sky_patch, sky_cell_in_patch, analyser_reading_phase,
        search_vector, leftover_error,
    )
    arrived = lax.all_to_all(
        outgoing.reshape(ranks, 1, rows * LANES), "tm", split_axis=0, concat_axis=0, tiled=True
    )
    swap = [(i, groups - 1 - i) for i in range(groups)]
    other = lax.ppermute(arrived, "det", swap)
    pages = max(1, ranks * nodes // LANES)
    big = pltpu.VMEM((2 * slots, LANES), jnp.float32)
    partials, packs = pl.pallas_call(
        functools.partial(main_kernel, ranks, cap, dets, nodes, spacing),
        out_shape=(
            jax.ShapeDtypeStruct((ranks * groups * packed, LANES), jnp.float32),
            jax.ShapeDtypeStruct((2, groups * packed, LANES), jnp.float32),
        ),
        in_specs=[vmem] * 2,
        out_specs=(vmem, vmem),
        scratch_shapes=[
            big, big, big, big,
            pltpu.VMEM((2, LANES, LANES), jnp.float32),
            pltpu.VMEM((LANES, LANES), jnp.float32),
            pltpu.VMEM((pages, 2 * slots, LANES), jnp.float32),
            pltpu.VMEM((2, 2 * slots, LANES), jnp.float32),
            big,
            pltpu.VMEM((2 * slots * CHANNELS, LANES), jnp.float32),
            pltpu.VMEM((2 * slots * CHANNELS, LANES), jnp.float32),
        ],
        compiler_params=params,
        name="main",
    )(arrived.reshape(ranks * rows, LANES), other.reshape(ranks * rows, LANES))
    gathered = lax.all_to_all(
        partials.reshape(ranks * groups, 1, packed * LANES),
        ("tm", "det"), split_axis=0, concat_axis=0, tiled=True,
    )
    small = jax.ShapeDtypeStruct((dets, nodes), jnp.float32)
    return pl.pallas_call(
        functools.partial(finish_kernel, ranks, spacing),
        out_shape=(small, small, small),
        in_specs=[vmem] * 5,
        out_specs=(vmem, vmem, vmem),
        compiler_params=params,
        name="finish",
    )(
        gathered.reshape(ranks * groups * packed, LANES), packs,
        offset_coeffs, leftover_error, search_vector,
    )


def solution(mesh):
    return jax.shard_map(
        body,
        mesh=mesh,
        in_specs=(
            P("det", "tm"),
            P("det", "tm"),
            P("det", "tm"),
            P("det"),
            P("det", "tm"),
            P("det", "tm"),
            P("det", "tm"),
        ),
        out_specs=(P("det", "tm"), P("det", "tm"), P("det", "tm")),
        check_vma=False,
    )
```

```python
import functools

import jax
import jax.numpy as jnp
from jax import lax
from jax.experimental import pallas as pl
from jax.experimental.pallas import tpu as pltpu
from jax.sharding import PartitionSpec as P

PIX_OWN = 131072
MAP_PRIOR = 1.0
BASE_PRIOR = 0.1
LANES = 128
OWNER_TILES = PIX_OWN // LANES
CHANNELS = 8
BLOCK = 256
CHUNK = 32
VMEM_BYTES = 32 * 1024 * 1024

SIN_TERMS = (1.0, -1.0 / 6, 1.0 / 120, -1.0 / 5040, 1.0 / 362880, -1.0 / 39916800, 1.0 / 6227020800)
COS_TERMS = (1.0, -0.5, 1.0 / 24, -1.0 / 720, 1.0 / 40320, -1.0 / 3628800, 1.0 / 479001600, -1.0 / 87178291200)
PI_PARTS = (3.140625, 0.0009670257568359375, 6.2771141529083252e-07)


def iota(shape, dim):
    return lax.broadcasted_iota(jnp.int32, shape, dim)


def log2(number):
    assert number & (number - 1) == 0
    return number.bit_length() - 1


def split3(x):
    high = x.astype(jnp.bfloat16)
    rest = x - high.astype(jnp.float32)
    middle = rest.astype(jnp.bfloat16)
    low = (rest - middle.astype(jnp.float32)).astype(jnp.bfloat16)
    return high, middle, low


def dot(a, b):
    return jnp.dot(a, b, preferred_element_type=jnp.float32)


def exact_dot(selector, x):
    high, middle, low = split3(x)
    return (dot(selector, high) + dot(selector, middle)) + dot(selector, low)


def horner(x, terms):
    total = jnp.full_like(x, terms[-1])
    for term in terms[-2::-1]:
        total = total * x + term
    return total


def cos_sin(angle):
    turns = jnp.round(angle * (1.0 / 3.14159265358979))
    rest = angle - turns * PI_PARTS[0]
    rest = rest - turns * PI_PARTS[1]
    rest = rest - turns * PI_PARTS[2]
    half = turns * 0.5
    sign = 1.0 - 4.0 * (half - jnp.floor(half))
    square = rest * rest
    cosine = sign * horner(square, COS_TERMS)
    sine = sign * rest * horner(square, SIN_TERMS)
    return cosine, sine


def spline_weights(fraction):
    square = fraction * fraction
    cube = square * fraction
    rest = 1.0 - fraction
    first = rest * rest * rest * (1.0 / 6.0)
    second = (3.0 * cube - 6.0 * square + 4.0) * (1.0 / 6.0)
    third = (-3.0 * cube + 3.0 * square + 3.0 * fraction + 1.0) * (1.0 / 6.0)
    fourth = cube * (1.0 / 6.0)
    return (first, second, third, fourth)


def lane_gather(table, index):
    return jnp.take_along_axis(table, index, axis=1, mode="promise_in_bounds")


def send_kernel(
    ranks, cap, offset_ref, patch_ref, cell_hbm, phase_hbm, search_ref, left_ref, out_ref,
    cell_ref, phase_ref, sems,
):
    big_copies = (
        pltpu.make_async_copy(cell_hbm, cell_ref, sems.at[0]),
        pltpu.make_async_copy(phase_hbm, phase_ref, sems.at[1]),
    )
    for copy in big_copies:
        copy.start()
    dets, columns = patch_ref.shape
    blocks = dets * columns
    samples = phase_ref.shape[1]
    nodes = search_ref.shape[0]
    span = lax.axis_index("tm")
    rows = 2 * cap + 1
    square = (blocks, blocks)
    tiles = jnp.concatenate(
        [jnp.broadcast_to(patch_ref[:, c : c + 1], (dets, LANES)) for c in range(columns)], axis=0
    )
    owner = (tiles >> log2(OWNER_TILES)).astype(jnp.float32)
    owner_t = owner.T
    same = owner == owner_t
    here, there = iota(square, 0), iota(square, 1)
    rank_row = jnp.sum(jnp.where(same & (here < there), 1.0, 0.0), axis=0, keepdims=True)
    rank_col = jnp.sum(jnp.where(same & (there < here), 1.0, 0.0), axis=1, keepdims=True)
    slot_row = (owner_t[0:1, :] * cap + rank_row).astype(jnp.int32)
    place = (iota((ranks * cap, blocks), 0) == slot_row).astype(jnp.bfloat16)
    lane = iota(square, 1)
    small = iota((dets, LANES), 1)
    det_lane = iota((dets, LANES), 0)
    offsets = jnp.broadcast_to(offset_ref[...], (dets, dets))
    diagonal = iota((dets, dets), 0) == iota((dets, dets), 1)
    shift = jnp.sum(jnp.where(diagonal, offsets, 0).astype(jnp.float32), axis=1, keepdims=True)
    shift = jnp.broadcast_to(shift.astype(jnp.int32), (dets, LANES))
    start = jnp.concatenate([c * LANES - shift for c in range(columns)], axis=0) + span * samples
    which = (iota(square, 0) & (dets - 1)) + 1
    rank = rank_col.astype(jnp.int32)
    listing = jnp.where(lane == rank, start, 0) + jnp.where(lane == rank + cap, which, 0)
    listing = listing + jnp.where(lane == rank + 2 * cap, tiles + 1, 0)
    chosen = (iota((ranks, blocks), 0).astype(jnp.float32) == owner_t[0:1, :]).astype(jnp.bfloat16)
    info = exact_dot(chosen, listing.astype(jnp.float32))
    knots = jnp.zeros((1, LANES), jnp.float32)
    for kind, ref in enumerate((search_ref, left_ref)):
        for n in range(nodes):
            column = jnp.broadcast_to(ref[n : n + 1, :], (dets, dets))
            column = jnp.sum(jnp.where(diagonal, column, 0.0), axis=1, keepdims=True)
            at = (3 * cap + kind * dets * nodes + n) + det_lane * nodes
            knots = knots + jnp.sum(jnp.where(small == at, column, 0.0), axis=0, keepdims=True)
    info = info + knots
    big_copies[0].wait()
    cells = jnp.concatenate([cell_ref[:, c * LANES : (c + 1) * LANES] for c in range(columns)], axis=0)
    slot_pixel = exact_dot(place, (tiles * LANES + cells).astype(jnp.float32))
    big_copies[1].wait()
    phases = jnp.concatenate([phase_ref[:, c * LANES : (c + 1) * LANES] for c in range(columns)], axis=0)
    slot_phase = exact_dot(place, phases)
    for o in range(ranks):
        out_ref[o * rows : o * rows + cap, :] = slot_phase[o * cap : (o + 1) * cap, :]
        out_ref[o * rows + cap : o * rows + 2 * cap, :] = slot_pixel[o * cap : (o + 1) * cap, :]
        out_ref[o * rows + 2 * cap : (o + 1) * rows, :] = info[o : o + 1, :]


def main_kernel(
    ranks, cap, dets, nodes, spacing, own_ref, other_ref, out_ref, packs_ref,
    phase_ref, cell_ref, info_ref, meta_ref, few_phase, few_cell, few_info, table_ref,
    cos_ref, sin_ref, stream_ref, bin_ref, total_ref, turned_ref,
):
    slots = ranks * cap
    rows = 2 * cap + 1
    knots = ranks * nodes
    width = dets * nodes
    pages = max(1, knots // LANES)
    group = lax.axis_index("det")
    packed = knots * dets // LANES
    per_row = LANES // width
    row_count = 2 * slots // LANES

    for half, ref in enumerate((own_ref, other_ref)):
        for o in range(ranks):
            here = half * slots + o * cap
            phase_ref[here : here + cap, :] = ref[o * rows : o * rows + cap, :]
            cell_ref[here : here + cap, :] = ref[o * rows + cap : o * rows + 2 * cap, :]
            info = ref[o * rows + 2 * cap : (o + 1) * rows, :]
            info_ref[here : here + cap, :] = jnp.broadcast_to(info, (cap, LANES))
            meta_ref[half, o : o + 1, :] = info

    lists = []
    spans = LANES // cap
    for half in range(2):
        for k in range(slots // LANES):
            names = meta_ref[half, k * spans : (k + 1) * spans, :]
            lane = iota((spans, LANES), 1)
            spread = lane_gather(names, 2 * cap + (lane & (cap - 1)))
            mine = (lane >> log2(cap)) == iota((spans, LANES), 0)
            lists.append(jnp.sum(jnp.where(mine, spread, 0.0), axis=0, keepdims=True))
    names = jnp.concatenate(lists, axis=0).astype(jnp.int32)
    mine = (names > 0) & (((names - 1) & 1) == group)
    ones = jnp.where(mine, 1.0, 0.0)
    earlier = (iota((LANES, LANES), 0) < iota((LANES, LANES), 1)).astype(jnp.bfloat16)
    rank = dot(ones.astype(jnp.bfloat16), earlier)
    sums = jnp.sum(ones, axis=1, keepdims=True)
    before = [jnp.zeros((1, 1), jnp.float32)]
    for k in range(row_count):
        before.append(before[-1] + sums[k : k + 1, :])
    rank = rank + jnp.concatenate(before[:-1], axis=0)
    rank = jnp.where(mine, rank, -1.0).astype(jnp.int32)
    number = jnp.sum(ones).astype(jnp.int32)
    blocks = (number + (BLOCK - 1)) >> log2(BLOCK)
    chunks = (number + (CHUNK - 1)) >> log2(CHUNK)

    tables = [[], []]
    for half in range(2):
        side = group if half == 0 else 1 - group
        packs = []
        for kind in range(2):
            for p in range(packed):
                names = meta_ref[half, p * per_row : (p + 1) * per_row, :]
                lane = iota((per_row, LANES), 1)
                spread = lane_gather(names, (3 * cap + kind * width) + (lane & (width - 1)))
                here = (lane >> log2(width)) == iota((per_row, LANES), 0)
                line = jnp.sum(jnp.where(here, spread, 0.0), axis=0, keepdims=True)
                packs_ref[kind, pl.ds(side * packed + p, 1), :] = line
                packs.append(line)
        lane = iota((dets, LANES), 1)
        for page in range(pages):
            knot = lane + page * LANES
            index = ((knot >> log2(nodes)) & (per_row - 1)) * width
            index = index + iota((dets, LANES), 0) * nodes + (knot & (nodes - 1))
            table = jnp.zeros((dets, LANES), jnp.float32)
            for p in range(packed):
                values = lane_gather(jnp.broadcast_to(packs[p], (dets, LANES)), index)
                table = jnp.where((knot >> log2(per_row * nodes)) == p, values, table)
            tables[half].append(table)

    slot = iota((slots, LANES), 0) & (cap - 1)
    lane = iota((slots, LANES), 1)
    listed = []
    for half in range(2):
        side = group if half == 0 else 1 - group
        found = lane_gather(info_ref[half * slots : (half + 1) * slots, :], jnp.minimum(lane, 2) * cap + slot)
        listed.append(found + jnp.where(lane == 1, (side * dets).astype(jnp.float32), 0.0))
    listed = jnp.concatenate(listed, axis=0)
    pixel = cell_ref[...]
    cell = (pixel - jnp.floor(pixel * (1.0 / LANES)) * LANES).astype(jnp.bfloat16)
    source = jnp.concatenate(split3(phase_ref[...]) + split3(listed) + (cell,), axis=1)

    def gather_block(block, carry):
        at = pl.multiple_of(block * BLOCK, BLOCK)
        down = iota((BLOCK, LANES), 0) + at
        place = jnp.concatenate(
            [(down == rank[k : k + 1, :]).astype(jnp.bfloat16) for k in range(row_count)], axis=1
        )
        taken = dot(place, source)
        parts = [taken[:, k * LANES : (k + 1) * LANES] for k in range(7)]
        few_phase[pl.ds(at, BLOCK), :] = (parts[0] + parts[1]) + parts[2]
        info = (parts[3] + parts[4]) + parts[5]
        few_info[pl.ds(at, BLOCK), :] = info
        few_cell[pl.ds(at, BLOCK), :] = parts[6]
        for k in range(BLOCK // LANES):
            turned_ref[pl.ds(block * (BLOCK // LANES) + k, 1), :] = info[k * LANES : (k + 1) * LANES, :].T[2:3, :]
        chosen = (info[:, 1:2] == (iota((BLOCK, LANES), 1) + 1).astype(jnp.float32)).astype(jnp.bfloat16)
        for page in range(pages):
            first, second = tables[0][page], tables[1][page]
            low = jnp.where(group == 0, first, second)
            high = jnp.where(group == 0, second, first)
            table = jnp.concatenate(
                [low, high, jnp.zeros((LANES - 2 * dets, LANES), jnp.float32)], axis=0
            )
            table_ref[page, pl.ds(at, BLOCK), :] = exact_dot(chosen, table)
        bin_ref[pl.ds(at * CHANNELS, BLOCK * CHANNELS), :] = jnp.zeros((BLOCK * CHANNELS, LANES), jnp.float32)
        return carry

    lax.fori_loop(0, blocks, gather_block, 0)

    def spline(at):
        start = jnp.broadcast_to(few_info[pl.ds(at, CHUNK), 0:1], (CHUNK, LANES)).astype(jnp.int32)
        time = start + iota((CHUNK, LANES), 1)
        interval = time >> log2(spacing)
        fraction = (time & (spacing - 1)).astype(jnp.float32) * (1.0 / spacing)
        return start >> log2(spacing), interval, spline_weights(fraction)

    def prepare(step, carry):
        at = pl.multiple_of(step * CHUNK, CHUNK)
        cosine, sine = cos_sin(2.0 * few_phase[pl.ds(at, CHUNK), :])
        _, interval, weights = spline(at)
        stream = jnp.zeros((CHUNK, LANES), jnp.float32)
        for term in range(4):
            knot = (interval + (term - 1)) & (knots - 1)
            value = lane_gather(table_ref[0, pl.ds(at, CHUNK), :], knot & (LANES - 1))
            for page in range(1, pages):
                more = lane_gather(table_ref[page, pl.ds(at, CHUNK), :], knot & (LANES - 1))
                value = jnp.where((knot >> log2(LANES)) == page, more, value)
            stream = stream + weights[term] * value
        cos_ref[pl.ds(at, CHUNK), :] = cosine
        sin_ref[pl.ds(at, CHUNK), :] = sine
        stream_ref[pl.ds(at, CHUNK), :] = stream
        return carry

    lax.fori_loop(0, chunks, prepare, 0)

    down = iota((LANES, 2 * LANES), 0).astype(jnp.float32).astype(jnp.bfloat16)
    channel = iota((CHANNELS, LANES), 0)
    zeros = jnp.zeros((4 * CHANNELS, LANES), jnp.bfloat16)

    def collect(step, carry):
        for k in range(CHUNK // 2):
            at = step * CHUNK + 2 * k
            pieces, cells = [], []
            for slot in (at, at + 1):
                stream = jnp.broadcast_to(stream_ref[pl.ds(slot, 1), :], (CHANNELS, LANES))
                cosine = jnp.broadcast_to(cos_ref[pl.ds(slot, 1), :], (CHANNELS, LANES))
                sine = jnp.broadcast_to(sin_ref[pl.ds(slot, 1), :], (CHANNELS, LANES))
                left = jnp.where(channel < 3, stream, jnp.where(channel < 6, 1.0, cosine))
                is_one = (channel == 0) | (channel == 3)
                is_sine = (channel == 2) | (channel == 5) | (channel == 7)
                right = jnp.where(is_one, 1.0, jnp.where(is_sine, sine, cosine))
                entry = left * right
                high = entry.astype(jnp.bfloat16).astype(jnp.float32)
                rest = entry - high
                middle = rest.astype(jnp.bfloat16).astype(jnp.float32)
                low = rest - middle
                stack = jnp.concatenate([high, middle, low, jnp.zeros_like(low)], axis=0)
                pieces.append(stack.astype(jnp.bfloat16))
                cells.append(jnp.broadcast_to(few_cell[pl.ds(slot, 1), :].astype(jnp.bfloat16), (LANES, LANES)))
            entry = jnp.concatenate(
                [
                    jnp.concatenate([pieces[0], zeros], axis=1),
                    jnp.concatenate([zeros, pieces[1]], axis=1),
                ],
                axis=0,
            )
            hits = jnp.where(jnp.concatenate(cells, axis=1) == down, jnp.bfloat16(1), jnp.bfloat16(0))
            sums = lax.dot_general(
                entry, hits, (((1,), (1,)), ((), ())), preferred_element_type=jnp.float32
            )
            for m in range(2):
                base = 4 * CHANNELS * m
                bin_ref[pl.ds((at + m) * CHANNELS, CHANNELS), :] = (
                    sums[base : base + CHANNELS] + sums[base + CHANNELS : base + 2 * CHANNELS]
                ) + sums[base + 2 * CHANNELS : base + 3 * CHANNELS]
        return carry

    lax.fori_loop(0, chunks, collect, 0)

    def merge(block, carry):
        at = pl.multiple_of(block * BLOCK, BLOCK)
        names = few_info[pl.ds(at, BLOCK), 2:3]

        def add(other, carry):
            there = pl.multiple_of(other * BLOCK, BLOCK)
            across = [
                turned_ref[pl.ds(other * (BLOCK // LANES) + k, 1), :] for k in range(BLOCK // LANES)
            ]
            same = (names == jnp.concatenate(across, axis=1)).astype(jnp.bfloat16)
            for c in range(CHANNELS):
                binned = bin_ref[pl.ds(there * CHANNELS + c, BLOCK, stride=CHANNELS), :]
                share = exact_dot(same, binned)
                before = total_ref[c, pl.ds(at, BLOCK), :]
                total_ref[c, pl.ds(at, BLOCK), :] = jnp.where(other == 0, share, before + share)
            return carry

        lax.fori_loop(0, blocks, add, 0)
        return carry

    lax.fori_loop(0, blocks, merge, 0)

    def project(step, lines):
        at = pl.multiple_of(step * CHUNK, CHUNK)
        here = pl.ds(at, CHUNK)
        signal, signal_cos, signal_sin, count, cos_sum, sin_sum, cos_cos, cos_sin_sum = (
            total_ref[c, here, :] for c in range(CHANNELS)
        )
        sin_sin = count - cos_cos
        stokes_i = count + MAP_PRIOR
        stokes_q = cos_cos + MAP_PRIOR
        stokes_u = sin_sin + MAP_PRIOR
        minor_one = stokes_q * stokes_u - cos_sin_sum * cos_sin_sum
        minor_two = sin_sum * cos_sin_sum - cos_sum * stokes_u
        minor_three = cos_sum * cos_sin_sum - sin_sum * stokes_q
        minor_four = stokes_i * stokes_u - sin_sum * sin_sum
        minor_five = cos_sum * sin_sum - stokes_i * cos_sin_sum
        minor_six = stokes_i * stokes_q - cos_sum * cos_sum
        determinant = stokes_i * minor_one + cos_sum * minor_two + sin_sum * minor_three
        scale = 1.0 / determinant
        map_i = (minor_one * signal + minor_two * signal_cos + minor_three * signal_sin) * scale
        map_q = (minor_two * signal + minor_four * signal_cos + minor_five * signal_sin) * scale
        map_u = (minor_three * signal + minor_five * signal_cos + minor_six * signal_sin) * scale
        cell = few_cell[here, :].astype(jnp.int32)
        projected = (
            lane_gather(map_i, cell) + cos_ref[here, :] * lane_gather(map_q, cell)
        ) + sin_ref[here, :] * lane_gather(map_u, cell)
        which = few_info[here, 1:2].astype(jnp.int32) - 1
        cleaned = jnp.where(which >= 0, stream_ref[here, :] - projected, 0.0)
        base, interval, weights = spline(at)
        early = interval == base
        lane = iota((CHUNK, LANES), 1)
        side = which >> log2(dets)
        det = which & (dets - 1)
        lines = list(lines)
        for term in range(5):
            low = weights[term] if term < 4 else 0.0
            high = weights[term - 1] if term > 0 else 0.0
            value = jnp.sum(jnp.where(early, low, high) * cleaned, axis=1, keepdims=True)
            knot = (base + (term - 1)) & (knots - 1)
            spot = side * (knots * dets) + (knot >> log2(nodes)) * width + det * nodes
            spot = spot + (knot & (nodes - 1))
            for p in range(2 * packed):
                part = jnp.where(lane + p * LANES == spot, value, 0.0)
                for q in range(CHUNK // 8):
                    lines[p] = lines[p] + part[q * 8 : (q + 1) * 8, :]
        return tuple(lines)

    lines = tuple(jnp.zeros((8, LANES), jnp.float32) for _ in range(2 * packed))
    lines = lax.fori_loop(0, chunks, project, lines)
    partial = jnp.concatenate([jnp.sum(line, axis=0, keepdims=True) for line in lines], axis=0)
    for target in range(out_ref.shape[0] // (2 * packed)):
        out_ref[target * 2 * packed : (target + 1) * 2 * packed, :] = partial


def finish_kernel(
    ranks, spacing, arrived_ref, packs_ref, offset_ref, left_ref, search_ref,
    new_offset_ref, new_left_ref, new_search_ref,
):
    nodes, dets = search_ref.shape
    height = packs_ref.shape[1]
    total = arrived_ref[0:height, :]
    for o in range(1, arrived_ref.shape[0] // height):
        total = total + arrived_ref[o * height : (o + 1) * height, :]
    search, left = packs_ref[0], packs_ref[1]
    image = total * (1.0 / spacing) + BASE_PRIOR * search
    norm_old = jnp.sum(left * left, keepdims=True)
    stride_factor = norm_old / jnp.sum(search * image, keepdims=True)
    fresh = left - stride_factor * image
    beta = jnp.sum(fresh * fresh, keepdims=True) / norm_old
    span, group = lax.axis_index("tm"), lax.axis_index("det")
    per_row = LANES // (dets * nodes)
    row = group * (height // 2) + (span >> log2(per_row))
    mine = jnp.sum(jnp.where(iota((height, LANES), 0) == row, image, 0.0), axis=0, keepdims=True)
    lane = iota((8, LANES), 1)
    first = (span & (per_row - 1)) * (dets * nodes)
    index = first + (lane & (dets - 1)) * nodes + (iota((8, LANES), 0) & (nodes - 1))
    mine = lane_gather(jnp.broadcast_to(mine, (8, LANES)), index)[:nodes, :dets]
    new_offset_ref[...] = offset_ref[...] + stride_factor * search_ref[...]
    new_left = left_ref[...] - stride_factor * mine
    new_left_ref[...] = new_left
    new_search_ref[...] = new_left + beta * search_ref[...]


def body(
    offset_coeffs,
    leftover_error,
    search_vector,
    node_lattice_offset,
    sky_cell_in_patch,
    analyser_reading_phase,
    segment_sky_patch,
):
    ranks, groups = lax.axis_size("tm"), lax.axis_size("det")
    dets, samples = analyser_reading_phase.shape
    nodes = search_vector.shape[1]
    spacing = samples // nodes
    blocks = segment_sky_patch.size
    cap = max(2, 2 * blocks // ranks)
    slots = ranks * cap
    rows = 2 * cap + 1
    height = groups * ranks * nodes * dets // LANES
    vmem = pl.BlockSpec(memory_space=pltpu.VMEM)
    hbm = pl.BlockSpec(memory_space=pltpu.HBM)
    params = pltpu.CompilerParams(vmem_limit_bytes=VMEM_BYTES)
    search, left, coeffs = search_vector.T, leftover_error.T, offset_coeffs.T

    outgoing = pl.pallas_call(
        functools.partial(send_kernel, ranks, cap),
        out_shape=jax.ShapeDtypeStruct((ranks * rows, LANES), jnp.float32),
        in_specs=[vmem, vmem, hbm, hbm, vmem, vmem],
        out_specs=vmem,
        scratch_shapes=[
            pltpu.VMEM((dets, samples), jnp.int32),
            pltpu.VMEM((dets, samples), jnp.float32),
            pltpu.SemaphoreType.DMA((2,)),
        ],
        compiler_params=params,
        name="send",
    )(
        node_lattice_offset.reshape(1, dets), segment_sky_patch, sky_cell_in_patch,
        analyser_reading_phase, search, left,
    )
    arrived = lax.all_to_all(
        outgoing.reshape(ranks, 1, rows * LANES), "tm", split_axis=0, concat_axis=0, tiled=True
    )
    swap = [(i, groups - 1 - i) for i in range(groups)]
    other = lax.ppermute(arrived, "det", swap)
    pages = max(1, ranks * nodes // LANES)
    big = pltpu.VMEM((2 * slots, LANES), jnp.float32)
    partials, packs = pl.pallas_call(
        functools.partial(main_kernel, ranks, cap, dets, nodes, spacing),
        out_shape=(
            jax.ShapeDtypeStruct((ranks * groups * height, LANES), jnp.float32),
            jax.ShapeDtypeStruct((2, height, LANES), jnp.float32),
        ),
        in_specs=[vmem] * 2,
        out_specs=(vmem, vmem),
        scratch_shapes=[
            big, big, big,
            pltpu.VMEM((2, ranks, LANES), jnp.float32),
            big, big, big,
            pltpu.VMEM((pages, 2 * slots, LANES), jnp.float32),
            big, big, big,
            pltpu.VMEM((2 * slots * CHANNELS, LANES), jnp.float32),
            pltpu.VMEM((CHANNELS, 2 * slots, LANES), jnp.float32),
            pltpu.VMEM((max(8, 2 * slots // LANES), LANES), jnp.float32),
        ],
        compiler_params=params,
        name="main",
    )(arrived.reshape(ranks * rows, LANES), other.reshape(ranks * rows, LANES))
    gathered = lax.all_to_all(
        partials.reshape(ranks * groups, 1, height * LANES),
        ("tm", "det"), split_axis=0, concat_axis=0, tiled=True,
    )
    small = jax.ShapeDtypeStruct((nodes, dets), jnp.float32)
    results = pl.pallas_call(
        functools.partial(finish_kernel, ranks, spacing),
        out_shape=(small, small, small),
        in_specs=[vmem] * 5,
        out_specs=(vmem, vmem, vmem),
        compiler_params=params,
        name="finish",
    )(gathered.reshape(ranks * groups * height, LANES), packs, coeffs, left, search)
    return tuple(result.T for result in results)


def solution(mesh):
    return jax.shard_map(
        body,
        mesh=mesh,
        in_specs=(
            P("det", "tm"),
            P("det", "tm"),
            P("det", "tm"),
            P("det"),
            P("det", "tm"),
            P("det", "tm"),
            P("det", "tm"),
        ),
        out_specs=(P("det", "tm"), P("det", "tm"), P("det", "tm")),
        check_vma=False,
    )
```

```python
import functools

import jax
import jax.numpy as jnp
from jax import lax
from jax.experimental import pallas as pl
from jax.experimental.pallas import tpu as pltpu
from jax.sharding import PartitionSpec as P

PIX_OWN = 131072
MAP_PRIOR = 1.0
BASE_PRIOR = 0.1
LANES = 128
OWNER_TILES = PIX_OWN // LANES
CHANNELS = 8
BLOCK = 256
CHUNK = 32
VMEM_BYTES = 32 * 1024 * 1024

SIN_TERMS = (1.0, -1.0 / 6, 1.0 / 120, -1.0 / 5040, 1.0 / 362880, -1.0 / 39916800, 1.0 / 6227020800)
COS_TERMS = (1.0, -0.5, 1.0 / 24, -1.0 / 720, 1.0 / 40320, -1.0 / 3628800, 1.0 / 479001600, -1.0 / 87178291200)
PI_PARTS = (3.140625, 0.0009670257568359375, 6.2771141529083252e-07)


def iota(shape, dim):
    return lax.broadcasted_iota(jnp.int32, shape, dim)


def log2(number):
    assert number & (number - 1) == 0
    return number.bit_length() - 1


def split3(x):
    high = x.astype(jnp.bfloat16)
    rest = x - high.astype(jnp.float32)
    middle = rest.astype(jnp.bfloat16)
    low = (rest - middle.astype(jnp.float32)).astype(jnp.bfloat16)
    return high, middle, low


def dot(a, b):
    return jnp.dot(a, b, preferred_element_type=jnp.float32)


def exact_dot(selector, x):
    high, middle, low = split3(x)
    return (dot(selector, high) + dot(selector, middle)) + dot(selector, low)


def horner(x, terms):
    total = jnp.full_like(x, terms[-1])
    for term in terms[-2::-1]:
        total = total * x + term
    return total


def cos_sin(angle):
    turns = jnp.round(angle * (1.0 / 3.14159265358979))
    rest = angle - turns * PI_PARTS[0]
    rest = rest - turns * PI_PARTS[1]
    rest = rest - turns * PI_PARTS[2]
    half = turns * 0.5
    sign = 1.0 - 4.0 * (half - jnp.floor(half))
    square = rest * rest
    cosine = sign * horner(square, COS_TERMS)
    sine = sign * rest * horner(square, SIN_TERMS)
    return cosine, sine


def spline_weights(fraction):
    square = fraction * fraction
    cube = square * fraction
    rest = 1.0 - fraction
    first = rest * rest * rest * (1.0 / 6.0)
    second = (3.0 * cube - 6.0 * square + 4.0) * (1.0 / 6.0)
    third = (-3.0 * cube + 3.0 * square + 3.0 * fraction + 1.0) * (1.0 / 6.0)
    fourth = cube * (1.0 / 6.0)
    return (first, second, third, fourth)


def lane_gather(table, index):
    return jnp.take_along_axis(table, index, axis=1, mode="promise_in_bounds")


def send_kernel(
    ranks, cap, patch_hbm, offset_hbm, search_hbm, left_hbm, cell_hbm, phase_hbm, out_ref,
    patch_ref, offset_ref, search_ref, left_ref, cell_ref, phase_ref, sems,
):
    pairs = (
        (patch_hbm, patch_ref), (offset_hbm, offset_ref), (search_hbm, search_ref),
        (left_hbm, left_ref), (cell_hbm, cell_ref), (phase_hbm, phase_ref),
    )
    copies = [pltpu.make_async_copy(src, dst, sems.at[k]) for k, (src, dst) in enumerate(pairs)]
    for copy in copies:
        copy.start()
    copies[0].wait()
    dets, columns = patch_ref.shape
    blocks = dets * columns
    samples = phase_ref.shape[1]
    nodes = search_ref.shape[0]
    span = lax.axis_index("tm")
    rows = 2 * cap + 1
    square = (blocks, blocks)
    tiles = jnp.concatenate(
        [jnp.broadcast_to(patch_ref[:, c : c + 1], (dets, LANES)) for c in range(columns)], axis=0
    )
    owner = (tiles >> log2(OWNER_TILES)).astype(jnp.float32)
    owner_t = owner.T
    same = owner == owner_t
    here, there = iota(square, 0), iota(square, 1)
    rank_row = jnp.sum(jnp.where(same & (here < there), 1.0, 0.0), axis=0, keepdims=True)
    rank_col = jnp.sum(jnp.where(same & (there < here), 1.0, 0.0), axis=1, keepdims=True)
    slot_row = (owner_t[0:1, :] * cap + rank_row).astype(jnp.int32)
    place = (iota((ranks * cap, blocks), 0) == slot_row).astype(jnp.bfloat16)
    lane = iota(square, 1)
    small = iota((dets, LANES), 1)
    det_lane = iota((dets, LANES), 0)
    for copy in copies[1:4]:
        copy.wait()
    offsets = jnp.broadcast_to(offset_ref[...], (dets, dets))
    diagonal = iota((dets, dets), 0) == iota((dets, dets), 1)
    shift = jnp.sum(jnp.where(diagonal, offsets, 0).astype(jnp.float32), axis=1, keepdims=True)
    shift = jnp.broadcast_to(shift.astype(jnp.int32), (dets, LANES))
    start = jnp.concatenate([c * LANES - shift for c in range(columns)], axis=0) + span * samples
    which = (iota(square, 0) & (dets - 1)) + 1
    rank = rank_col.astype(jnp.int32)
    listing = jnp.where(lane == rank, start, 0) + jnp.where(lane == rank + cap, which, 0)
    listing = listing + jnp.where(lane == rank + 2 * cap, tiles + 1, 0)
    chosen = (iota((ranks, blocks), 0).astype(jnp.float32) == owner_t[0:1, :]).astype(jnp.bfloat16)
    info = exact_dot(chosen, listing.astype(jnp.float32))
    knots = jnp.zeros((1, LANES), jnp.float32)
    for kind, ref in enumerate((search_ref, left_ref)):
        for n in range(nodes):
            column = jnp.broadcast_to(ref[n : n + 1, :], (dets, dets))
            column = jnp.sum(jnp.where(diagonal, column, 0.0), axis=1, keepdims=True)
            at = (3 * cap + kind * dets * nodes + n) + det_lane * nodes
            knots = knots + jnp.sum(jnp.where(small == at, column, 0.0), axis=0, keepdims=True)
    info = info + knots
    copies[4].wait()
    cells = jnp.concatenate([cell_ref[:, c * LANES : (c + 1) * LANES] for c in range(columns)], axis=0)
    slot_pixel = exact_dot(place, (tiles * LANES + cells).astype(jnp.float32))
    copies[5].wait()
    phases = jnp.concatenate([phase_ref[:, c * LANES : (c + 1) * LANES] for c in range(columns)], axis=0)
    slot_phase = exact_dot(place, phases)
    for o in range(ranks):
        out_ref[o * rows : o * rows + cap, :] = slot_phase[o * cap : (o + 1) * cap, :]
        out_ref[o * rows + cap : o * rows + 2 * cap, :] = slot_pixel[o * cap : (o + 1) * cap, :]
        out_ref[o * rows + 2 * cap : (o + 1) * rows, :] = info[o : o + 1, :]


def main_kernel(
    ranks, cap, dets, nodes, spacing, own_ref, other_ref, coeffs_hbm, out_ref, packs_ref, coeffs_ref,
    phase_ref, cell_ref, info_ref, meta_ref, few_phase, few_cell, few_info, table_ref,
    cos_ref, sin_ref, stream_ref, bin_ref, total_ref, turned_ref, sems,
):
    coeffs_copy = pltpu.make_async_copy(coeffs_hbm, coeffs_ref, sems.at[0])
    coeffs_copy.start()
    slots = ranks * cap
    rows = 2 * cap + 1
    knots = ranks * nodes
    width = dets * nodes
    pages = max(1, knots // LANES)
    group = lax.axis_index("det")
    packed = knots * dets // LANES
    per_row = LANES // width
    row_count = 2 * slots // LANES

    for half, ref in enumerate((own_ref, other_ref)):
        for o in range(ranks):
            here = half * slots + o * cap
            phase_ref[here : here + cap, :] = ref[o * rows : o * rows + cap, :]
            cell_ref[here : here + cap, :] = ref[o * rows + cap : o * rows + 2 * cap, :]
            info = ref[o * rows + 2 * cap : (o + 1) * rows, :]
            info_ref[here : here + cap, :] = jnp.broadcast_to(info, (cap, LANES))
            meta_ref[half, o : o + 1, :] = info

    lists = []
    spans = LANES // cap
    for half in range(2):
        for k in range(slots // LANES):
            names = meta_ref[half, k * spans : (k + 1) * spans, :]
            lane = iota((spans, LANES), 1)
            spread = lane_gather(names, 2 * cap + (lane & (cap - 1)))
            mine = (lane >> log2(cap)) == iota((spans, LANES), 0)
            lists.append(jnp.sum(jnp.where(mine, spread, 0.0), axis=0, keepdims=True))
    names = jnp.concatenate(lists, axis=0).astype(jnp.int32)
    mine = (names > 0) & (((names - 1) & 1) == group)
    ones = jnp.where(mine, 1.0, 0.0)
    earlier = (iota((LANES, LANES), 0) < iota((LANES, LANES), 1)).astype(jnp.bfloat16)
    rank = dot(ones.astype(jnp.bfloat16), earlier)
    sums = jnp.sum(ones, axis=1, keepdims=True)
    before = [jnp.zeros((1, 1), jnp.float32)]
    for k in range(row_count):
        before.append(before[-1] + sums[k : k + 1, :])
    rank = rank + jnp.concatenate(before[:-1], axis=0)
    rank = jnp.where(mine, rank, -1.0).astype(jnp.int32)
    number = jnp.sum(ones).astype(jnp.int32)
    blocks = (number + (BLOCK - 1)) >> log2(BLOCK)
    chunks = (number + (CHUNK - 1)) >> log2(CHUNK)

    tables = [[], []]
    for half in range(2):
        side = group if half == 0 else 1 - group
        packs = []
        for kind in range(2):
            for p in range(packed):
                names = meta_ref[half, p * per_row : (p + 1) * per_row, :]
                lane = iota((per_row, LANES), 1)
                spread = lane_gather(names, (3 * cap + kind * width) + (lane & (width - 1)))
                here = (lane >> log2(width)) == iota((per_row, LANES), 0)
                line = jnp.sum(jnp.where(here, spread, 0.0), axis=0, keepdims=True)
                packs_ref[kind, pl.ds(side * packed + p, 1), :] = line
                packs.append(line)
        lane = iota((dets, LANES), 1)
        for page in range(pages):
            knot = lane + page * LANES
            index = ((knot >> log2(nodes)) & (per_row - 1)) * width
            index = index + iota((dets, LANES), 0) * nodes + (knot & (nodes - 1))
            table = jnp.zeros((dets, LANES), jnp.float32)
            for p in range(packed):
                values = lane_gather(jnp.broadcast_to(packs[p], (dets, LANES)), index)
                table = jnp.where((knot >> log2(per_row * nodes)) == p, values, table)
            tables[half].append(table)

    slot = iota((slots, LANES), 0) & (cap - 1)
    lane = iota((slots, LANES), 1)
    listed = []
    for half in range(2):
        side = group if half == 0 else 1 - group
        found = lane_gather(info_ref[half * slots : (half + 1) * slots, :], jnp.minimum(lane, 2) * cap + slot)
        listed.append(found + jnp.where(lane == 1, (side * dets).astype(jnp.float32), 0.0))
    listed = jnp.concatenate(listed, axis=0)
    pixel = cell_ref[...]
    cell = (pixel - jnp.floor(pixel * (1.0 / LANES)) * LANES).astype(jnp.bfloat16)
    source = jnp.concatenate(split3(phase_ref[...]) + split3(listed) + (cell,), axis=1)

    def gather_block(block, carry):
        at = pl.multiple_of(block * BLOCK, BLOCK)
        down = iota((BLOCK, LANES), 0) + at
        place = jnp.concatenate(
            [(down == rank[k : k + 1, :]).astype(jnp.bfloat16) for k in range(row_count)], axis=1
        )
        taken = dot(place, source)
        parts = [taken[:, k * LANES : (k + 1) * LANES] for k in range(7)]
        few_phase[pl.ds(at, BLOCK), :] = (parts[0] + parts[1]) + parts[2]
        info = (parts[3] + parts[4]) + parts[5]
        few_info[pl.ds(at, BLOCK), :] = info
        few_cell[pl.ds(at, BLOCK), :] = parts[6]
        for k in range(BLOCK // LANES):
            turned_ref[pl.ds(block * (BLOCK // LANES) + k, 1), :] = info[k * LANES : (k + 1) * LANES, :].T[2:3, :]
        chosen = (info[:, 1:2] == (iota((BLOCK, LANES), 1) + 1).astype(jnp.float32)).astype(jnp.bfloat16)
        for page in range(pages):
            first, second = tables[0][page], tables[1][page]
            low = jnp.where(group == 0, first, second)
            high = jnp.where(group == 0, second, first)
            table = jnp.concatenate(
                [low, high, jnp.zeros((LANES - 2 * dets, LANES), jnp.float32)], axis=0
            )
            table_ref[page, pl.ds(at, BLOCK), :] = exact_dot(chosen, table)
        bin_ref[pl.ds(at * CHANNELS, BLOCK * CHANNELS), :] = jnp.zeros((BLOCK * CHANNELS, LANES), jnp.float32)
        return carry

    lax.fori_loop(0, blocks, gather_block, 0)

    def spline(at):
        start = jnp.broadcast_to(few_info[pl.ds(at, CHUNK), 0:1], (CHUNK, LANES)).astype(jnp.int32)
        time = start + iota((CHUNK, LANES), 1)
        interval = time >> log2(spacing)
        fraction = (time & (spacing - 1)).astype(jnp.float32) * (1.0 / spacing)
        return start >> log2(spacing), interval, spline_weights(fraction)

    def prepare(step, carry):
        at = pl.multiple_of(step * CHUNK, CHUNK)
        cosine, sine = cos_sin(2.0 * few_phase[pl.ds(at, CHUNK), :])
        _, interval, weights = spline(at)
        stream = jnp.zeros((CHUNK, LANES), jnp.float32)
        for term in range(4):
            knot = (interval + (term - 1)) & (knots - 1)
            value = lane_gather(table_ref[0, pl.ds(at, CHUNK), :], knot & (LANES - 1))
            for page in range(1, pages):
                more = lane_gather(table_ref[page, pl.ds(at, CHUNK), :], knot & (LANES - 1))
                value = jnp.where((knot >> log2(LANES)) == page, more, value)
            stream = stream + weights[term] * value
        cos_ref[pl.ds(at, CHUNK), :] = cosine
        sin_ref[pl.ds(at, CHUNK), :] = sine
        stream_ref[pl.ds(at, CHUNK), :] = stream
        return carry

    lax.fori_loop(0, chunks, prepare, 0)

    down = iota((LANES, 2 * LANES), 0).astype(jnp.float32).astype(jnp.bfloat16)
    channel = iota((CHANNELS, LANES), 0)
    zeros = jnp.zeros((4 * CHANNELS, LANES), jnp.bfloat16)

    def collect(step, carry):
        for k in range(CHUNK // 2):
            at = step * CHUNK + 2 * k
            pieces, cells = [], []
            for slot in (at, at + 1):
                stream = jnp.broadcast_to(stream_ref[pl.ds(slot, 1), :], (CHANNELS, LANES))
                cosine = jnp.broadcast_to(cos_ref[pl.ds(slot, 1), :], (CHANNELS, LANES))
                sine = jnp.broadcast_to(sin_ref[pl.ds(slot, 1), :], (CHANNELS, LANES))
                left = jnp.where(channel < 3, stream, jnp.where(channel < 6, 1.0, cosine))
                is_one = (channel == 0) | (channel == 3)
                is_sine = (channel == 2) | (channel == 5) | (channel == 7)
                right = jnp.where(is_one, 1.0, jnp.where(is_sine, sine, cosine))
                entry = left * right
                high = entry.astype(jnp.bfloat16).astype(jnp.float32)
                rest = entry - high
                middle = rest.astype(jnp.bfloat16).astype(jnp.float32)
                low = rest - middle
                stack = jnp.concatenate([high, middle, low, jnp.zeros_like(low)], axis=0)
                pieces.append(stack.astype(jnp.bfloat16))
                cells.append(jnp.broadcast_to(few_cell[pl.ds(slot, 1), :].astype(jnp.bfloat16), (LANES, LANES)))
            entry = jnp.concatenate(
                [
                    jnp.concatenate([pieces[0], zeros], axis=1),
                    jnp.concatenate([zeros, pieces[1]], axis=1),
                ],
                axis=0,
            )
            hits = jnp.where(jnp.concatenate(cells, axis=1) == down, jnp.bfloat16(1), jnp.bfloat16(0))
            sums = lax.dot_general(
                entry, hits, (((1,), (1,)), ((), ())), preferred_element_type=jnp.float32
            )
            for m in range(2):
                base = 4 * CHANNELS * m
                bin_ref[pl.ds((at + m) * CHANNELS, CHANNELS), :] = (
                    sums[base : base + CHANNELS] + sums[base + CHANNELS : base + 2 * CHANNELS]
                ) + sums[base + 2 * CHANNELS : base + 3 * CHANNELS]
        return carry

    lax.fori_loop(0, chunks, collect, 0)

    def merge(block, carry):
        at = pl.multiple_of(block * BLOCK, BLOCK)
        names = few_info[pl.ds(at, BLOCK), 2:3]

        def add(other, carry):
            there = pl.multiple_of(other * BLOCK, BLOCK)
            across = [
                turned_ref[pl.ds(other * (BLOCK // LANES) + k, 1), :] for k in range(BLOCK // LANES)
            ]
            same = (names == jnp.concatenate(across, axis=1)).astype(jnp.bfloat16)
            for c in range(CHANNELS):
                binned = bin_ref[pl.ds(there * CHANNELS + c, BLOCK, stride=CHANNELS), :]
                share = exact_dot(same, binned)
                before = total_ref[c, pl.ds(at, BLOCK), :]
                total_ref[c, pl.ds(at, BLOCK), :] = jnp.where(other == 0, share, before + share)
            return carry

        lax.fori_loop(0, blocks, add, 0)
        return carry

    lax.fori_loop(0, blocks, merge, 0)

    def project(step, lines):
        at = pl.multiple_of(step * CHUNK, CHUNK)
        here = pl.ds(at, CHUNK)
        signal, signal_cos, signal_sin, count, cos_sum, sin_sum, cos_cos, cos_sin_sum = (
            total_ref[c, here, :] for c in range(CHANNELS)
        )
        sin_sin = count - cos_cos
        stokes_i = count + MAP_PRIOR
        stokes_q = cos_cos + MAP_PRIOR
        stokes_u = sin_sin + MAP_PRIOR
        minor_one = stokes_q * stokes_u - cos_sin_sum * cos_sin_sum
        minor_two = sin_sum * cos_sin_sum - cos_sum * stokes_u
        minor_three = cos_sum * cos_sin_sum - sin_sum * stokes_q
        minor_four = stokes_i * stokes_u - sin_sum * sin_sum
        minor_five = cos_sum * sin_sum - stokes_i * cos_sin_sum
        minor_six = stokes_i * stokes_q - cos_sum * cos_sum
        determinant = stokes_i * minor_one + cos_sum * minor_two + sin_sum * minor_three
        scale = 1.0 / determinant
        map_i = (minor_one * signal + minor_two * signal_cos + minor_three * signal_sin) * scale
        map_q = (minor_two * signal + minor_four * signal_cos + minor_five * signal_sin) * scale
        map_u = (minor_three * signal + minor_five * signal_cos + minor_six * signal_sin) * scale
        cell = few_cell[here, :].astype(jnp.int32)
        projected = (
            lane_gather(map_i, cell) + cos_ref[here, :] * lane_gather(map_q, cell)
        ) + sin_ref[here, :] * lane_gather(map_u, cell)
        which = few_info[here, 1:2].astype(jnp.int32) - 1
        cleaned = jnp.where(which >= 0, stream_ref[here, :] - projected, 0.0)
        base, interval, weights = spline(at)
        early = interval == base
        lane = iota((CHUNK, LANES), 1)
        side = which >> log2(dets)
        det = which & (dets - 1)
        lines = list(lines)
        for term in range(5):
            low = weights[term] if term < 4 else 0.0
            high = weights[term - 1] if term > 0 else 0.0
            value = jnp.sum(jnp.where(early, low, high) * cleaned, axis=1, keepdims=True)
            knot = (base + (term - 1)) & (knots - 1)
            spot = side * (knots * dets) + (knot >> log2(nodes)) * width + det * nodes
            spot = spot + (knot & (nodes - 1))
            for p in range(2 * packed):
                part = jnp.where(lane + p * LANES == spot, value, 0.0)
                for q in range(CHUNK // 8):
                    lines[p] = lines[p] + part[q * 8 : (q + 1) * 8, :]
        return tuple(lines)

    lines = tuple(jnp.zeros((8, LANES), jnp.float32) for _ in range(2 * packed))
    lines = lax.fori_loop(0, chunks, project, lines)
    partial = jnp.concatenate([jnp.sum(line, axis=0, keepdims=True) for line in lines], axis=0)
    for target in range(out_ref.shape[0] // (2 * packed)):
        out_ref[target * 2 * packed : (target + 1) * 2 * packed, :] = partial
    coeffs_copy.wait()


def finish_kernel(
    ranks, spacing, arrived_ref, packs_ref, coeffs_ref, new_offset_ref, new_left_ref, new_search_ref,
):
    nodes, dets = coeffs_ref.shape
    height = packs_ref.shape[1]
    total = arrived_ref[0:height, :]
    for o in range(1, arrived_ref.shape[0] // height):
        total = total + arrived_ref[o * height : (o + 1) * height, :]
    search, left = packs_ref[0], packs_ref[1]
    image = total * (1.0 / spacing) + BASE_PRIOR * search
    norm_old = jnp.sum(left * left, keepdims=True)
    stride_factor = norm_old / jnp.sum(search * image, keepdims=True)
    fresh = left - stride_factor * image
    beta = jnp.sum(fresh * fresh, keepdims=True) / norm_old
    span, group = lax.axis_index("tm"), lax.axis_index("det")
    per_row = LANES // (dets * nodes)
    row = group * (height // 2) + (span >> log2(per_row))
    lane = iota((8, LANES), 1)
    first = (span & (per_row - 1)) * (dets * nodes)
    index = first + (lane & (dets - 1)) * nodes + (iota((8, LANES), 0) & (nodes - 1))
    here = iota((height, LANES), 0) == row

    def own(x):
        line = jnp.sum(jnp.where(here, x, 0.0), axis=0, keepdims=True)
        return lane_gather(jnp.broadcast_to(line, (8, LANES)), index)[:nodes, :dets]

    my_search = own(search)
    my_left = own(fresh)
    new_offset_ref[...] = coeffs_ref[...] + stride_factor * my_search
    new_left_ref[...] = my_left
    new_search_ref[...] = my_left + beta * my_search


def body(
    offset_coeffs,
    leftover_error,
    search_vector,
    node_lattice_offset,
    sky_cell_in_patch,
    analyser_reading_phase,
    segment_sky_patch,
):
    ranks, groups = lax.axis_size("tm"), lax.axis_size("det")
    dets, samples = analyser_reading_phase.shape
    nodes = search_vector.shape[1]
    spacing = samples // nodes
    blocks = segment_sky_patch.size
    cap = max(2, 2 * blocks // ranks)
    slots = ranks * cap
    rows = 2 * cap + 1
    height = groups * ranks * nodes * dets // LANES
    vmem = pl.BlockSpec(memory_space=pltpu.VMEM)
    hbm = pl.BlockSpec(memory_space=pltpu.HBM)
    pin = functools.partial(pltpu.with_memory_space_constraint, memory_space=pltpu.HBM)
    params = pltpu.CompilerParams(vmem_limit_bytes=VMEM_BYTES)
    inputs = (
        segment_sky_patch, node_lattice_offset.reshape(1, dets), search_vector.T, leftover_error.T,
        sky_cell_in_patch, analyser_reading_phase,
    )
    small = jax.ShapeDtypeStruct((nodes, dets), jnp.float32)

    outgoing = pl.pallas_call(
        functools.partial(send_kernel, ranks, cap),
        out_shape=jax.ShapeDtypeStruct((ranks * rows, LANES), jnp.float32),
        in_specs=[hbm] * len(inputs),
        out_specs=vmem,
        scratch_shapes=[pltpu.VMEM(x.shape, x.dtype) for x in inputs]
        + [pltpu.SemaphoreType.DMA((len(inputs),))],
        compiler_params=params,
        name="send",
    )(*[pin(x) for x in inputs])
    arrived = lax.all_to_all(
        outgoing.reshape(ranks, 1, rows * LANES), "tm", split_axis=0, concat_axis=0, tiled=True
    )
    swap = [(i, groups - 1 - i) for i in range(groups)]
    other = lax.ppermute(arrived, "det", swap)
    pages = max(1, ranks * nodes // LANES)
    big = pltpu.VMEM((2 * slots, LANES), jnp.float32)
    partials, packs, coeffs = pl.pallas_call(
        functools.partial(main_kernel, ranks, cap, dets, nodes, spacing),
        out_shape=(
            jax.ShapeDtypeStruct((ranks * groups * height, LANES), jnp.float32),
            jax.ShapeDtypeStruct((2, height, LANES), jnp.float32),
            small,
        ),
        in_specs=[vmem, vmem, hbm],
        out_specs=(vmem, vmem, vmem),
        scratch_shapes=[
            big, big, big,
            pltpu.VMEM((2, ranks, LANES), jnp.float32),
            big, big, big,
            pltpu.VMEM((pages, 2 * slots, LANES), jnp.float32),
            big, big, big,
            pltpu.VMEM((2 * slots * CHANNELS, LANES), jnp.float32),
            pltpu.VMEM((CHANNELS, 2 * slots, LANES), jnp.float32),
            pltpu.VMEM((max(8, 2 * slots // LANES), LANES), jnp.float32),
            pltpu.SemaphoreType.DMA((1,)),
        ],
        compiler_params=params,
        name="main",
    )(arrived.reshape(ranks * rows, LANES), other.reshape(ranks * rows, LANES), pin(offset_coeffs.T))
    gathered = lax.all_to_all(
        partials.reshape(ranks * groups, 1, height * LANES),
        ("tm", "det"), split_axis=0, concat_axis=0, tiled=True,
    )
    results = pl.pallas_call(
        functools.partial(finish_kernel, ranks, spacing),
        out_shape=(small, small, small),
        in_specs=[vmem] * 3,
        out_specs=(vmem, vmem, vmem),
        compiler_params=params,
        name="finish",
    )(gathered.reshape(ranks * groups * height, LANES), packs, coeffs)
    return tuple(result.T for result in results)


def solution(mesh):
    return jax.shard_map(
        body,
        mesh=mesh,
        in_specs=(
            P("det", "tm"),
            P("det", "tm"),
            P("det", "tm"),
            P("det"),
            P("det", "tm"),
            P("det", "tm"),
            P("det", "tm"),
        ),
        out_specs=(P("det", "tm"), P("det", "tm"), P("det", "tm")),
        check_vma=False,
    )
```

```python
import functools

import jax
import jax.numpy as jnp
from jax import lax
from jax.experimental import pallas as pl
from jax.experimental.pallas import tpu as pltpu
from jax.sharding import PartitionSpec as P

PIX_OWN = 131072
MAP_PRIOR = 1.0
BASE_PRIOR = 0.1
LANES = 128
OWNER_TILES = PIX_OWN // LANES
CHANNELS = 8
COUNT = 3
BLOCK = 192
PREPARE = 32
COLLECT = 32
PROJECT = 64
VMEM_BYTES = 32 * 1024 * 1024

SIN_TERMS = (1.0, -1.0 / 6, 1.0 / 120, -1.0 / 5040, 1.0 / 362880, -1.0 / 39916800, 1.0 / 6227020800)
COS_TERMS = (1.0, -0.5, 1.0 / 24, -1.0 / 720, 1.0 / 40320, -1.0 / 3628800, 1.0 / 479001600, -1.0 / 87178291200)
PI_PARTS = (3.140625, 0.0009670257568359375, 6.2771141529083252e-07)


def iota(shape, dim):
    return lax.broadcasted_iota(jnp.int32, shape, dim)


def log2(number):
    assert number & (number - 1) == 0
    return number.bit_length() - 1


def split3(x):
    high = x.astype(jnp.bfloat16)
    rest = x - high.astype(jnp.float32)
    middle = rest.astype(jnp.bfloat16)
    low = (rest - middle.astype(jnp.float32)).astype(jnp.bfloat16)
    return high, middle, low


def dot(a, b):
    return jnp.dot(a, b, preferred_element_type=jnp.float32)


def exact_dot(selector, x):
    high, middle, low = split3(x)
    return (dot(selector, high) + dot(selector, middle)) + dot(selector, low)


def horner(x, terms):
    total = jnp.full_like(x, terms[-1])
    for term in terms[-2::-1]:
        total = total * x + term
    return total


def cos_sin(angle):
    turns = jnp.round(angle * (1.0 / 3.14159265358979))
    rest = angle - turns * PI_PARTS[0]
    rest = rest - turns * PI_PARTS[1]
    rest = rest - turns * PI_PARTS[2]
    half = turns * 0.5
    sign = 1.0 - 4.0 * (half - jnp.floor(half))
    square = rest * rest
    cosine = sign * horner(square, COS_TERMS)
    sine = sign * rest * horner(square, SIN_TERMS)
    return cosine, sine


def spline_weights(fraction):
    square = fraction * fraction
    cube = square * fraction
    rest = 1.0 - fraction
    first = rest * rest * rest * (1.0 / 6.0)
    second = (3.0 * cube - 6.0 * square + 4.0) * (1.0 / 6.0)
    third = (-3.0 * cube + 3.0 * square + 3.0 * fraction + 1.0) * (1.0 / 6.0)
    fourth = cube * (1.0 / 6.0)
    return (first, second, third, fourth)


def lane_gather(table, index):
    return jnp.take_along_axis(table, index, axis=1, mode="promise_in_bounds")


def send_kernel(
    ranks, cap, patch_hbm, offset_hbm, search_hbm, left_hbm, cell_hbm, phase_hbm, out_ref,
    patch_ref, offset_ref, search_ref, left_ref, cell_ref, phase_ref, sems,
):
    pairs = (
        (patch_hbm, patch_ref), (offset_hbm, offset_ref), (search_hbm, search_ref),
        (left_hbm, left_ref), (cell_hbm, cell_ref), (phase_hbm, phase_ref),
    )
    copies = [pltpu.make_async_copy(src, dst, sems.at[k]) for k, (src, dst) in enumerate(pairs)]
    for copy in copies:
        copy.start()
    copies[0].wait()
    dets, columns = patch_ref.shape
    blocks = dets * columns
    samples = phase_ref.shape[1]
    nodes = search_ref.shape[0]
    span = lax.axis_index("tm")
    rows = 2 * cap + 1
    square = (blocks, blocks)
    tiles = jnp.concatenate(
        [jnp.broadcast_to(patch_ref[:, c : c + 1], (dets, LANES)) for c in range(columns)], axis=0
    )
    owner = (tiles >> log2(OWNER_TILES)).astype(jnp.float32)
    owner_t = owner.T
    same = owner == owner_t
    here, there = iota(square, 0), iota(square, 1)
    rank_row = jnp.sum(jnp.where(same & (here < there), 1.0, 0.0), axis=0, keepdims=True)
    rank_col = jnp.sum(jnp.where(same & (there < here), 1.0, 0.0), axis=1, keepdims=True)
    slot_row = (owner_t[0:1, :] * cap + rank_row).astype(jnp.int32)
    place = (iota((ranks * cap, blocks), 0) == slot_row).astype(jnp.bfloat16)
    lane = iota(square, 1)
    small = iota((dets, LANES), 1)
    det_lane = iota((dets, LANES), 0)
    for copy in copies[1:4]:
        copy.wait()
    offsets = jnp.broadcast_to(offset_ref[...], (dets, dets))
    diagonal = iota((dets, dets), 0) == iota((dets, dets), 1)
    shift = jnp.sum(jnp.where(diagonal, offsets, 0).astype(jnp.float32), axis=1, keepdims=True)
    shift = jnp.broadcast_to(shift.astype(jnp.int32), (dets, LANES))
    start = jnp.concatenate([c * LANES - shift for c in range(columns)], axis=0) + span * samples
    which = (iota(square, 0) & (dets - 1)) + 1
    rank = rank_col.astype(jnp.int32)
    listing = jnp.where(lane == rank, start, 0) + jnp.where(lane == rank + cap, which, 0)
    listing = listing + jnp.where(lane == rank + 2 * cap, tiles + 1, 0)
    chosen = (iota((ranks, blocks), 0).astype(jnp.float32) == owner_t[0:1, :]).astype(jnp.bfloat16)
    info = exact_dot(chosen, listing.astype(jnp.float32))
    knots = jnp.zeros((1, LANES), jnp.float32)
    for kind, ref in enumerate((search_ref, left_ref)):
        for n in range(nodes):
            column = jnp.broadcast_to(ref[n : n + 1, :], (dets, dets))
            column = jnp.sum(jnp.where(diagonal, column, 0.0), axis=1, keepdims=True)
            at = (3 * cap + kind * dets * nodes + n) + det_lane * nodes
            knots = knots + jnp.sum(jnp.where(small == at, column, 0.0), axis=0, keepdims=True)
    info = info + knots
    copies[4].wait()
    cells = jnp.concatenate([cell_ref[:, c * LANES : (c + 1) * LANES] for c in range(columns)], axis=0)
    slot_pixel = exact_dot(place, (tiles * LANES + cells).astype(jnp.float32))
    copies[5].wait()
    phases = jnp.concatenate([phase_ref[:, c * LANES : (c + 1) * LANES] for c in range(columns)], axis=0)
    slot_phase = exact_dot(place, phases)
    for o in range(ranks):
        out_ref[o * rows : o * rows + cap, :] = slot_phase[o * cap : (o + 1) * cap, :]
        out_ref[o * rows + cap : o * rows + 2 * cap, :] = slot_pixel[o * cap : (o + 1) * cap, :]
        out_ref[o * rows + 2 * cap : (o + 1) * rows, :] = info[o : o + 1, :]


def main_kernel(
    ranks, cap, dets, nodes, spacing, own_ref, other_ref, coeffs_hbm, out_ref, packs_ref, coeffs_ref,
    phase_ref, cell_ref, info_ref, meta_ref, few_phase, few_cell, few_info, table_ref,
    cos_ref, sin_ref, stream_ref, bin_ref, total_ref, turned_ref, sems,
):
    coeffs_copy = pltpu.make_async_copy(coeffs_hbm, coeffs_ref, sems.at[0])
    coeffs_copy.start()
    slots = ranks * cap
    rows = 2 * cap + 1
    knots = ranks * nodes
    width = dets * nodes
    pages = max(1, knots // LANES)
    group = lax.axis_index("det")
    packed = knots * dets // LANES
    per_row = LANES // width
    row_count = 2 * slots // LANES

    for half, ref in enumerate((own_ref, other_ref)):
        for o in range(ranks):
            here = half * slots + o * cap
            phase_ref[here : here + cap, :] = ref[o * rows : o * rows + cap, :]
            cell_ref[here : here + cap, :] = ref[o * rows + cap : o * rows + 2 * cap, :]
            info = ref[o * rows + 2 * cap : (o + 1) * rows, :]
            info_ref[here : here + cap, :] = jnp.broadcast_to(info, (cap, LANES))
            meta_ref[half, o : o + 1, :] = info

    lists = []
    spans = LANES // cap
    for half in range(2):
        for k in range(slots // LANES):
            names = meta_ref[half, k * spans : (k + 1) * spans, :]
            lane = iota((spans, LANES), 1)
            spread = lane_gather(names, 2 * cap + (lane & (cap - 1)))
            mine = (lane >> log2(cap)) == iota((spans, LANES), 0)
            lists.append(jnp.sum(jnp.where(mine, spread, 0.0), axis=0, keepdims=True))
    names = jnp.concatenate(lists, axis=0).astype(jnp.int32)
    mine = (names > 0) & (((names - 1) & 1) == group)
    ones = jnp.where(mine, 1.0, 0.0)
    earlier = (iota((LANES, LANES), 0) < iota((LANES, LANES), 1)).astype(jnp.bfloat16)
    rank = dot(ones.astype(jnp.bfloat16), earlier)
    sums = jnp.sum(ones, axis=1, keepdims=True)
    before = [jnp.zeros((1, 1), jnp.float32)]
    for k in range(row_count):
        before.append(before[-1] + sums[k : k + 1, :])
    rank = rank + jnp.concatenate(before[:-1], axis=0)
    rank = jnp.where(mine, rank, -1.0).astype(jnp.int32)
    number = jnp.sum(ones).astype(jnp.int32)
    blocks = sum(
        jnp.where(number > start, 1, 0) for start in range(0, 2 * slots, BLOCK)
    )

    def steps(chunk):
        return (number + (chunk - 1)) >> log2(chunk)

    tables = [[], []]
    for half in range(2):
        side = group if half == 0 else 1 - group
        packs = []
        for kind in range(2):
            for p in range(packed):
                names = meta_ref[half, p * per_row : (p + 1) * per_row, :]
                lane = iota((per_row, LANES), 1)
                spread = lane_gather(names, (3 * cap + kind * width) + (lane & (width - 1)))
                here = (lane >> log2(width)) == iota((per_row, LANES), 0)
                line = jnp.sum(jnp.where(here, spread, 0.0), axis=0, keepdims=True)
                packs_ref[kind, pl.ds(side * packed + p, 1), :] = line
                packs.append(line)
        lane = iota((dets, LANES), 1)
        for page in range(pages):
            knot = lane + page * LANES
            index = ((knot >> log2(nodes)) & (per_row - 1)) * width
            index = index + iota((dets, LANES), 0) * nodes + (knot & (nodes - 1))
            table = jnp.zeros((dets, LANES), jnp.float32)
            for p in range(packed):
                values = lane_gather(jnp.broadcast_to(packs[p], (dets, LANES)), index)
                table = jnp.where((knot >> log2(per_row * nodes)) == p, values, table)
            tables[half].append(table)

    slot = iota((slots, LANES), 0) & (cap - 1)
    lane = iota((slots, LANES), 1)
    listed = []
    for half in range(2):
        side = group if half == 0 else 1 - group
        found = lane_gather(info_ref[half * slots : (half + 1) * slots, :], jnp.minimum(lane, 2) * cap + slot)
        listed.append(found + jnp.where(lane == 1, (side * dets).astype(jnp.float32), 0.0))
    listed = jnp.concatenate(listed, axis=0)
    pixel = cell_ref[...]
    cell = (pixel - jnp.floor(pixel * (1.0 / LANES)) * LANES).astype(jnp.bfloat16)
    whole = split3(listed)
    if max(ranks * nodes * spacing, ranks * OWNER_TILES) <= 65536:
        whole = whole[:2]
    source = jnp.concatenate(split3(phase_ref[...]) + (cell,) + whole, axis=1)

    def gather_block(block, carry):
        at = pl.multiple_of(block * BLOCK, 64)
        down = iota((BLOCK, LANES), 0) + at
        place = jnp.concatenate(
            [(down == rank[k : k + 1, :]).astype(jnp.bfloat16) for k in range(row_count)], axis=1
        )
        taken = dot(place, source)
        parts = [taken[:, k * LANES : (k + 1) * LANES] for k in range(4 + len(whole))]
        few_phase[pl.ds(at, BLOCK), :] = (parts[0] + parts[1]) + parts[2]
        info = sum(parts[5:], parts[4])
        few_info[pl.ds(at, BLOCK), :] = info
        few_cell[pl.ds(at, BLOCK), :] = parts[3]
        turned_ref[pl.ds(block, 1), :] = info.T[2:3, :]
        chosen = (info[:, 1:2] == (iota((BLOCK, LANES), 1) + 1).astype(jnp.float32)).astype(jnp.bfloat16)
        for page in range(pages):
            first, second = tables[0][page], tables[1][page]
            low = jnp.where(group == 0, first, second)
            high = jnp.where(group == 0, second, first)
            table = jnp.concatenate(
                [low, high, jnp.zeros((LANES - 2 * dets, LANES), jnp.float32)], axis=0
            )
            table_ref[page, pl.ds(at, BLOCK), :] = exact_dot(chosen, table)
        bin_ref[pl.ds(at * CHANNELS, BLOCK * CHANNELS), :] = jnp.zeros((BLOCK * CHANNELS, LANES), jnp.float32)
        return carry

    lax.fori_loop(0, blocks, gather_block, 0)

    def spline(at, chunk):
        start = jnp.broadcast_to(few_info[pl.ds(at, chunk), 0:1], (chunk, LANES)).astype(jnp.int32)
        time = start + iota((chunk, LANES), 1)
        interval = time >> log2(spacing)
        fraction = (time & (spacing - 1)).astype(jnp.float32) * (1.0 / spacing)
        return start >> log2(spacing), interval, spline_weights(fraction)

    def prepare(step, carry):
        at = pl.multiple_of(step * PREPARE, PREPARE)
        cosine, sine = cos_sin(2.0 * few_phase[pl.ds(at, PREPARE), :])
        _, interval, weights = spline(at, PREPARE)
        stream = jnp.zeros((PREPARE, LANES), jnp.float32)
        for term in range(4):
            knot = (interval + (term - 1)) & (knots - 1)
            value = lane_gather(table_ref[0, pl.ds(at, PREPARE), :], knot & (LANES - 1))
            for page in range(1, pages):
                more = lane_gather(table_ref[page, pl.ds(at, PREPARE), :], knot & (LANES - 1))
                value = jnp.where((knot >> log2(LANES)) == page, more, value)
            stream = stream + weights[term] * value
        cos_ref[pl.ds(at, PREPARE), :] = cosine
        sin_ref[pl.ds(at, PREPARE), :] = sine
        stream_ref[pl.ds(at, PREPARE), :] = stream
        return carry


    down = iota((LANES, 2 * LANES), 0).astype(jnp.float32).astype(jnp.bfloat16)
    channel = iota((CHANNELS, LANES), 0)
    zeros = jnp.zeros((2 * CHANNELS, LANES), jnp.bfloat16)

    def collect(step, carry):
        for k in range(COLLECT // 2):
            at = step * COLLECT + 2 * k
            pieces, cells = [], []
            for slot in (at, at + 1):
                stream = jnp.broadcast_to(stream_ref[pl.ds(slot, 1), :], (CHANNELS, LANES))
                cosine = jnp.broadcast_to(cos_ref[pl.ds(slot, 1), :], (CHANNELS, LANES))
                sine = jnp.broadcast_to(sin_ref[pl.ds(slot, 1), :], (CHANNELS, LANES))
                left = jnp.where(channel < 3, stream, jnp.where(channel < 6, 1.0, cosine))
                is_one = (channel == 0) | (channel == 3)
                is_sine = (channel == 2) | (channel == 5) | (channel == 7)
                right = jnp.where(is_one, 1.0, jnp.where(is_sine, sine, cosine))
                entry = left * right
                high = entry.astype(jnp.bfloat16).astype(jnp.float32)
                rest = entry - high
                stack = jnp.concatenate([high, rest], axis=0)
                pieces.append(stack.astype(jnp.bfloat16))
                cells.append(jnp.broadcast_to(few_cell[pl.ds(slot, 1), :].astype(jnp.bfloat16), (LANES, LANES)))
            entry = jnp.concatenate(
                [
                    jnp.concatenate([pieces[0], zeros], axis=1),
                    jnp.concatenate([zeros, pieces[1]], axis=1),
                ],
                axis=0,
            )
            hits = jnp.where(jnp.concatenate(cells, axis=1) == down, jnp.bfloat16(1), jnp.bfloat16(0))
            sums = lax.dot_general(
                entry, hits, (((1,), (1,)), ((), ())), preferred_element_type=jnp.float32
            )
            for m in range(2):
                base = 2 * CHANNELS * m
                bin_ref[pl.ds((at + m) * CHANNELS, CHANNELS), :] = (
                    sums[base : base + CHANNELS] + sums[base + CHANNELS : base + 2 * CHANNELS]
                )
        return prepare(step + 1, carry)

    prepare(0, 0)
    lax.fori_loop(0, steps(COLLECT), collect, 0)

    def merge(block, carry):
        at = pl.multiple_of(block * BLOCK, 64)
        names = few_info[pl.ds(at, BLOCK), 2:3]

        def add(other, carry):
            there = pl.multiple_of(other * BLOCK, 64)
            same = (names == turned_ref[pl.ds(other, 1), :]).astype(jnp.bfloat16)
            for c in range(CHANNELS):
                binned = bin_ref[pl.ds(there * CHANNELS + c, BLOCK, stride=CHANNELS), :]
                high = binned.astype(jnp.bfloat16)
                share = dot(same, high)
                if c != COUNT:
                    share = share + dot(same, (binned - high.astype(jnp.float32)).astype(jnp.bfloat16))
                before = total_ref[c, pl.ds(at, BLOCK), :]
                total_ref[c, pl.ds(at, BLOCK), :] = jnp.where(other == 0, share, before + share)
            return carry

        lax.fori_loop(0, blocks, add, 0)
        return carry

    lax.fori_loop(0, blocks, merge, 0)

    def project(step, lines):
        at = pl.multiple_of(step * PROJECT, PROJECT)
        here = pl.ds(at, PROJECT)
        signal, signal_cos, signal_sin, count, cos_sum, sin_sum, cos_cos, cos_sin_sum = (
            total_ref[c, here, :] for c in range(CHANNELS)
        )
        sin_sin = count - cos_cos
        stokes_i = count + MAP_PRIOR
        stokes_q = cos_cos + MAP_PRIOR
        stokes_u = sin_sin + MAP_PRIOR
        minor_one = stokes_q * stokes_u - cos_sin_sum * cos_sin_sum
        minor_two = sin_sum * cos_sin_sum - cos_sum * stokes_u
        minor_three = cos_sum * cos_sin_sum - sin_sum * stokes_q
        minor_four = stokes_i * stokes_u - sin_sum * sin_sum
        minor_five = cos_sum * sin_sum - stokes_i * cos_sin_sum
        minor_six = stokes_i * stokes_q - cos_sum * cos_sum
        determinant = stokes_i * minor_one + cos_sum * minor_two + sin_sum * minor_three
        scale = 1.0 / determinant
        map_i = (minor_one * signal + minor_two * signal_cos + minor_three * signal_sin) * scale
        map_q = (minor_two * signal + minor_four * signal_cos + minor_five * signal_sin) * scale
        map_u = (minor_three * signal + minor_five * signal_cos + minor_six * signal_sin) * scale
        cell = few_cell[here, :].astype(jnp.int32)
        projected = (
            lane_gather(map_i, cell) + cos_ref[here, :] * lane_gather(map_q, cell)
        ) + sin_ref[here, :] * lane_gather(map_u, cell)
        which = few_info[here, 1:2].astype(jnp.int32) - 1
        cleaned = jnp.where(which >= 0, stream_ref[here, :] - projected, 0.0)
        base, interval, weights = spline(at, PROJECT)
        early = interval == base
        lane = iota((PROJECT, LANES), 1)
        side = which >> log2(dets)
        det = which & (dets - 1)
        lines = list(lines)
        for term in range(5):
            low = weights[term] if term < 4 else 0.0
            high = weights[term - 1] if term > 0 else 0.0
            value = jnp.sum(jnp.where(early, low, high) * cleaned, axis=1, keepdims=True)
            knot = (base + (term - 1)) & (knots - 1)
            spot = side * (knots * dets) + (knot >> log2(nodes)) * width + det * nodes
            spot = spot + (knot & (nodes - 1))
            for p in range(2 * packed):
                part = jnp.where(lane + p * LANES == spot, value, 0.0)
                for q in range(PROJECT // 8):
                    lines[p] = lines[p] + part[q * 8 : (q + 1) * 8, :]
        return tuple(lines)

    lines = tuple(jnp.zeros((8, LANES), jnp.float32) for _ in range(2 * packed))
    lines = lax.fori_loop(0, steps(PROJECT), project, lines)
    partial = jnp.concatenate([jnp.sum(line, axis=0, keepdims=True) for line in lines], axis=0)
    for target in range(out_ref.shape[0] // (2 * packed)):
        out_ref[target * 2 * packed : (target + 1) * 2 * packed, :] = partial
    coeffs_copy.wait()


def finish_kernel(
    ranks, spacing, arrived_ref, packs_ref, coeffs_ref, new_offset_ref, new_left_ref, new_search_ref,
):
    nodes, dets = coeffs_ref.shape
    height = packs_ref.shape[1]
    total = arrived_ref[0:height, :]
    for o in range(1, arrived_ref.shape[0] // height):
        total = total + arrived_ref[o * height : (o + 1) * height, :]
    search, left = packs_ref[0], packs_ref[1]
    image = total * (1.0 / spacing) + BASE_PRIOR * search
    norm_old = jnp.sum(left * left, keepdims=True)
    stride_factor = norm_old / jnp.sum(search * image, keepdims=True)
    fresh = left - stride_factor * image
    beta = jnp.sum(fresh * fresh, keepdims=True) / norm_old
    span, group = lax.axis_index("tm"), lax.axis_index("det")
    per_row = LANES // (dets * nodes)
    row = group * (height // 2) + (span >> log2(per_row))
    lane = iota((8, LANES), 1)
    first = (span & (per_row - 1)) * (dets * nodes)
    index = first + (lane & (dets - 1)) * nodes + (iota((8, LANES), 0) & (nodes - 1))
    here = iota((height, LANES), 0) == row

    def own(x):
        line = jnp.sum(jnp.where(here, x, 0.0), axis=0, keepdims=True)
        return lane_gather(jnp.broadcast_to(line, (8, LANES)), index)[:nodes, :dets]

    my_search = own(search)
    my_left = own(fresh)
    new_offset_ref[...] = coeffs_ref[...] + stride_factor * my_search
    new_left_ref[...] = my_left
    new_search_ref[...] = my_left + beta * my_search


def body(
    offset_coeffs,
    leftover_error,
    search_vector,
    node_lattice_offset,
    sky_cell_in_patch,
    analyser_reading_phase,
    segment_sky_patch,
):
    ranks, groups = lax.axis_size("tm"), lax.axis_size("det")
    dets, samples = analyser_reading_phase.shape
    nodes = search_vector.shape[1]
    spacing = samples // nodes
    blocks = segment_sky_patch.size
    cap = max(2, 2 * blocks // ranks)
    slots = ranks * cap
    rows = 2 * cap + 1
    height = groups * ranks * nodes * dets // LANES
    vmem = pl.BlockSpec(memory_space=pltpu.VMEM)
    hbm = pl.BlockSpec(memory_space=pltpu.HBM)
    pin = functools.partial(pltpu.with_memory_space_constraint, memory_space=pltpu.HBM)
    params = pltpu.CompilerParams(vmem_limit_bytes=VMEM_BYTES)
    inputs = (
        segment_sky_patch, node_lattice_offset.reshape(1, dets), search_vector.T, leftover_error.T,
        sky_cell_in_patch, analyser_reading_phase,
    )
    small = jax.ShapeDtypeStruct((nodes, dets), jnp.float32)

    outgoing = pl.pallas_call(
        functools.partial(send_kernel, ranks, cap),
        out_shape=jax.ShapeDtypeStruct((ranks * rows, LANES), jnp.float32),
        in_specs=[hbm] * len(inputs),
        out_specs=vmem,
        scratch_shapes=[pltpu.VMEM(x.shape, x.dtype) for x in inputs]
        + [pltpu.SemaphoreType.DMA((len(inputs),))],
        compiler_params=params,
        name="send",
    )(*[pin(x) for x in inputs])
    arrived = lax.all_to_all(
        outgoing.reshape(ranks, 1, rows * LANES), "tm", split_axis=0, concat_axis=0, tiled=True
    )
    swap = [(i, groups - 1 - i) for i in range(groups)]
    other = lax.ppermute(arrived, "det", swap)
    pages = max(1, ranks * nodes // LANES)
    big = pltpu.VMEM((2 * slots, LANES), jnp.float32)
    room = pl.cdiv(2 * slots, BLOCK) * BLOCK + max(PREPARE, COLLECT, PROJECT)
    few = pltpu.VMEM((room, LANES), jnp.float32)
    partials, packs, coeffs = pl.pallas_call(
        functools.partial(main_kernel, ranks, cap, dets, nodes, spacing),
        out_shape=(
            jax.ShapeDtypeStruct((ranks * groups * height, LANES), jnp.float32),
            jax.ShapeDtypeStruct((2, height, LANES), jnp.float32),
            small,
        ),
        in_specs=[vmem, vmem, hbm],
        out_specs=(vmem, vmem, vmem),
        scratch_shapes=[
            big, big, big,
            pltpu.VMEM((2, ranks, LANES), jnp.float32),
            few, few, few,
            pltpu.VMEM((pages, room, LANES), jnp.float32),
            few, few, few,
            pltpu.VMEM((room * CHANNELS, LANES), jnp.float32),
            pltpu.VMEM((CHANNELS, room, LANES), jnp.float32),
            pltpu.VMEM((8, BLOCK), jnp.float32),
            pltpu.SemaphoreType.DMA((1,)),
        ],
        compiler_params=params,
        name="main",
    )(arrived.reshape(ranks * rows, LANES), other.reshape(ranks * rows, LANES), pin(offset_coeffs.T))
    gathered = lax.all_to_all(
        partials.reshape(ranks * groups, 1, height * LANES),
        ("tm", "det"), split_axis=0, concat_axis=0, tiled=True,
    )
    results = pl.pallas_call(
        functools.partial(finish_kernel, ranks, spacing),
        out_shape=(small, small, small),
        in_specs=[vmem] * 3,
        out_specs=(vmem, vmem, vmem),
        compiler_params=params,
        name="finish",
    )(gathered.reshape(ranks * groups * height, LANES), packs, coeffs)
    return tuple(result.T for result in results)


def solution(mesh):
    return jax.shard_map(
        body,
        mesh=mesh,
        in_specs=(
            P("det", "tm"),
            P("det", "tm"),
            P("det", "tm"),
            P("det"),
            P("det", "tm"),
            P("det", "tm"),
            P("det", "tm"),
        ),
        out_specs=(P("det", "tm"), P("det", "tm"), P("det", "tm")),
        check_vma=False,
    )
```

```python
import functools

import jax
import jax.numpy as jnp
from jax import lax
from jax.experimental import pallas as pl
from jax.experimental.pallas import tpu as pltpu
from jax.sharding import PartitionSpec as P

PIX_OWN = 131072
MAP_PRIOR = 1.0
BASE_PRIOR = 0.1
LANES = 128
OWNER_TILES = PIX_OWN // LANES
CHANNELS = 8
COUNT = 3
BLOCK = 160
COLLECT = 32
PROJECT = 80
VMEM_BYTES = 32 * 1024 * 1024

SIN_TERMS = (1.0, -1.0 / 6, 1.0 / 120, -1.0 / 5040, 1.0 / 362880, -1.0 / 39916800, 1.0 / 6227020800)
COS_TERMS = (1.0, -0.5, 1.0 / 24, -1.0 / 720, 1.0 / 40320, -1.0 / 3628800, 1.0 / 479001600, -1.0 / 87178291200)
PI_PARTS = (3.140625, 0.0009670257568359375, 6.2771141529083252e-07)


def iota(shape, dim):
    return lax.broadcasted_iota(jnp.int32, shape, dim)


def log2(number):
    assert number & (number - 1) == 0
    return number.bit_length() - 1


def split3(x):
    high = x.astype(jnp.bfloat16)
    rest = x - high.astype(jnp.float32)
    middle = rest.astype(jnp.bfloat16)
    low = (rest - middle.astype(jnp.float32)).astype(jnp.bfloat16)
    return high, middle, low


def dot(a, b):
    return jnp.dot(a, b, preferred_element_type=jnp.float32)


def exact_dot(selector, x):
    high, middle, low = split3(x)
    return (dot(selector, high) + dot(selector, middle)) + dot(selector, low)


def horner(x, terms):
    total = jnp.full_like(x, terms[-1])
    for term in terms[-2::-1]:
        total = total * x + term
    return total


def cos_sin(angle):
    turns = jnp.round(angle * (1.0 / 3.14159265358979))
    rest = angle - turns * PI_PARTS[0]
    rest = rest - turns * PI_PARTS[1]
    rest = rest - turns * PI_PARTS[2]
    half = turns * 0.5
    sign = 1.0 - 4.0 * (half - jnp.floor(half))
    square = rest * rest
    cosine = sign * horner(square, COS_TERMS)
    sine = sign * rest * horner(square, SIN_TERMS)
    return cosine, sine


def spline_weights(fraction):
    square = fraction * fraction
    cube = square * fraction
    rest = 1.0 - fraction
    first = rest * rest * rest * (1.0 / 6.0)
    second = (3.0 * cube - 6.0 * square + 4.0) * (1.0 / 6.0)
    third = (-3.0 * cube + 3.0 * square + 3.0 * fraction + 1.0) * (1.0 / 6.0)
    fourth = cube * (1.0 / 6.0)
    return (first, second, third, fourth)


def lane_gather(table, index):
    return jnp.take_along_axis(table, index, axis=1, mode="promise_in_bounds")


def send_kernel(
    ranks, cap, patch_hbm, offset_hbm, search_hbm, left_hbm, cell_hbm, phase_hbm, out_ref,
    patch_ref, offset_ref, search_ref, left_ref, cell_ref, phase_ref, sems,
):
    pairs = (
        (patch_hbm, patch_ref), (offset_hbm, offset_ref), (search_hbm, search_ref),
        (left_hbm, left_ref), (cell_hbm, cell_ref), (phase_hbm, phase_ref),
    )
    copies = [pltpu.make_async_copy(src, dst, sems.at[k]) for k, (src, dst) in enumerate(pairs)]
    for copy in copies:
        copy.start()
    copies[0].wait()
    dets, columns = patch_ref.shape
    blocks = dets * columns
    samples = phase_ref.shape[1]
    nodes = search_ref.shape[0]
    span = lax.axis_index("tm")
    rows = 2 * cap + 1
    square = (blocks, blocks)
    tiles = jnp.concatenate(
        [jnp.broadcast_to(patch_ref[:, c : c + 1], (dets, LANES)) for c in range(columns)], axis=0
    )
    owner = (tiles >> log2(OWNER_TILES)).astype(jnp.float32)
    owner_t = owner.T
    same = owner == owner_t
    here, there = iota(square, 0), iota(square, 1)
    rank_row = jnp.sum(jnp.where(same & (here < there), 1.0, 0.0), axis=0, keepdims=True)
    rank_col = jnp.sum(jnp.where(same & (there < here), 1.0, 0.0), axis=1, keepdims=True)
    slot_row = (owner_t[0:1, :] * cap + rank_row).astype(jnp.int32)
    place = (iota((ranks * cap, blocks), 0) == slot_row).astype(jnp.bfloat16)
    lane = iota(square, 1)
    small = iota((dets, LANES), 1)
    det_lane = iota((dets, LANES), 0)
    for copy in copies[1:4]:
        copy.wait()
    offsets = jnp.broadcast_to(offset_ref[...], (dets, dets))
    diagonal = iota((dets, dets), 0) == iota((dets, dets), 1)
    shift = jnp.sum(jnp.where(diagonal, offsets, 0).astype(jnp.float32), axis=1, keepdims=True)
    shift = jnp.broadcast_to(shift.astype(jnp.int32), (dets, LANES))
    start = jnp.concatenate([c * LANES - shift for c in range(columns)], axis=0) + span * samples
    which = (iota(square, 0) & (dets - 1)) + 1
    rank = rank_col.astype(jnp.int32)
    listing = jnp.where(lane == rank, start, 0) + jnp.where(lane == rank + cap, which, 0)
    listing = listing + jnp.where(lane == rank + 2 * cap, tiles + 1, 0)
    chosen = (iota((ranks, blocks), 0).astype(jnp.float32) == owner_t[0:1, :]).astype(jnp.bfloat16)
    info = exact_dot(chosen, listing.astype(jnp.float32))
    knots = jnp.zeros((1, LANES), jnp.float32)
    for kind, ref in enumerate((search_ref, left_ref)):
        for n in range(nodes):
            column = jnp.broadcast_to(ref[n : n + 1, :], (dets, dets))
            column = jnp.sum(jnp.where(diagonal, column, 0.0), axis=1, keepdims=True)
            at = (3 * cap + kind * dets * nodes + n) + det_lane * nodes
            knots = knots + jnp.sum(jnp.where(small == at, column, 0.0), axis=0, keepdims=True)
    info = info + knots
    copies[4].wait()
    cells = jnp.concatenate([cell_ref[:, c * LANES : (c + 1) * LANES] for c in range(columns)], axis=0)
    pixels = (tiles * LANES + cells).astype(jnp.float32)
    copies[5].wait()
    phases = jnp.concatenate([phase_ref[:, c * LANES : (c + 1) * LANES] for c in range(columns)], axis=0)
    moved = exact_dot(place, jnp.concatenate([phases, pixels], axis=1))
    slot_phase, slot_pixel = moved[:, :LANES], moved[:, LANES:]
    for o in range(ranks):
        out_ref[o * rows : o * rows + cap, :] = slot_phase[o * cap : (o + 1) * cap, :]
        out_ref[o * rows + cap : o * rows + 2 * cap, :] = slot_pixel[o * cap : (o + 1) * cap, :]
        out_ref[o * rows + 2 * cap : (o + 1) * rows, :] = info[o : o + 1, :]


def unpack(ranks, cap, ref, phase_ref, cell_ref, info_ref, meta_ref):
    rows = 2 * cap + 1
    for o in range(ranks):
        here = o * cap
        phase_ref[here : here + cap, :] = ref[o * rows : o * rows + cap, :]
        cell_ref[here : here + cap, :] = ref[o * rows + cap : o * rows + 2 * cap, :]
        info = ref[o * rows + 2 * cap : (o + 1) * rows, :]
        info_ref[here : here + cap, :] = jnp.broadcast_to(info, (cap, LANES))
        meta_ref[o : o + 1, :] = info


def rank_slots(ranks, cap, meta_ref):
    lists = []
    spans = LANES // cap
    for k in range(ranks * cap // LANES):
        names = meta_ref[k * spans : (k + 1) * spans, :]
        lane = iota((spans, LANES), 1)
        spread = lane_gather(names, 2 * cap + (lane & (cap - 1)))
        mine = (lane >> log2(cap)) == iota((spans, LANES), 0)
        lists.append(jnp.sum(jnp.where(mine, spread, 0.0), axis=0, keepdims=True))
    names = jnp.concatenate(lists, axis=0).astype(jnp.int32)
    mine = (names > 0) & (((names - 1) & 1) == lax.axis_index("det"))
    ones = jnp.where(mine, 1.0, 0.0)
    earlier = (iota((LANES, LANES), 0) < iota((LANES, LANES), 1)).astype(jnp.bfloat16)
    rank = dot(ones.astype(jnp.bfloat16), earlier)
    sums = jnp.sum(ones, axis=1, keepdims=True)
    before = [jnp.zeros((1, 1), jnp.float32)]
    for k in range(len(lists)):
        before.append(before[-1] + sums[k : k + 1, :])
    rank = rank + jnp.concatenate(before[:-1], axis=0)
    return jnp.where(mine, rank, -1.0).astype(jnp.int32), jnp.sum(ones).astype(jnp.int32)


def flatten(pages, knots):
    dets = pages[0].shape[0]
    if knots >= LANES:
        return [page[d : d + 1, :] for d in range(dets) for page in pages]
    lane, det = iota((dets, LANES), 1), iota((dets, LANES), 0)
    spread = lane_gather(pages[0], lane & (knots - 1))
    per_row = LANES // knots
    mine = (det & (per_row - 1)) == (lane >> log2(knots))
    spread = jnp.where(mine, spread, 0.0)
    rows = []
    for first in range(0, dets, per_row):
        rows.append(jnp.sum(spread[first : first + per_row, :], axis=0, keepdims=True))
    return rows


def read_knots(ranks, cap, dets, nodes, meta_ref):
    width = dets * nodes
    knots = ranks * nodes
    per_row = LANES // width
    kinds = []
    for kind in range(2):
        lines = []
        for p in range(ranks // per_row):
            names = meta_ref[p * per_row : (p + 1) * per_row, :]
            lane = iota((per_row, LANES), 1)
            spread = lane_gather(names, (3 * cap + kind * width) + (lane & (width - 1)))
            here = (lane >> log2(width)) == iota((per_row, LANES), 0)
            lines.append(jnp.sum(jnp.where(here, spread, 0.0), axis=0, keepdims=True))
        lane = iota((dets, LANES), 1)
        tables = []
        for page in range(max(1, knots // LANES)):
            knot = lane + page * LANES
            index = ((knot >> log2(nodes)) & (per_row - 1)) * width
            index = index + iota((dets, LANES), 0) * nodes + (knot & (nodes - 1))
            table = jnp.zeros((dets, LANES), jnp.float32)
            for p, line in enumerate(lines):
                values = lane_gather(jnp.broadcast_to(line, (dets, LANES)), index)
                table = jnp.where((knot >> log2(per_row * nodes)) == p, values, table)
            tables.append(table)
        kinds.append(tables)
    return kinds


def source_of(ranks, cap, dets, total, side, phase_ref, cell_ref, info_ref):
    slots = ranks * cap
    slot = iota((slots, LANES), 0) & (cap - 1)
    lane = iota((slots, LANES), 1)
    listed = lane_gather(info_ref[...], jnp.minimum(lane, 2) * cap + slot)
    listed = listed + jnp.where(lane == 1, (side * dets).astype(jnp.float32), 0.0)
    pixel = cell_ref[...]
    cell = (pixel - jnp.floor(pixel * (1.0 / LANES)) * LANES).astype(jnp.bfloat16)
    whole = split3(listed)
    if max(total, ranks * OWNER_TILES) <= 65536:
        whole = whole[:2]
    return jnp.concatenate(split3(phase_ref[...]) + (cell,) + whole, axis=1)


def take_slots(at, rank, source, dets, side, tables):
    down = iota((BLOCK, LANES), 0) + at
    place = jnp.concatenate(
        [(down == rank[k : k + 1, :]).astype(jnp.bfloat16) for k in range(rank.shape[0])], axis=1
    )
    taken = dot(place, source)
    parts = [taken[:, k * LANES : (k + 1) * LANES] for k in range(taken.shape[1] // LANES)]
    phase = (parts[0] + parts[1]) + parts[2]
    info = sum(parts[5:], parts[4])
    lane = iota((BLOCK, LANES), 1) + (1 + side * dets)
    chosen = ((info[:, 1:2] == lane.astype(jnp.float32)) & (iota((BLOCK, LANES), 1) < dets)).astype(jnp.bfloat16)
    empty = jnp.zeros((LANES - dets, LANES), jnp.float32)
    knots = [exact_dot(chosen, jnp.concatenate([table, empty], axis=0)) for table in tables]
    return phase, parts[3], info, knots


def spline(info_ref, spacing, at, chunk):
    start = jnp.broadcast_to(info_ref[pl.ds(at, chunk), 0:1], (chunk, LANES)).astype(jnp.int32)
    time = start + iota((chunk, LANES), 1)
    interval = time >> log2(spacing)
    fraction = (time & (spacing - 1)).astype(jnp.float32) * (1.0 / spacing)
    return start >> log2(spacing), interval, spline_weights(fraction)


def five_weights(early, weights):
    padded = (0.0,) + weights + (0.0,)
    return [jnp.where(early, padded[term + 1], padded[term]) for term in range(5)]


def bin_chunks(first, last, knots, spacing, few_phase, few_cell, few_info, table_ref, cos_ref, sin_ref, stream_ref, basis_ref, bin_ref):
    pages = table_ref.shape[0]

    def prepare(step):
        at = pl.multiple_of(step * COLLECT, COLLECT)
        cosine, sine = cos_sin(2.0 * few_phase[pl.ds(at, COLLECT), :])
        base, interval, weights = spline(few_info, spacing, at, COLLECT)
        for term, weight in enumerate(five_weights(interval == base, weights)):
            basis_ref[term, pl.ds(at, COLLECT), :] = weight
        stream = jnp.zeros((COLLECT, LANES), jnp.float32)
        for term in range(4):
            knot = (interval + (term - 1)) & (knots - 1)
            value = lane_gather(table_ref[0, pl.ds(at, COLLECT), :], knot & (LANES - 1))
            for page in range(1, pages):
                more = lane_gather(table_ref[page, pl.ds(at, COLLECT), :], knot & (LANES - 1))
                value = jnp.where((knot >> log2(LANES)) == page, more, value)
            stream = stream + weights[term] * value
        cos_ref[pl.ds(at, COLLECT), :] = cosine
        sin_ref[pl.ds(at, COLLECT), :] = sine
        stream_ref[pl.ds(at, COLLECT), :] = stream

    down = iota((LANES, 2 * LANES), 0).astype(jnp.float32).astype(jnp.bfloat16)
    channel = iota((CHANNELS, LANES), 0)
    zeros = jnp.zeros((2 * CHANNELS, LANES), jnp.bfloat16)

    def collect(step, carry):
        for k in range(COLLECT // 2):
            at = step * COLLECT + 2 * k
            pieces, cells = [], []
            for slot in (at, at + 1):
                stream = jnp.broadcast_to(stream_ref[pl.ds(slot, 1), :], (CHANNELS, LANES))
                cosine = jnp.broadcast_to(cos_ref[pl.ds(slot, 1), :], (CHANNELS, LANES))
                sine = jnp.broadcast_to(sin_ref[pl.ds(slot, 1), :], (CHANNELS, LANES))
                left = jnp.where(channel < 3, stream, jnp.where(channel < 6, 1.0, cosine))
                is_one = (channel == 0) | (channel == 3)
                is_sine = (channel == 2) | (channel == 5) | (channel == 7)
                right = jnp.where(is_one, 1.0, jnp.where(is_sine, sine, cosine))
                entry = left * right
                high = entry.astype(jnp.bfloat16).astype(jnp.float32)
                rest = entry - high
                stack = jnp.concatenate([high, rest], axis=0)
                pieces.append(stack.astype(jnp.bfloat16))
                cells.append(jnp.broadcast_to(few_cell[pl.ds(slot, 1), :].astype(jnp.bfloat16), (LANES, LANES)))
            entry = jnp.concatenate(
                [
                    jnp.concatenate([pieces[0], zeros], axis=1),
                    jnp.concatenate([zeros, pieces[1]], axis=1),
                ],
                axis=0,
            )
            hits = jnp.where(jnp.concatenate(cells, axis=1) == down, jnp.bfloat16(1), jnp.bfloat16(0))
            sums = lax.dot_general(
                entry, hits, (((1,), (1,)), ((), ())), preferred_element_type=jnp.float32
            )
            for m in range(2):
                base = 2 * CHANNELS * m
                bin_ref[pl.ds((at + m) * CHANNELS, CHANNELS), :] = (
                    sums[base : base + CHANNELS] + sums[base + CHANNELS : base + 2 * CHANNELS]
                )
        prepare(step + 1)
        return carry

    prepare(first)
    lax.fori_loop(first, last, collect, 0)


def own_kernel(
    ranks, cap, dets, nodes, spacing, own_ref,
    few_phase, few_cell, few_info, table_ref, cos_ref, sin_ref, stream_ref, basis_ref, bin_ref, packs_ref, count_ref,
    phase_ref, cell_ref, info_ref, meta_ref,
):
    knots = ranks * nodes
    side = lax.axis_index("det")
    unpack(ranks, cap, own_ref, phase_ref, cell_ref, info_ref, meta_ref)
    rank, number = rank_slots(ranks, cap, meta_ref)
    count_ref[...] = jnp.full((8, LANES), number, jnp.int32)
    tables, left = read_knots(ranks, cap, dets, nodes, meta_ref)
    packs_ref[...] = jnp.concatenate(flatten(tables, knots) + flatten(left, knots), axis=0)
    source = source_of(ranks, cap, dets, knots * spacing, side, phase_ref, cell_ref, info_ref)

    def gather_block(block, carry):
        here = pl.ds(pl.multiple_of(block * BLOCK, 32), BLOCK)
        few_phase[here, :], few_cell[here, :], few_info[here, :], found = take_slots(
            block * BLOCK, rank, source, dets, side, tables
        )
        for page, rows in enumerate(found):
            table_ref[page, here, :] = rows
        return carry

    lax.fori_loop(0, block_count(number, ranks * cap), gather_block, 0)
    bin_chunks(
        0, number >> log2(COLLECT), knots, spacing, few_phase, few_cell, few_info, table_ref,
        cos_ref, sin_ref, stream_ref, basis_ref, bin_ref,
    )


def block_count(number, most):
    return sum(jnp.where(number > start, 1, 0) for start in range(0, most, BLOCK))


def main_kernel(
    ranks, cap, dets, nodes, spacing, other_ref, coeffs_hbm, packs_own, count_ref, *refs,
):
    few_phase, few_cell, few_info, table_ref, cos_ref, sin_ref, stream_ref, basis_ref, bin_ref = refs[9:18]
    out_ref, packs_ref, coeffs_ref = refs[18:21]
    phase_ref, cell_ref, info_ref, meta_ref, total_ref, turned_ref, knots_ref, sems = refs[21:]
    coeffs_copy = pltpu.make_async_copy(coeffs_hbm, coeffs_ref, sems.at[0])
    coeffs_copy.start()
    slots = ranks * cap
    knots = ranks * nodes
    packed = knots * dets // LANES
    group = lax.axis_index("det")
    side = 1 - group

    unpack(ranks, cap, other_ref, phase_ref, cell_ref, info_ref, meta_ref)
    rank, more = rank_slots(ranks, cap, meta_ref)
    ready = jnp.max(count_ref[...])
    rank = jnp.where(rank >= 0, rank + ready, -1)
    number = ready + more
    tables, left = read_knots(ranks, cap, dets, nodes, meta_ref)
    for kind, pages in enumerate((tables, left)):
        here = slice(kind * packed, (kind + 1) * packed)
        packs_ref[kind, pl.ds(group * packed, packed), :] = packs_own[here, :]
        packs_ref[kind, pl.ds(side * packed, packed), :] = jnp.concatenate(flatten(pages, knots), axis=0)
    source = source_of(ranks, cap, dets, knots * spacing, side, phase_ref, cell_ref, info_ref)
    blocks = block_count(number, 2 * slots)
    ready_blocks = block_count(ready, slots)

    def gather_block(block, carry):
        here = pl.ds(pl.multiple_of(block * BLOCK, 32), BLOCK)
        started = block < ready_blocks
        phase, cell, info, found = take_slots(block * BLOCK, rank, source, dets, side, tables)
        few_phase[here, :] = jnp.where(started, few_phase[here, :], 0.0) + phase
        few_cell[here, :] = jnp.where(started, few_cell[here, :], 0.0) + cell
        info = jnp.where(started, few_info[here, :], 0.0) + info
        few_info[here, :] = info
        turned = info.T
        turned_ref[0, pl.ds(block, 1), :] = turned[1:2, :]
        turned_ref[1, pl.ds(block, 1), :] = turned[2:3, :]
        for page, rows in enumerate(found):
            table_ref[page, here, :] = jnp.where(started, table_ref[page, here, :], 0.0) + rows
        return carry

    lax.fori_loop(0, blocks, gather_block, 0)

    def steps(chunk):
        return (number + (chunk - 1)) >> log2(chunk)

    bin_chunks(
        ready >> log2(COLLECT), steps(COLLECT), knots, spacing, few_phase, few_cell, few_info, table_ref,
        cos_ref, sin_ref, stream_ref, basis_ref, bin_ref,
    )

    def clear(step, carry):
        at = pl.multiple_of(step * COLLECT * CHANNELS, COLLECT * CHANNELS)
        bin_ref[pl.ds(at, COLLECT * CHANNELS), :] = jnp.zeros((COLLECT * CHANNELS, LANES), jnp.float32)
        return carry

    lax.fori_loop(steps(COLLECT), blocks * (BLOCK // COLLECT), clear, 0)

    def merge(block, carry):
        at = pl.multiple_of(block * BLOCK, 32)
        names = few_info[pl.ds(at, BLOCK), 2:3]

        def add(other, carry):
            there = pl.multiple_of(other * BLOCK, 32)
            same = (names == turned_ref[1, pl.ds(other, 1), :]).astype(jnp.bfloat16)
            for c in range(CHANNELS):
                binned = bin_ref[pl.ds(there * CHANNELS + c, BLOCK, stride=CHANNELS), :]
                high = binned.astype(jnp.bfloat16)
                share = dot(same, high)
                if c != COUNT:
                    share = share + dot(same, (binned - high.astype(jnp.float32)).astype(jnp.bfloat16))
                before = total_ref[c, pl.ds(at, BLOCK), :]
                total_ref[c, pl.ds(at, BLOCK), :] = jnp.where(other == 0, share, before + share)
            return carry

        lax.fori_loop(0, blocks, add, 0)
        return carry

    lax.fori_loop(0, blocks, merge, 0)

    def project(at):
        here = pl.ds(pl.multiple_of(at, 16), PROJECT)
        signal, signal_cos, signal_sin, count, cos_sum, sin_sum, cos_cos, cos_sin_sum = (
            total_ref[c, here, :] for c in range(CHANNELS)
        )
        sin_sin = count - cos_cos
        stokes_i = count + MAP_PRIOR
        stokes_q = cos_cos + MAP_PRIOR
        stokes_u = sin_sin + MAP_PRIOR
        minor_one = stokes_q * stokes_u - cos_sin_sum * cos_sin_sum
        minor_two = sin_sum * cos_sin_sum - cos_sum * stokes_u
        minor_three = cos_sum * cos_sin_sum - sin_sum * stokes_q
        minor_four = stokes_i * stokes_u - sin_sum * sin_sum
        minor_five = cos_sum * sin_sum - stokes_i * cos_sin_sum
        minor_six = stokes_i * stokes_q - cos_sum * cos_sum
        determinant = stokes_i * minor_one + cos_sum * minor_two + sin_sum * minor_three
        scale = 1.0 / determinant
        map_i = (minor_one * signal + minor_two * signal_cos + minor_three * signal_sin) * scale
        map_q = (minor_two * signal + minor_four * signal_cos + minor_five * signal_sin) * scale
        map_u = (minor_three * signal + minor_five * signal_cos + minor_six * signal_sin) * scale
        cell = few_cell[here, :].astype(jnp.int32)
        projected = (
            lane_gather(map_i, cell) + cos_ref[here, :] * lane_gather(map_q, cell)
        ) + sin_ref[here, :] * lane_gather(map_u, cell)
        cleaned = stream_ref[here, :] - projected
        valid = few_info[here, 1:2] > 0.5
        base = few_info[here, 0:1].astype(jnp.int32) >> log2(spacing)
        lane = iota((PROJECT, LANES), 1)
        pages = [jnp.zeros((PROJECT, LANES), jnp.float32) for _ in range(knots_ref.shape[0])]
        for term in range(5):
            value = jnp.sum(basis_ref[term, here, :] * cleaned, axis=1, keepdims=True)
            knot = (base + (term - 1)) & (knots - 1)
            for page in range(len(pages)):
                pages[page] = pages[page] + jnp.where(lane + page * LANES == knot, value, 0.0)
        for page, sums in enumerate(pages):
            knots_ref[page, here, :] = jnp.where(valid, sums, 0.0)

    def image_of(block, sums):
        at = pl.multiple_of(block * BLOCK, 32)
        for first in range(0, BLOCK, PROJECT):
            project(at + first)
        det = (iota((2 * dets, BLOCK), 0) + 1).astype(jnp.float32)
        chosen = (turned_ref[0, pl.ds(block, 1), :] == det).astype(jnp.bfloat16)
        return tuple(
            total + exact_dot(chosen, knots_ref[page, pl.ds(at, BLOCK), :]) for page, total in enumerate(sums)
        )

    image = tuple(jnp.zeros((2 * dets, LANES), jnp.float32) for _ in range(knots_ref.shape[0]))
    image = lax.fori_loop(0, blocks, image_of, image)
    partial = jnp.concatenate(flatten(image, knots), axis=0)
    for target in range(out_ref.shape[0] // (2 * packed)):
        out_ref[target * 2 * packed : (target + 1) * 2 * packed, :] = partial
    coeffs_copy.wait()


def finish_kernel(
    ranks, spacing, arrived_ref, packs_ref, coeffs_ref, new_offset_ref, new_left_ref, new_search_ref,
):
    nodes, dets = coeffs_ref.shape
    height = packs_ref.shape[1]
    total = arrived_ref[0:height, :]
    for o in range(1, arrived_ref.shape[0] // height):
        total = total + arrived_ref[o * height : (o + 1) * height, :]
    search, left = packs_ref[0], packs_ref[1]
    image = total * (1.0 / spacing) + BASE_PRIOR * search
    norm_old = jnp.sum(left * left, keepdims=True)
    stride_factor = norm_old / jnp.sum(search * image, keepdims=True)
    fresh = left - stride_factor * image
    beta = jnp.sum(fresh * fresh, keepdims=True) / norm_old
    span, group = lax.axis_index("tm"), lax.axis_index("det")
    lines = height // 2
    knots = lines * LANES // dets
    place = (iota((8, LANES), 1) & (dets - 1)) * knots + span * nodes + (iota((8, LANES), 0) & (nodes - 1))

    def own(x):
        x = jnp.where(group == 0, x[:lines, :], x[lines:, :])
        found = jnp.zeros((8, LANES), jnp.float32)
        for p in range(lines):
            values = lane_gather(jnp.broadcast_to(x[p : p + 1, :], (8, LANES)), place & (LANES - 1))
            found = jnp.where((place >> log2(LANES)) == p, values, found)
        return found[:nodes, :dets]

    my_search = own(search)
    my_left = own(fresh)
    new_offset_ref[...] = coeffs_ref[...] + stride_factor * my_search
    new_left_ref[...] = my_left
    new_search_ref[...] = my_left + beta * my_search


def body(
    offset_coeffs,
    leftover_error,
    search_vector,
    node_lattice_offset,
    sky_cell_in_patch,
    analyser_reading_phase,
    segment_sky_patch,
):
    ranks, groups = lax.axis_size("tm"), lax.axis_size("det")
    dets, samples = analyser_reading_phase.shape
    nodes = search_vector.shape[1]
    spacing = samples // nodes
    blocks = segment_sky_patch.size
    cap = max(2, 2 * blocks // ranks)
    slots = ranks * cap
    rows = 2 * cap + 1
    height = groups * ranks * nodes * dets // LANES
    vmem = pl.BlockSpec(memory_space=pltpu.VMEM)
    hbm = pl.BlockSpec(memory_space=pltpu.HBM)
    pin = functools.partial(pltpu.with_memory_space_constraint, memory_space=pltpu.HBM)
    params = pltpu.CompilerParams(vmem_limit_bytes=VMEM_BYTES)
    inputs = (
        segment_sky_patch, node_lattice_offset.reshape(1, dets), search_vector.T, leftover_error.T,
        sky_cell_in_patch, analyser_reading_phase,
    )
    small = jax.ShapeDtypeStruct((nodes, dets), jnp.float32)

    outgoing = pl.pallas_call(
        functools.partial(send_kernel, ranks, cap),
        out_shape=jax.ShapeDtypeStruct((ranks * rows, LANES), jnp.float32),
        in_specs=[hbm] * len(inputs),
        out_specs=vmem,
        scratch_shapes=[pltpu.VMEM(x.shape, x.dtype) for x in inputs]
        + [pltpu.SemaphoreType.DMA((len(inputs),))],
        compiler_params=params,
        name="send",
    )(*[pin(x) for x in inputs])
    arrived = lax.all_to_all(
        outgoing.reshape(ranks, 1, rows * LANES), "tm", split_axis=0, concat_axis=0, tiled=True
    )
    swap = [(i, groups - 1 - i) for i in range(groups)]
    other = lax.ppermute(arrived, "det", swap)
    pages = max(1, ranks * nodes // LANES)
    f32 = jnp.float32
    room = pl.cdiv(2 * slots, BLOCK) * BLOCK + max(COLLECT, PROJECT)
    few = jax.ShapeDtypeStruct((room, LANES), f32)
    shared = (
        few, few, few, jax.ShapeDtypeStruct((pages, room, LANES), f32), few, few, few,
        jax.ShapeDtypeStruct((5, room, LANES), f32),
        jax.ShapeDtypeStruct((room * CHANNELS, LANES), f32),
    )
    arrival = [pltpu.VMEM((slots, LANES), f32)] * 3 + [pltpu.VMEM((ranks, LANES), f32)]
    sizes = (ranks, cap, dets, nodes, spacing)
    *state, packs, count = pl.pallas_call(
        functools.partial(own_kernel, *sizes),
        out_shape=shared + (
            jax.ShapeDtypeStruct((2 * height // groups, LANES), f32),
            jax.ShapeDtypeStruct((8, LANES), jnp.int32),
        ),
        in_specs=[vmem],
        out_specs=(vmem,) * 11,
        scratch_shapes=arrival,
        compiler_params=params,
        cost_estimate=pl.CostEstimate(flops=4_000_000_000, bytes_accessed=4_000_000, transcendentals=0),
        name="own",
    )(arrived.reshape(ranks * rows, LANES))
    *_, partials, packs, coeffs = pl.pallas_call(
        functools.partial(main_kernel, *sizes),
        out_shape=shared + (
            jax.ShapeDtypeStruct((ranks * groups * height, LANES), f32),
            jax.ShapeDtypeStruct((2, height, LANES), f32),
            small,
        ),
        in_specs=[vmem, hbm] + [vmem] * 11,
        out_specs=(vmem,) * 12,
        scratch_shapes=arrival + [
            pltpu.VMEM((CHANNELS, room, LANES), f32),
            pltpu.VMEM((2, 8, BLOCK), f32),
            pltpu.VMEM((pages, room, LANES), f32),
            pltpu.SemaphoreType.DMA((1,)),
        ],
        input_output_aliases={4 + k: k for k in range(9)},
        compiler_params=params,
        name="main",
    )(other.reshape(ranks * rows, LANES), pin(offset_coeffs.T), packs, count, *state)
    gathered = lax.all_to_all(
        partials.reshape(ranks * groups, 1, height * LANES),
        ("tm", "det"), split_axis=0, concat_axis=0, tiled=True,
    )
    results = pl.pallas_call(
        functools.partial(finish_kernel, ranks, spacing),
        out_shape=(small, small, small),
        in_specs=[vmem] * 3,
        out_specs=(vmem, vmem, vmem),
        compiler_params=params,
        name="finish",
    )(gathered.reshape(ranks * groups * height, LANES), packs, coeffs)
    return tuple(result.T for result in results)


def solution(mesh):
    return jax.shard_map(
        body,
        mesh=mesh,
        in_specs=(
            P("det", "tm"),
            P("det", "tm"),
            P("det", "tm"),
            P("det"),
            P("det", "tm"),
            P("det", "tm"),
            P("det", "tm"),
        ),
        out_specs=(P("det", "tm"), P("det", "tm"), P("det", "tm")),
        check_vma=False,
    )
```

```python
import functools

import jax
import jax.numpy as jnp
from jax import lax
from jax.experimental import pallas as pl
from jax.experimental.pallas import tpu as pltpu
from jax.sharding import PartitionSpec as P

PIX_OWN = 131072
MAP_PRIOR = 1.0
BASE_PRIOR = 0.1
LANES = 128
OWNER_TILES = PIX_OWN // LANES
CHANNELS = 8
COUNT = 3
BLOCK = 160
COLLECT = 32
PROJECT = 80
VMEM_BYTES = 32 * 1024 * 1024

SIN_TERMS = (1.0, -1.0 / 6, 1.0 / 120, -1.0 / 5040, 1.0 / 362880, -1.0 / 39916800, 1.0 / 6227020800)
COS_TERMS = (1.0, -0.5, 1.0 / 24, -1.0 / 720, 1.0 / 40320, -1.0 / 3628800, 1.0 / 479001600, -1.0 / 87178291200)
PI_PARTS = (3.140625, 0.0009670257568359375, 6.2771141529083252e-07)


def iota(shape, dim):
    return lax.broadcasted_iota(jnp.int32, shape, dim)


def log2(number):
    assert number & (number - 1) == 0
    return number.bit_length() - 1


def split3(x):
    high = x.astype(jnp.bfloat16)
    rest = x - high.astype(jnp.float32)
    middle = rest.astype(jnp.bfloat16)
    low = (rest - middle.astype(jnp.float32)).astype(jnp.bfloat16)
    return high, middle, low


def dot(a, b):
    return jnp.dot(a, b, preferred_element_type=jnp.float32)


def exact_dot(selector, x):
    high, middle, low = split3(x)
    return (dot(selector, high) + dot(selector, middle)) + dot(selector, low)


def horner(x, terms):
    total = jnp.full_like(x, terms[-1])
    for term in terms[-2::-1]:
        total = total * x + term
    return total


def cos_sin(angle):
    turns = jnp.round(angle * (1.0 / 3.14159265358979))
    rest = angle - turns * PI_PARTS[0]
    rest = rest - turns * PI_PARTS[1]
    rest = rest - turns * PI_PARTS[2]
    half = turns * 0.5
    sign = 1.0 - 4.0 * (half - jnp.floor(half))
    square = rest * rest
    cosine = sign * horner(square, COS_TERMS)
    sine = sign * rest * horner(square, SIN_TERMS)
    return cosine, sine


def spline_weights(fraction):
    square = fraction * fraction
    cube = square * fraction
    rest = 1.0 - fraction
    first = rest * rest * rest * (1.0 / 6.0)
    second = (3.0 * cube - 6.0 * square + 4.0) * (1.0 / 6.0)
    third = (-3.0 * cube + 3.0 * square + 3.0 * fraction + 1.0) * (1.0 / 6.0)
    fourth = cube * (1.0 / 6.0)
    return (first, second, third, fourth)


def aligned(index, unit):
    return index if isinstance(index, int) else pl.multiple_of(index, unit)


def lane_gather(table, index):
    return jnp.take_along_axis(table, index, axis=1, mode="promise_in_bounds")


def send_kernel(
    ranks, cap, patch_hbm, offset_hbm, search_hbm, left_hbm, cell_hbm, phase_hbm, out_ref,
    patch_ref, offset_ref, search_ref, left_ref, cell_ref, phase_ref, sems,
):
    pairs = (
        (patch_hbm, patch_ref), (offset_hbm, offset_ref), (search_hbm, search_ref),
        (left_hbm, left_ref), (cell_hbm, cell_ref), (phase_hbm, phase_ref),
    )
    copies = [pltpu.make_async_copy(src, dst, sems.at[k]) for k, (src, dst) in enumerate(pairs)]
    for copy in copies:
        copy.start()
    copies[0].wait()
    dets, columns = patch_ref.shape
    blocks = dets * columns
    samples = phase_ref.shape[1]
    nodes = search_ref.shape[0]
    span = lax.axis_index("tm")
    rows = 2 * cap + 1
    square = (blocks, blocks)
    tiles = jnp.concatenate(
        [jnp.broadcast_to(patch_ref[:, c : c + 1], (dets, LANES)) for c in range(columns)], axis=0
    )
    owner = (tiles >> log2(OWNER_TILES)).astype(jnp.float32)
    owner_t = owner.T
    same = owner == owner_t
    here, there = iota(square, 0), iota(square, 1)
    rank_row = jnp.sum(jnp.where(same & (here < there), 1.0, 0.0), axis=0, keepdims=True)
    rank_col = jnp.sum(jnp.where(same & (there < here), 1.0, 0.0), axis=1, keepdims=True)
    slot_row = (owner_t[0:1, :] * cap + rank_row).astype(jnp.int32)
    place = (iota((ranks * cap, blocks), 0) == slot_row).astype(jnp.bfloat16)
    lane = iota(square, 1)
    small = iota((dets, LANES), 1)
    det_lane = iota((dets, LANES), 0)
    for copy in copies[1:4]:
        copy.wait()
    offsets = jnp.broadcast_to(offset_ref[...], (dets, dets))
    diagonal = iota((dets, dets), 0) == iota((dets, dets), 1)
    shift = jnp.sum(jnp.where(diagonal, offsets, 0).astype(jnp.float32), axis=1, keepdims=True)
    shift = jnp.broadcast_to(shift.astype(jnp.int32), (dets, LANES))
    start = jnp.concatenate([c * LANES - shift for c in range(columns)], axis=0) + span * samples
    which = (iota(square, 0) & (dets - 1)) + 1
    rank = rank_col.astype(jnp.int32)
    listing = jnp.where(lane == rank, start, 0) + jnp.where(lane == rank + cap, which, 0)
    listing = listing + jnp.where(lane == rank + 2 * cap, tiles + 1, 0)
    chosen = (iota((ranks, blocks), 0).astype(jnp.float32) == owner_t[0:1, :]).astype(jnp.bfloat16)
    info = exact_dot(chosen, listing.astype(jnp.float32))
    knots = jnp.zeros((1, LANES), jnp.float32)
    for kind, ref in enumerate((search_ref, left_ref)):
        for n in range(nodes):
            column = jnp.broadcast_to(ref[n : n + 1, :], (dets, dets))
            column = jnp.sum(jnp.where(diagonal, column, 0.0), axis=1, keepdims=True)
            at = (3 * cap + kind * dets * nodes + n) + det_lane * nodes
            knots = knots + jnp.sum(jnp.where(small == at, column, 0.0), axis=0, keepdims=True)
    info = info + knots
    copies[4].wait()
    cells = jnp.concatenate([cell_ref[:, c * LANES : (c + 1) * LANES] for c in range(columns)], axis=0)
    pixels = (tiles * LANES + cells).astype(jnp.float32)
    copies[5].wait()
    phases = jnp.concatenate([phase_ref[:, c * LANES : (c + 1) * LANES] for c in range(columns)], axis=0)
    moved = exact_dot(place, jnp.concatenate([phases, pixels], axis=1))
    slot_phase, slot_pixel = moved[:, :LANES], moved[:, LANES:]
    for o in range(ranks):
        out_ref[o * rows : o * rows + cap, :] = slot_phase[o * cap : (o + 1) * cap, :]
        out_ref[o * rows + cap : o * rows + 2 * cap, :] = slot_pixel[o * cap : (o + 1) * cap, :]
        out_ref[o * rows + 2 * cap : (o + 1) * rows, :] = info[o : o + 1, :]


def unpack(ranks, cap, ref, phase_ref, cell_ref, info_ref, meta_ref):
    rows = 2 * cap + 1
    for o in range(ranks):
        here = o * cap
        phase_ref[here : here + cap, :] = ref[o * rows : o * rows + cap, :]
        cell_ref[here : here + cap, :] = ref[o * rows + cap : o * rows + 2 * cap, :]
        info = ref[o * rows + 2 * cap : (o + 1) * rows, :]
        info_ref[here : here + cap, :] = jnp.broadcast_to(info, (cap, LANES))
        meta_ref[o : o + 1, :] = info


def rank_slots(ranks, cap, meta_ref):
    lists = []
    spans = LANES // cap
    for k in range(ranks * cap // LANES):
        names = meta_ref[k * spans : (k + 1) * spans, :]
        lane = iota((spans, LANES), 1)
        spread = lane_gather(names, 2 * cap + (lane & (cap - 1)))
        mine = (lane >> log2(cap)) == iota((spans, LANES), 0)
        lists.append(jnp.sum(jnp.where(mine, spread, 0.0), axis=0, keepdims=True))
    names = jnp.concatenate(lists, axis=0).astype(jnp.int32)
    mine = (names > 0) & (((names - 1) & 1) == lax.axis_index("det"))
    ones = jnp.where(mine, 1.0, 0.0)
    earlier = (iota((LANES, LANES), 0) < iota((LANES, LANES), 1)).astype(jnp.bfloat16)
    rank = dot(ones.astype(jnp.bfloat16), earlier)
    sums = jnp.sum(ones, axis=1, keepdims=True)
    before = [jnp.zeros((1, 1), jnp.float32)]
    for k in range(len(lists)):
        before.append(before[-1] + sums[k : k + 1, :])
    rank = rank + jnp.concatenate(before[:-1], axis=0)
    return jnp.where(mine, rank, -1.0).astype(jnp.int32), jnp.sum(ones).astype(jnp.int32)


def flatten(pages, knots):
    dets = pages[0].shape[0]
    if knots >= LANES:
        return [page[d : d + 1, :] for d in range(dets) for page in pages]
    lane, det = iota((dets, LANES), 1), iota((dets, LANES), 0)
    spread = lane_gather(pages[0], lane & (knots - 1))
    per_row = LANES // knots
    mine = (det & (per_row - 1)) == (lane >> log2(knots))
    spread = jnp.where(mine, spread, 0.0)
    rows = []
    for first in range(0, dets, per_row):
        rows.append(jnp.sum(spread[first : first + per_row, :], axis=0, keepdims=True))
    return rows


def read_knots(ranks, cap, dets, nodes, meta_ref):
    width = dets * nodes
    knots = ranks * nodes
    per_row = LANES // width
    kinds = []
    for kind in range(2):
        lines = []
        for p in range(ranks // per_row):
            names = meta_ref[p * per_row : (p + 1) * per_row, :]
            lane = iota((per_row, LANES), 1)
            spread = lane_gather(names, (3 * cap + kind * width) + (lane & (width - 1)))
            here = (lane >> log2(width)) == iota((per_row, LANES), 0)
            lines.append(jnp.sum(jnp.where(here, spread, 0.0), axis=0, keepdims=True))
        lane = iota((dets, LANES), 1)
        tables = []
        for page in range(max(1, knots // LANES)):
            knot = lane + page * LANES
            index = ((knot >> log2(nodes)) & (per_row - 1)) * width
            index = index + iota((dets, LANES), 0) * nodes + (knot & (nodes - 1))
            table = jnp.zeros((dets, LANES), jnp.float32)
            for p, line in enumerate(lines):
                values = lane_gather(jnp.broadcast_to(line, (dets, LANES)), index)
                table = jnp.where((knot >> log2(per_row * nodes)) == p, values, table)
            tables.append(table)
        kinds.append(tables)
    return kinds


def source_of(ranks, cap, dets, total, side, phase_ref, cell_ref, info_ref):
    slots = ranks * cap
    slot = iota((slots, LANES), 0) & (cap - 1)
    lane = iota((slots, LANES), 1)
    listed = lane_gather(info_ref[...], jnp.minimum(lane, 2) * cap + slot)
    listed = listed + jnp.where(lane == 1, (side * dets).astype(jnp.float32), 0.0)
    pixel = cell_ref[...]
    cell = (pixel - jnp.floor(pixel * (1.0 / LANES)) * LANES).astype(jnp.bfloat16)
    whole = split3(listed)
    if max(total, ranks * OWNER_TILES) <= 65536:
        whole = whole[:2]
    return jnp.concatenate(split3(phase_ref[...]) + (cell,) + whole, axis=1)


def take_slots(at, rank, source, dets, side, tables):
    down = iota((BLOCK, LANES), 0) + at
    place = jnp.concatenate(
        [(down == rank[k : k + 1, :]).astype(jnp.bfloat16) for k in range(rank.shape[0])], axis=1
    )
    taken = dot(place, source)
    parts = [taken[:, k * LANES : (k + 1) * LANES] for k in range(taken.shape[1] // LANES)]
    phase = (parts[0] + parts[1]) + parts[2]
    info = sum(parts[5:], parts[4])
    lane = iota((BLOCK, LANES), 1) + (1 + side * dets)
    chosen = ((info[:, 1:2] == lane.astype(jnp.float32)) & (iota((BLOCK, LANES), 1) < dets)).astype(jnp.bfloat16)
    empty = jnp.zeros((LANES - dets, LANES), jnp.float32)
    knots = [exact_dot(chosen, jnp.concatenate([table, empty], axis=0)) for table in tables]
    return phase, parts[3], info, knots


def spline(info_ref, spacing, at, chunk):
    start = jnp.broadcast_to(info_ref[pl.ds(at, chunk), 0:1], (chunk, LANES)).astype(jnp.int32)
    time = start + iota((chunk, LANES), 1)
    interval = time >> log2(spacing)
    fraction = (time & (spacing - 1)).astype(jnp.float32) * (1.0 / spacing)
    return start >> log2(spacing), interval, spline_weights(fraction)


def five_weights(early, weights):
    padded = (0.0,) + weights + (0.0,)
    return [jnp.where(early, padded[term + 1], padded[term]) for term in range(5)]


def bin_chunks(first, last, knots, spacing, few_phase, few_cell, few_info, table_ref, cos_ref, sin_ref, stream_ref, basis_ref, bin_ref):
    pages = table_ref.shape[0]

    def prepare(step):
        at = pl.multiple_of(step * COLLECT, COLLECT)
        cosine, sine = cos_sin(2.0 * few_phase[pl.ds(at, COLLECT), :])
        base, interval, weights = spline(few_info, spacing, at, COLLECT)
        for term, weight in enumerate(five_weights(interval == base, weights)):
            basis_ref[term, pl.ds(at, COLLECT), :] = weight
        stream = jnp.zeros((COLLECT, LANES), jnp.float32)
        for term in range(4):
            knot = (interval + (term - 1)) & (knots - 1)
            value = lane_gather(table_ref[0, pl.ds(at, COLLECT), :], knot & (LANES - 1))
            for page in range(1, pages):
                more = lane_gather(table_ref[page, pl.ds(at, COLLECT), :], knot & (LANES - 1))
                value = jnp.where((knot >> log2(LANES)) == page, more, value)
            stream = stream + weights[term] * value
        cos_ref[pl.ds(at, COLLECT), :] = cosine
        sin_ref[pl.ds(at, COLLECT), :] = sine
        stream_ref[pl.ds(at, COLLECT), :] = stream

    down = iota((LANES, 2 * LANES), 0).astype(jnp.float32).astype(jnp.bfloat16)
    channel = iota((CHANNELS, LANES), 0)
    zeros = jnp.zeros((2 * CHANNELS, LANES), jnp.bfloat16)

    def collect(step, carry):
        for k in range(COLLECT // 2):
            at = step * COLLECT + 2 * k
            pieces, cells = [], []
            for slot in (at, at + 1):
                stream = jnp.broadcast_to(stream_ref[pl.ds(slot, 1), :], (CHANNELS, LANES))
                cosine = jnp.broadcast_to(cos_ref[pl.ds(slot, 1), :], (CHANNELS, LANES))
                sine = jnp.broadcast_to(sin_ref[pl.ds(slot, 1), :], (CHANNELS, LANES))
                left = jnp.where(channel < 3, stream, jnp.where(channel < 6, 1.0, cosine))
                is_one = (channel == 0) | (channel == 3)
                is_sine = (channel == 2) | (channel == 5) | (channel == 7)
                right = jnp.where(is_one, 1.0, jnp.where(is_sine, sine, cosine))
                entry = left * right
                high = entry.astype(jnp.bfloat16).astype(jnp.float32)
                rest = entry - high
                stack = jnp.concatenate([high, rest], axis=0)
                pieces.append(stack.astype(jnp.bfloat16))
                cells.append(jnp.broadcast_to(few_cell[pl.ds(slot, 1), :].astype(jnp.bfloat16), (LANES, LANES)))
            entry = jnp.concatenate(
                [
                    jnp.concatenate([pieces[0], zeros], axis=1),
                    jnp.concatenate([zeros, pieces[1]], axis=1),
                ],
                axis=0,
            )
            hits = jnp.where(jnp.concatenate(cells, axis=1) == down, jnp.bfloat16(1), jnp.bfloat16(0))
            sums = lax.dot_general(
                entry, hits, (((1,), (1,)), ((), ())), preferred_element_type=jnp.float32
            )
            for m in range(2):
                base = 2 * CHANNELS * m
                bin_ref[pl.ds((at + m) * CHANNELS, CHANNELS), :] = (
                    sums[base : base + CHANNELS] + sums[base + CHANNELS : base + 2 * CHANNELS]
                )
        prepare(step + 1)
        return carry

    prepare(first)
    lax.fori_loop(first, last, collect, 0)


def own_kernel(
    ranks, cap, dets, nodes, spacing, own_ref,
    few_phase, few_cell, few_info, table_ref, cos_ref, sin_ref, stream_ref, basis_ref, bin_ref, packs_ref, count_ref,
    phase_ref, cell_ref, info_ref, meta_ref,
):
    knots = ranks * nodes
    side = lax.axis_index("det")
    unpack(ranks, cap, own_ref, phase_ref, cell_ref, info_ref, meta_ref)
    rank, number = rank_slots(ranks, cap, meta_ref)
    count_ref[...] = jnp.full((8, LANES), number, jnp.int32)
    tables, left = read_knots(ranks, cap, dets, nodes, meta_ref)
    packs_ref[...] = jnp.concatenate(flatten(tables, knots) + flatten(left, knots), axis=0)
    source = source_of(ranks, cap, dets, knots * spacing, side, phase_ref, cell_ref, info_ref)

    def gather_block(block, carry):
        here = pl.ds(aligned(block * BLOCK, 32), BLOCK)
        few_phase[here, :], few_cell[here, :], few_info[here, :], found = take_slots(
            block * BLOCK, rank, source, dets, side, tables
        )
        for page, rows in enumerate(found):
            table_ref[page, here, :] = rows
        return carry

    gather_block(0, 0)
    lax.fori_loop(1, block_count(number, ranks * cap), gather_block, 0)
    bin_chunks(
        0, number >> log2(COLLECT), knots, spacing, few_phase, few_cell, few_info, table_ref,
        cos_ref, sin_ref, stream_ref, basis_ref, bin_ref,
    )


def block_count(number, most):
    return sum(jnp.where(number > start, 1, 0) for start in range(0, most, BLOCK))


def main_kernel(
    ranks, cap, dets, nodes, spacing, other_ref, coeffs_hbm, packs_own, count_ref, *refs,
):
    few_phase, few_cell, few_info, table_ref, cos_ref, sin_ref, stream_ref, basis_ref, bin_ref = refs[9:18]
    out_ref, packs_ref, coeffs_ref = refs[18:21]
    phase_ref, cell_ref, info_ref, meta_ref, total_ref, turned_ref, knots_ref, sems = refs[21:]
    coeffs_copy = pltpu.make_async_copy(coeffs_hbm, coeffs_ref, sems.at[0])
    coeffs_copy.start()
    slots = ranks * cap
    knots = ranks * nodes
    packed = knots * dets // LANES
    group = lax.axis_index("det")
    side = 1 - group

    unpack(ranks, cap, other_ref, phase_ref, cell_ref, info_ref, meta_ref)
    rank, more = rank_slots(ranks, cap, meta_ref)
    ready = jnp.max(count_ref[...])
    rank = jnp.where(rank >= 0, rank + ready, -1)
    number = ready + more
    tables, left = read_knots(ranks, cap, dets, nodes, meta_ref)
    for kind, pages in enumerate((tables, left)):
        here = slice(kind * packed, (kind + 1) * packed)
        packs_ref[kind, pl.ds(group * packed, packed), :] = packs_own[here, :]
        packs_ref[kind, pl.ds(side * packed, packed), :] = jnp.concatenate(flatten(pages, knots), axis=0)
    source = source_of(ranks, cap, dets, knots * spacing, side, phase_ref, cell_ref, info_ref)
    blocks = block_count(number, 2 * slots)
    ready_blocks = block_count(ready, slots)

    def gather_block(block, carry):
        here = pl.ds(aligned(block * BLOCK, 32), BLOCK)
        def before(rows):
            return rows if isinstance(block, int) else jnp.where(block < ready_blocks, rows, 0.0)

        phase, cell, info, found = take_slots(block * BLOCK, rank, source, dets, side, tables)
        few_phase[here, :] = before(few_phase[here, :]) + phase
        few_cell[here, :] = before(few_cell[here, :]) + cell
        info = before(few_info[here, :]) + info
        few_info[here, :] = info
        turned = info.T
        turned_ref[0, pl.ds(block, 1), :] = turned[1:2, :]
        turned_ref[1, pl.ds(block, 1), :] = turned[2:3, :]
        for page, rows in enumerate(found):
            table_ref[page, here, :] = before(table_ref[page, here, :]) + rows
        return carry

    gather_block(0, 0)
    lax.fori_loop(1, blocks, gather_block, 0)

    def steps(chunk):
        return (number + (chunk - 1)) >> log2(chunk)

    bin_chunks(
        ready >> log2(COLLECT), steps(COLLECT), knots, spacing, few_phase, few_cell, few_info, table_ref,
        cos_ref, sin_ref, stream_ref, basis_ref, bin_ref,
    )

    def clear(step, carry):
        at = pl.multiple_of(step * COLLECT * CHANNELS, COLLECT * CHANNELS)
        bin_ref[pl.ds(at, COLLECT * CHANNELS), :] = jnp.zeros((COLLECT * CHANNELS, LANES), jnp.float32)
        return carry

    lax.fori_loop(steps(COLLECT), jnp.maximum(blocks, 1) * (BLOCK // COLLECT), clear, 0)

    def merge(block, carry):
        at = aligned(block * BLOCK, 32)
        names = few_info[pl.ds(at, BLOCK), 2:3]

        def add(other, carry):
            there = aligned(other * BLOCK, 32)
            same = (names == turned_ref[1, pl.ds(other, 1), :]).astype(jnp.bfloat16)
            for c in range(CHANNELS):
                binned = bin_ref[pl.ds(there * CHANNELS + c, BLOCK, stride=CHANNELS), :]
                high = binned.astype(jnp.bfloat16)
                share = dot(same, high)
                if c != COUNT:
                    share = share + dot(same, (binned - high.astype(jnp.float32)).astype(jnp.bfloat16))
                if not isinstance(other, int):
                    share = share + total_ref[c, pl.ds(at, BLOCK), :]
                total_ref[c, pl.ds(at, BLOCK), :] = share
            return carry

        add(0, 0)
        lax.fori_loop(1, blocks, add, 0)
        return carry

    merge(0, 0)
    lax.fori_loop(1, blocks, merge, 0)

    def project(at):
        here = pl.ds(aligned(at, 16), PROJECT)
        signal, signal_cos, signal_sin, count, cos_sum, sin_sum, cos_cos, cos_sin_sum = (
            total_ref[c, here, :] for c in range(CHANNELS)
        )
        sin_sin = count - cos_cos
        stokes_i = count + MAP_PRIOR
        stokes_q = cos_cos + MAP_PRIOR
        stokes_u = sin_sin + MAP_PRIOR
        minor_one = stokes_q * stokes_u - cos_sin_sum * cos_sin_sum
        minor_two = sin_sum * cos_sin_sum - cos_sum * stokes_u
        minor_three = cos_sum * cos_sin_sum - sin_sum * stokes_q
        minor_four = stokes_i * stokes_u - sin_sum * sin_sum
        minor_five = cos_sum * sin_sum - stokes_i * cos_sin_sum
        minor_six = stokes_i * stokes_q - cos_sum * cos_sum
        determinant = stokes_i * minor_one + cos_sum * minor_two + sin_sum * minor_three
        scale = 1.0 / determinant
        map_i = (minor_one * signal + minor_two * signal_cos + minor_three * signal_sin) * scale
        map_q = (minor_two * signal + minor_four * signal_cos + minor_five * signal_sin) * scale
        map_u = (minor_three * signal + minor_five * signal_cos + minor_six * signal_sin) * scale
        cell = few_cell[here, :].astype(jnp.int32)
        projected = (
            lane_gather(map_i, cell) + cos_ref[here, :] * lane_gather(map_q, cell)
        ) + sin_ref[here, :] * lane_gather(map_u, cell)
        cleaned = stream_ref[here, :] - projected
        valid = few_info[here, 1:2] > 0.5
        base = few_info[here, 0:1].astype(jnp.int32) >> log2(spacing)
        lane = iota((PROJECT, LANES), 1)
        pages = [jnp.zeros((PROJECT, LANES), jnp.float32) for _ in range(knots_ref.shape[0])]
        for term in range(5):
            value = basis_ref[term, here, :] * cleaned
            high = value.astype(jnp.bfloat16)
            low = (value - high.astype(jnp.float32)).astype(jnp.bfloat16)
            value = dot(jnp.concatenate([high, low], axis=1), jnp.ones((2 * LANES, LANES), jnp.bfloat16))
            knot = (base + (term - 1)) & (knots - 1)
            for page in range(len(pages)):
                pages[page] = pages[page] + jnp.where(lane + page * LANES == knot, value, 0.0)
        for page, sums in enumerate(pages):
            knots_ref[page, here, :] = jnp.where(valid, sums, 0.0)

    def image_of(block, sums):
        at = aligned(block * BLOCK, 32)
        for first in range(0, BLOCK, PROJECT):
            project(at + first)
        det = (iota((2 * dets, BLOCK), 0) + 1).astype(jnp.float32)
        chosen = (turned_ref[0, pl.ds(block, 1), :] == det).astype(jnp.bfloat16)
        return tuple(
            total + exact_dot(chosen, knots_ref[page, pl.ds(at, BLOCK), :]) for page, total in enumerate(sums)
        )

    image = tuple(jnp.zeros((2 * dets, LANES), jnp.float32) for _ in range(knots_ref.shape[0]))
    image = lax.fori_loop(1, blocks, image_of, image_of(0, image))
    partial = jnp.concatenate(flatten(image, knots), axis=0)
    for target in range(out_ref.shape[0] // (2 * packed)):
        out_ref[target * 2 * packed : (target + 1) * 2 * packed, :] = partial
    coeffs_copy.wait()


def finish_kernel(
    ranks, spacing, arrived_ref, packs_ref, coeffs_ref, new_offset_ref, new_left_ref, new_search_ref,
):
    nodes, dets = coeffs_ref.shape
    height = packs_ref.shape[1]
    total = arrived_ref[0:height, :]
    for o in range(1, arrived_ref.shape[0] // height):
        total = total + arrived_ref[o * height : (o + 1) * height, :]
    search, left = packs_ref[0], packs_ref[1]
    image = total * (1.0 / spacing) + BASE_PRIOR * search
    norm_old = jnp.sum(left * left, keepdims=True)
    stride_factor = norm_old / jnp.sum(search * image, keepdims=True)
    fresh = left - stride_factor * image
    beta = jnp.sum(fresh * fresh, keepdims=True) / norm_old
    span, group = lax.axis_index("tm"), lax.axis_index("det")
    lines = height // 2
    knots = lines * LANES // dets
    place = (iota((8, LANES), 1) & (dets - 1)) * knots + span * nodes + (iota((8, LANES), 0) & (nodes - 1))

    def own(x):
        x = jnp.where(group == 0, x[:lines, :], x[lines:, :])
        found = jnp.zeros((8, LANES), jnp.float32)
        for p in range(lines):
            values = lane_gather(jnp.broadcast_to(x[p : p + 1, :], (8, LANES)), place & (LANES - 1))
            found = jnp.where((place >> log2(LANES)) == p, values, found)
        return found[:nodes, :dets]

    my_search = own(search)
    my_left = own(fresh)
    new_offset_ref[...] = coeffs_ref[...] + stride_factor * my_search
    new_left_ref[...] = my_left
    new_search_ref[...] = my_left + beta * my_search


def body(
    offset_coeffs,
    leftover_error,
    search_vector,
    node_lattice_offset,
    sky_cell_in_patch,
    analyser_reading_phase,
    segment_sky_patch,
):
    ranks, groups = lax.axis_size("tm"), lax.axis_size("det")
    dets, samples = analyser_reading_phase.shape
    nodes = search_vector.shape[1]
    spacing = samples // nodes
    blocks = segment_sky_patch.size
    cap = max(2, 2 * blocks // ranks)
    slots = ranks * cap
    rows = 2 * cap + 1
    height = groups * ranks * nodes * dets // LANES
    vmem = pl.BlockSpec(memory_space=pltpu.VMEM)
    hbm = pl.BlockSpec(memory_space=pltpu.HBM)
    pin = functools.partial(pltpu.with_memory_space_constraint, memory_space=pltpu.HBM)
    params = pltpu.CompilerParams(vmem_limit_bytes=VMEM_BYTES)
    inputs = (
        segment_sky_patch, node_lattice_offset.reshape(1, dets), search_vector.T, leftover_error.T,
        sky_cell_in_patch, analyser_reading_phase,
    )
    small = jax.ShapeDtypeStruct((nodes, dets), jnp.float32)

    outgoing = pl.pallas_call(
        functools.partial(send_kernel, ranks, cap),
        out_shape=jax.ShapeDtypeStruct((ranks * rows, LANES), jnp.float32),
        in_specs=[hbm] * len(inputs),
        out_specs=vmem,
        scratch_shapes=[pltpu.VMEM(x.shape, x.dtype) for x in inputs]
        + [pltpu.SemaphoreType.DMA((len(inputs),))],
        compiler_params=params,
        name="send",
    )(*[pin(x) for x in inputs])
    arrived = lax.all_to_all(
        outgoing.reshape(ranks, 1, rows * LANES), "tm", split_axis=0, concat_axis=0, tiled=True
    )
    swap = [(i, groups - 1 - i) for i in range(groups)]
    other = lax.ppermute(arrived, "det", swap)
    pages = max(1, ranks * nodes // LANES)
    f32 = jnp.float32
    room = pl.cdiv(2 * slots, BLOCK) * BLOCK + max(COLLECT, PROJECT)
    few = jax.ShapeDtypeStruct((room, LANES), f32)
    shared = (
        few, few, few, jax.ShapeDtypeStruct((pages, room, LANES), f32), few, few, few,
        jax.ShapeDtypeStruct((5, room, LANES), f32),
        jax.ShapeDtypeStruct((room * CHANNELS, LANES), f32),
    )
    arrival = [pltpu.VMEM((slots, LANES), f32)] * 3 + [pltpu.VMEM((ranks, LANES), f32)]
    sizes = (ranks, cap, dets, nodes, spacing)
    *state, packs, count = pl.pallas_call(
        functools.partial(own_kernel, *sizes),
        out_shape=shared + (
            jax.ShapeDtypeStruct((2 * height // groups, LANES), f32),
            jax.ShapeDtypeStruct((8, LANES), jnp.int32),
        ),
        in_specs=[vmem],
        out_specs=(vmem,) * 11,
        scratch_shapes=arrival,
        compiler_params=params,
        cost_estimate=pl.CostEstimate(flops=4_000_000_000, bytes_accessed=4_000_000, transcendentals=0),
        name="own",
    )(arrived.reshape(ranks * rows, LANES))
    *_, partials, packs, coeffs = pl.pallas_call(
        functools.partial(main_kernel, *sizes),
        out_shape=shared + (
            jax.ShapeDtypeStruct((ranks * groups * height, LANES), f32),
            jax.ShapeDtypeStruct((2, height, LANES), f32),
            small,
        ),
        in_specs=[vmem, hbm] + [vmem] * 11,
        out_specs=(vmem,) * 12,
        scratch_shapes=arrival + [
            pltpu.VMEM((CHANNELS, room, LANES), f32),
            pltpu.VMEM((2, 8, BLOCK), f32),
            pltpu.VMEM((pages, room, LANES), f32),
            pltpu.SemaphoreType.DMA((1,)),
        ],
        input_output_aliases={4 + k: k for k in range(9)},
        compiler_params=params,
        name="main",
    )(other.reshape(ranks * rows, LANES), pin(offset_coeffs.T), packs, count, *state)
    gathered = lax.all_to_all(
        partials.reshape(ranks * groups, 1, height * LANES),
        ("tm", "det"), split_axis=0, concat_axis=0, tiled=True,
    )
    results = pl.pallas_call(
        functools.partial(finish_kernel, ranks, spacing),
        out_shape=(small, small, small),
        in_specs=[vmem] * 3,
        out_specs=(vmem, vmem, vmem),
        compiler_params=params,
        name="finish",
    )(gathered.reshape(ranks * groups * height, LANES), packs, coeffs)
    return tuple(result.T for result in results)


def solution(mesh):
    return jax.shard_map(
        body,
        mesh=mesh,
        in_specs=(
            P("det", "tm"),
            P("det", "tm"),
            P("det", "tm"),
            P("det"),
            P("det", "tm"),
            P("det", "tm"),
            P("det", "tm"),
        ),
        out_specs=(P("det", "tm"), P("det", "tm"), P("det", "tm")),
        check_vma=False,
    )
```

```python
import functools

import jax
import jax.numpy as jnp
from jax import lax
from jax.experimental import pallas as pl
from jax.experimental.pallas import tpu as pltpu
from jax.sharding import PartitionSpec as P

PIX_OWN = 131072
MAP_PRIOR = 1.0
BASE_PRIOR = 0.1
LANES = 128
OWNER_TILES = PIX_OWN // LANES
CHANNELS = 8
COUNT = 3
BLOCK = 176
COLLECT = 32
PROJECT = 64
VMEM_BYTES = 32 * 1024 * 1024

SIN_TERMS = (1.0, -1.0 / 6, 1.0 / 120, -1.0 / 5040, 1.0 / 362880, -1.0 / 39916800, 1.0 / 6227020800)
COS_TERMS = (1.0, -0.5, 1.0 / 24, -1.0 / 720, 1.0 / 40320, -1.0 / 3628800, 1.0 / 479001600, -1.0 / 87178291200)
PI_PARTS = (3.140625, 0.0009670257568359375, 6.2771141529083252e-07)


def iota(shape, dim):
    return lax.broadcasted_iota(jnp.int32, shape, dim)


def log2(number):
    assert number & (number - 1) == 0
    return number.bit_length() - 1


def split3(x):
    high = x.astype(jnp.bfloat16)
    rest = x - high.astype(jnp.float32)
    middle = rest.astype(jnp.bfloat16)
    low = (rest - middle.astype(jnp.float32)).astype(jnp.bfloat16)
    return high, middle, low


def dot(a, b):
    return jnp.dot(a, b, preferred_element_type=jnp.float32)


def exact_dot(selector, x):
    high, middle, low = split3(x)
    return (dot(selector, high) + dot(selector, middle)) + dot(selector, low)


def horner(x, terms):
    total = jnp.full_like(x, terms[-1])
    for term in terms[-2::-1]:
        total = total * x + term
    return total


def cos_sin(angle):
    turns = jnp.round(angle * (1.0 / 3.14159265358979))
    rest = angle - turns * PI_PARTS[0]
    rest = rest - turns * PI_PARTS[1]
    rest = rest - turns * PI_PARTS[2]
    half = turns * 0.5
    sign = 1.0 - 4.0 * (half - jnp.floor(half))
    square = rest * rest
    cosine = sign * horner(square, COS_TERMS)
    sine = sign * rest * horner(square, SIN_TERMS)
    return cosine, sine


def spline_weights(fraction):
    square = fraction * fraction
    cube = square * fraction
    rest = 1.0 - fraction
    first = rest * rest * rest * (1.0 / 6.0)
    second = (3.0 * cube - 6.0 * square + 4.0) * (1.0 / 6.0)
    third = (-3.0 * cube + 3.0 * square + 3.0 * fraction + 1.0) * (1.0 / 6.0)
    fourth = cube * (1.0 / 6.0)
    return (first, second, third, fourth)


def aligned(index, unit):
    return index if isinstance(index, int) else pl.multiple_of(index, unit)


def lane_gather(table, index):
    return jnp.take_along_axis(table, index, axis=1, mode="promise_in_bounds")


def send_kernel(
    ranks, cap, patch_hbm, offset_hbm, search_hbm, left_hbm, cell_hbm, phase_hbm, out_ref,
    patch_ref, offset_ref, search_ref, left_ref, cell_ref, phase_ref, sems,
):
    pairs = (
        (patch_hbm, patch_ref), (offset_hbm, offset_ref), (search_hbm, search_ref),
        (left_hbm, left_ref), (cell_hbm, cell_ref), (phase_hbm, phase_ref),
    )
    copies = [pltpu.make_async_copy(src, dst, sems.at[k]) for k, (src, dst) in enumerate(pairs)]
    for copy in copies:
        copy.start()
    copies[0].wait()
    dets, columns = patch_ref.shape
    blocks = dets * columns
    samples = phase_ref.shape[1]
    nodes = search_ref.shape[0]
    span = lax.axis_index("tm")
    rows = 2 * cap + 1
    square = (blocks, blocks)
    tiles = jnp.concatenate(
        [jnp.broadcast_to(patch_ref[:, c : c + 1], (dets, LANES)) for c in range(columns)], axis=0
    )
    owner = (tiles >> log2(OWNER_TILES)).astype(jnp.float32)
    owner_t = owner.T
    same = owner == owner_t
    here, there = iota(square, 0), iota(square, 1)
    rank_row = jnp.sum(jnp.where(same & (here < there), 1.0, 0.0), axis=0, keepdims=True)
    rank_col = jnp.sum(jnp.where(same & (there < here), 1.0, 0.0), axis=1, keepdims=True)
    slot_row = (owner_t[0:1, :] * cap + rank_row).astype(jnp.int32)
    place = (iota((ranks * cap, blocks), 0) == slot_row).astype(jnp.bfloat16)
    lane = iota(square, 1)
    small = iota((dets, LANES), 1)
    det_lane = iota((dets, LANES), 0)
    for copy in copies[1:4]:
        copy.wait()
    offsets = jnp.broadcast_to(offset_ref[...], (dets, dets))
    diagonal = iota((dets, dets), 0) == iota((dets, dets), 1)
    shift = jnp.sum(jnp.where(diagonal, offsets, 0).astype(jnp.float32), axis=1, keepdims=True)
    shift = jnp.broadcast_to(shift.astype(jnp.int32), (dets, LANES))
    start = jnp.concatenate([c * LANES - shift for c in range(columns)], axis=0) + span * samples
    which = (iota(square, 0) & (dets - 1)) + 1
    rank = rank_col.astype(jnp.int32)
    listing = jnp.where(lane == rank, start, 0) + jnp.where(lane == rank + cap, which, 0)
    listing = listing + jnp.where(lane == rank + 2 * cap, tiles + 1, 0)
    chosen = (iota((ranks, blocks), 0).astype(jnp.float32) == owner_t[0:1, :]).astype(jnp.bfloat16)
    info = exact_dot(chosen, listing.astype(jnp.float32))
    knots = jnp.zeros((1, LANES), jnp.float32)
    for kind, ref in enumerate((search_ref, left_ref)):
        for n in range(nodes):
            column = jnp.broadcast_to(ref[n : n + 1, :], (dets, dets))
            column = jnp.sum(jnp.where(diagonal, column, 0.0), axis=1, keepdims=True)
            at = (3 * cap + kind * dets * nodes + n) + det_lane * nodes
            knots = knots + jnp.sum(jnp.where(small == at, column, 0.0), axis=0, keepdims=True)
    info = info + knots
    copies[4].wait()
    cells = jnp.concatenate([cell_ref[:, c * LANES : (c + 1) * LANES] for c in range(columns)], axis=0)
    pixels = (tiles * LANES + cells).astype(jnp.float32)
    copies[5].wait()
    phases = jnp.concatenate([phase_ref[:, c * LANES : (c + 1) * LANES] for c in range(columns)], axis=0)
    moved = exact_dot(place, jnp.concatenate([phases, pixels], axis=1))
    slot_phase, slot_pixel = moved[:, :LANES], moved[:, LANES:]
    for o in range(ranks):
        out_ref[o * rows : o * rows + cap, :] = slot_phase[o * cap : (o + 1) * cap, :]
        out_ref[o * rows + cap : o * rows + 2 * cap, :] = slot_pixel[o * cap : (o + 1) * cap, :]
        out_ref[o * rows + 2 * cap : (o + 1) * rows, :] = info[o : o + 1, :]


def unpack(ranks, cap, ref, phase_ref, cell_ref, info_ref, meta_ref):
    rows = 2 * cap + 1
    for o in range(ranks):
        here = o * cap
        phase_ref[here : here + cap, :] = ref[o * rows : o * rows + cap, :]
        cell_ref[here : here + cap, :] = ref[o * rows + cap : o * rows + 2 * cap, :]
        info = ref[o * rows + 2 * cap : (o + 1) * rows, :]
        info_ref[here : here + cap, :] = jnp.broadcast_to(info, (cap, LANES))
        meta_ref[o : o + 1, :] = info


def rank_slots(ranks, cap, meta_ref):
    lists = []
    spans = LANES // cap
    for k in range(ranks * cap // LANES):
        names = meta_ref[k * spans : (k + 1) * spans, :]
        lane = iota((spans, LANES), 1)
        spread = lane_gather(names, 2 * cap + (lane & (cap - 1)))
        mine = (lane >> log2(cap)) == iota((spans, LANES), 0)
        lists.append(jnp.sum(jnp.where(mine, spread, 0.0), axis=0, keepdims=True))
    names = jnp.concatenate(lists, axis=0).astype(jnp.int32)
    mine = (names > 0) & (((names - 1) & 1) == lax.axis_index("det"))
    ones = jnp.where(mine, 1.0, 0.0)
    earlier = (iota((LANES, LANES), 0) < iota((LANES, LANES), 1)).astype(jnp.bfloat16)
    rank = dot(ones.astype(jnp.bfloat16), earlier)
    sums = jnp.sum(ones, axis=1, keepdims=True)
    before = [jnp.zeros((1, 1), jnp.float32)]
    for k in range(len(lists)):
        before.append(before[-1] + sums[k : k + 1, :])
    rank = rank + jnp.concatenate(before[:-1], axis=0)
    return jnp.where(mine, rank, -1.0).astype(jnp.int32), jnp.sum(ones).astype(jnp.int32)


def flatten(pages, knots):
    dets = pages[0].shape[0]
    if knots >= LANES:
        return [page[d : d + 1, :] for d in range(dets) for page in pages]
    lane, det = iota((dets, LANES), 1), iota((dets, LANES), 0)
    spread = lane_gather(pages[0], lane & (knots - 1))
    per_row = LANES // knots
    mine = (det & (per_row - 1)) == (lane >> log2(knots))
    spread = jnp.where(mine, spread, 0.0)
    rows = []
    for first in range(0, dets, per_row):
        rows.append(jnp.sum(spread[first : first + per_row, :], axis=0, keepdims=True))
    return rows


def read_knots(ranks, cap, dets, nodes, meta_ref):
    width = dets * nodes
    knots = ranks * nodes
    per_row = LANES // width
    kinds = []
    for kind in range(2):
        lines = []
        for p in range(ranks // per_row):
            names = meta_ref[p * per_row : (p + 1) * per_row, :]
            lane = iota((per_row, LANES), 1)
            spread = lane_gather(names, (3 * cap + kind * width) + (lane & (width - 1)))
            here = (lane >> log2(width)) == iota((per_row, LANES), 0)
            lines.append(jnp.sum(jnp.where(here, spread, 0.0), axis=0, keepdims=True))
        lane = iota((dets, LANES), 1)
        tables = []
        for page in range(max(1, knots // LANES)):
            knot = lane + page * LANES
            index = ((knot >> log2(nodes)) & (per_row - 1)) * width
            index = index + iota((dets, LANES), 0) * nodes + (knot & (nodes - 1))
            table = jnp.zeros((dets, LANES), jnp.float32)
            for p, line in enumerate(lines):
                values = lane_gather(jnp.broadcast_to(line, (dets, LANES)), index)
                table = jnp.where((knot >> log2(per_row * nodes)) == p, values, table)
            tables.append(table)
        kinds.append(tables)
    return kinds


def source_of(ranks, cap, dets, total, side, phase_ref, cell_ref, info_ref):
    slots = ranks * cap
    slot = iota((slots, LANES), 0) & (cap - 1)
    lane = iota((slots, LANES), 1)
    listed = lane_gather(info_ref[...], jnp.minimum(lane, 2) * cap + slot)
    listed = listed + jnp.where(lane == 1, (side * dets).astype(jnp.float32), 0.0)
    pixel = cell_ref[...]
    cell = (pixel - jnp.floor(pixel * (1.0 / LANES)) * LANES).astype(jnp.bfloat16)
    whole = split3(listed)
    if max(total, ranks * OWNER_TILES) <= 65536:
        whole = whole[:2]
    return jnp.concatenate(split3(phase_ref[...]) + (cell,) + whole, axis=1)


def take_slots(at, rank, source, dets, side, tables):
    down = iota((BLOCK, LANES), 0) + at
    place = jnp.concatenate(
        [(down == rank[k : k + 1, :]).astype(jnp.bfloat16) for k in range(rank.shape[0])], axis=1
    )
    taken = dot(place, source)
    parts = [taken[:, k * LANES : (k + 1) * LANES] for k in range(taken.shape[1] // LANES)]
    phase = (parts[0] + parts[1]) + parts[2]
    info = sum(parts[5:], parts[4])
    lane = iota((BLOCK, LANES), 1) + (1 + side * dets)
    chosen = ((info[:, 1:2] == lane.astype(jnp.float32)) & (iota((BLOCK, LANES), 1) < dets)).astype(jnp.bfloat16)
    empty = jnp.zeros((LANES - dets, LANES), jnp.float32)
    knots = [exact_dot(chosen, jnp.concatenate([table, empty], axis=0)) for table in tables]
    return phase, parts[3], info, knots


def spline(info_ref, spacing, at, chunk):
    start = jnp.broadcast_to(info_ref[pl.ds(at, chunk), 0:1], (chunk, LANES)).astype(jnp.int32)
    time = start + iota((chunk, LANES), 1)
    interval = time >> log2(spacing)
    fraction = (time & (spacing - 1)).astype(jnp.float32) * (1.0 / spacing)
    return start >> log2(spacing), interval, spline_weights(fraction)


def five_weights(early, weights):
    padded = (0.0,) + weights + (0.0,)
    return [jnp.where(early, padded[term + 1], padded[term]) for term in range(5)]


def bin_chunks(first, last, knots, spacing, few_phase, few_cell, few_info, table_ref, cos_ref, sin_ref, stream_ref, basis_ref, bin_ref):
    pages = table_ref.shape[0]

    def prepare(step):
        at = aligned(step * COLLECT, COLLECT)
        cosine, sine = cos_sin(2.0 * few_phase[pl.ds(at, COLLECT), :])
        base, interval, weights = spline(few_info, spacing, at, COLLECT)
        for term, weight in enumerate(five_weights(interval == base, weights)):
            basis_ref[term, pl.ds(at, COLLECT), :] = weight
        stream = jnp.zeros((COLLECT, LANES), jnp.float32)
        for term in range(4):
            knot = (interval + (term - 1)) & (knots - 1)
            value = lane_gather(table_ref[0, pl.ds(at, COLLECT), :], knot & (LANES - 1))
            for page in range(1, pages):
                more = lane_gather(table_ref[page, pl.ds(at, COLLECT), :], knot & (LANES - 1))
                value = jnp.where((knot >> log2(LANES)) == page, more, value)
            stream = stream + weights[term] * value
        cos_ref[pl.ds(at, COLLECT), :] = cosine
        sin_ref[pl.ds(at, COLLECT), :] = sine
        stream_ref[pl.ds(at, COLLECT), :] = stream

    down = iota((LANES, 2 * LANES), 0).astype(jnp.float32).astype(jnp.bfloat16)
    channel = iota((CHANNELS, LANES), 0)
    zeros = jnp.zeros((2 * CHANNELS, LANES), jnp.bfloat16)

    def collect(step):
        for k in range(COLLECT // 2):
            at = step * COLLECT + 2 * k
            pieces, cells = [], []
            for slot in (at, at + 1):
                stream = jnp.broadcast_to(stream_ref[pl.ds(slot, 1), :], (CHANNELS, LANES))
                cosine = jnp.broadcast_to(cos_ref[pl.ds(slot, 1), :], (CHANNELS, LANES))
                sine = jnp.broadcast_to(sin_ref[pl.ds(slot, 1), :], (CHANNELS, LANES))
                left = jnp.where(channel < 3, stream, jnp.where(channel < 6, 1.0, cosine))
                is_one = (channel == 0) | (channel == 3)
                is_sine = (channel == 2) | (channel == 5) | (channel == 7)
                right = jnp.where(is_one, 1.0, jnp.where(is_sine, sine, cosine))
                entry = left * right
                high = entry.astype(jnp.bfloat16).astype(jnp.float32)
                rest = entry - high
                stack = jnp.concatenate([high, rest], axis=0)
                pieces.append(stack.astype(jnp.bfloat16))
                cells.append(jnp.broadcast_to(few_cell[pl.ds(slot, 1), :].astype(jnp.bfloat16), (LANES, LANES)))
            entry = jnp.concatenate(
                [
                    jnp.concatenate([pieces[0], zeros], axis=1),
                    jnp.concatenate([zeros, pieces[1]], axis=1),
                ],
                axis=0,
            )
            hits = jnp.where(jnp.concatenate(cells, axis=1) == down, jnp.int8(1), jnp.int8(0))
            sums = dot(entry, hits.T.astype(jnp.bfloat16))
            for m in range(2):
                base = 2 * CHANNELS * m
                bin_ref[pl.ds((at + m) * CHANNELS, CHANNELS), :] = (
                    sums[base : base + CHANNELS] + sums[base + CHANNELS : base + 2 * CHANNELS]
                )
    def both(step, carry):
        collect(step)
        prepare(step + 1)
        return carry


    prepare(first)
    lax.fori_loop(first, last, both, 0)


def own_kernel(
    ranks, cap, dets, nodes, spacing, own_ref,
    few_phase, few_cell, few_info, table_ref, cos_ref, sin_ref, stream_ref, basis_ref, bin_ref, packs_ref, count_ref,
    phase_ref, cell_ref, info_ref, meta_ref,
):
    knots = ranks * nodes
    side = lax.axis_index("det")
    unpack(ranks, cap, own_ref, phase_ref, cell_ref, info_ref, meta_ref)
    rank, number = rank_slots(ranks, cap, meta_ref)
    count_ref[...] = jnp.full((8, LANES), number, jnp.int32)
    tables, left = read_knots(ranks, cap, dets, nodes, meta_ref)
    packs_ref[...] = jnp.concatenate(flatten(tables, knots) + flatten(left, knots), axis=0)
    source = source_of(ranks, cap, dets, knots * spacing, side, phase_ref, cell_ref, info_ref)

    def gather_block(block, carry):
        here = pl.ds(aligned(block * BLOCK, 16), BLOCK)
        few_phase[here, :], few_cell[here, :], few_info[here, :], found = take_slots(
            block * BLOCK, rank, source, dets, side, tables
        )
        for page, rows in enumerate(found):
            table_ref[page, here, :] = rows
        return carry

    gather_block(0, 0)
    lax.fori_loop(1, block_count(number, ranks * cap), gather_block, 0)
    bin_chunks(
        0, number >> log2(COLLECT), knots, spacing, few_phase, few_cell, few_info, table_ref,
        cos_ref, sin_ref, stream_ref, basis_ref, bin_ref,
    )


def block_count(number, most):
    return sum(jnp.where(number > start, 1, 0) for start in range(0, most, BLOCK))


def main_kernel(
    ranks, cap, dets, nodes, spacing, other_ref, coeffs_hbm, packs_own, count_ref, *refs,
):
    few_phase, few_cell, few_info, table_ref, cos_ref, sin_ref, stream_ref, basis_ref, bin_ref = refs[9:18]
    out_ref, packs_ref, coeffs_ref = refs[18:21]
    phase_ref, cell_ref, info_ref, meta_ref, total_ref, turned_ref, knots_ref, sems = refs[21:]
    coeffs_copy = pltpu.make_async_copy(coeffs_hbm, coeffs_ref, sems.at[0])
    coeffs_copy.start()
    slots = ranks * cap
    knots = ranks * nodes
    packed = knots * dets // LANES
    group = lax.axis_index("det")
    side = 1 - group

    unpack(ranks, cap, other_ref, phase_ref, cell_ref, info_ref, meta_ref)
    rank, more = rank_slots(ranks, cap, meta_ref)
    ready = jnp.max(count_ref[...])
    rank = jnp.where(rank >= 0, rank + ready, -1)
    number = ready + more
    tables, left = read_knots(ranks, cap, dets, nodes, meta_ref)
    for kind, pages in enumerate((tables, left)):
        here = slice(kind * packed, (kind + 1) * packed)
        packs_ref[kind, pl.ds(group * packed, packed), :] = packs_own[here, :]
        packs_ref[kind, pl.ds(side * packed, packed), :] = jnp.concatenate(flatten(pages, knots), axis=0)
    source = source_of(ranks, cap, dets, knots * spacing, side, phase_ref, cell_ref, info_ref)
    blocks = block_count(number, 2 * slots)
    ready_blocks = block_count(ready, slots)

    def gather_block(block, carry):
        here = pl.ds(aligned(block * BLOCK, 16), BLOCK)
        def before(rows):
            return rows if isinstance(block, int) else jnp.where(block < ready_blocks, rows, 0.0)

        phase, cell, info, found = take_slots(block * BLOCK, rank, source, dets, side, tables)
        few_phase[here, :] = before(few_phase[here, :]) + phase
        few_cell[here, :] = before(few_cell[here, :]) + cell
        info = before(few_info[here, :]) + info
        few_info[here, :] = info
        turned = info.T
        turned_ref[0, pl.ds(block, 1), :] = turned[1:2, :]
        turned_ref[1, pl.ds(block, 1), :] = turned[2:3, :]
        for page, rows in enumerate(found):
            table_ref[page, here, :] = before(table_ref[page, here, :]) + rows
        return carry

    gather_block(0, 0)
    lax.fori_loop(1, blocks, gather_block, 0)

    def steps(chunk):
        return (number + (chunk - 1)) >> log2(chunk)

    bin_chunks(
        ready >> log2(COLLECT), steps(COLLECT), knots, spacing, few_phase, few_cell, few_info, table_ref,
        cos_ref, sin_ref, stream_ref, basis_ref, bin_ref,
    )

    def clear(step, carry):
        at = pl.multiple_of(step * COLLECT * CHANNELS, COLLECT * CHANNELS)
        bin_ref[pl.ds(at, COLLECT * CHANNELS), :] = jnp.zeros((COLLECT * CHANNELS, LANES), jnp.float32)
        return carry

    end = (jnp.maximum(blocks, 1) * BLOCK + (COLLECT - 1)) >> log2(COLLECT)
    lax.fori_loop(steps(COLLECT), end, clear, 0)

    def merge(block, carry):
        at = aligned(block * BLOCK, 16)
        names = few_info[pl.ds(at, BLOCK), 2:3]

        def add(other, carry):
            there = aligned(other * BLOCK, 16)
            same = (names == turned_ref[1, pl.ds(other, 1), :]).astype(jnp.bfloat16)
            for c in range(CHANNELS):
                binned = bin_ref[pl.ds(there * CHANNELS + c, BLOCK, stride=CHANNELS), :]
                high = binned.astype(jnp.bfloat16)
                share = dot(same, high)
                if c != COUNT:
                    share = share + dot(same, (binned - high.astype(jnp.float32)).astype(jnp.bfloat16))
                if not isinstance(other, int):
                    share = share + total_ref[c, pl.ds(at, BLOCK), :]
                total_ref[c, pl.ds(at, BLOCK), :] = share
            return carry

        add(0, 0)
        lax.fori_loop(1, blocks, add, 0)
        return carry

    merge(0, 0)
    lax.fori_loop(1, blocks, merge, 0)

    def project(at, size):
        here = pl.ds(aligned(at, 16), size)
        signal, signal_cos, signal_sin, count, cos_sum, sin_sum, cos_cos, cos_sin_sum = (
            total_ref[c, here, :] for c in range(CHANNELS)
        )
        sin_sin = count - cos_cos
        stokes_i = count + MAP_PRIOR
        stokes_q = cos_cos + MAP_PRIOR
        stokes_u = sin_sin + MAP_PRIOR
        minor_one = stokes_q * stokes_u - cos_sin_sum * cos_sin_sum
        minor_two = sin_sum * cos_sin_sum - cos_sum * stokes_u
        minor_three = cos_sum * cos_sin_sum - sin_sum * stokes_q
        minor_four = stokes_i * stokes_u - sin_sum * sin_sum
        minor_five = cos_sum * sin_sum - stokes_i * cos_sin_sum
        minor_six = stokes_i * stokes_q - cos_sum * cos_sum
        determinant = stokes_i * minor_one + cos_sum * minor_two + sin_sum * minor_three
        scale = 1.0 / determinant
        map_i = (minor_one * signal + minor_two * signal_cos + minor_three * signal_sin) * scale
        map_q = (minor_two * signal + minor_four * signal_cos + minor_five * signal_sin) * scale
        map_u = (minor_three * signal + minor_five * signal_cos + minor_six * signal_sin) * scale
        cell = few_cell[here, :].astype(jnp.int32)
        projected = (
            lane_gather(map_i, cell) + cos_ref[here, :] * lane_gather(map_q, cell)
        ) + sin_ref[here, :] * lane_gather(map_u, cell)
        cleaned = stream_ref[here, :] - projected
        valid = few_info[here, 1:2] > 0.5
        base = few_info[here, 0:1].astype(jnp.int32) >> log2(spacing)
        lane = iota((size, LANES), 1)
        pages = [jnp.zeros((size, LANES), jnp.float32) for _ in range(knots_ref.shape[0])]
        for term in range(5):
            value = basis_ref[term, here, :] * cleaned
            high = value.astype(jnp.bfloat16)
            low = (value - high.astype(jnp.float32)).astype(jnp.bfloat16)
            value = dot(jnp.concatenate([high, low], axis=1), jnp.ones((2 * LANES, LANES), jnp.bfloat16))
            knot = (base + (term - 1)) & (knots - 1)
            for page in range(len(pages)):
                pages[page] = pages[page] + jnp.where(lane + page * LANES == knot, value, 0.0)
        for page, sums in enumerate(pages):
            knots_ref[page, here, :] = jnp.where(valid, sums, 0.0)

    def image_of(block, sums):
        at = aligned(block * BLOCK, 16)
        for first in range(0, BLOCK, PROJECT):
            project(at + first, min(PROJECT, BLOCK - first))
        det = (iota((2 * dets, BLOCK), 0) + 1).astype(jnp.float32)
        chosen = (turned_ref[0, pl.ds(block, 1), :] == det).astype(jnp.bfloat16)
        return tuple(
            total + exact_dot(chosen, knots_ref[page, pl.ds(at, BLOCK), :]) for page, total in enumerate(sums)
        )

    image = tuple(jnp.zeros((2 * dets, LANES), jnp.float32) for _ in range(knots_ref.shape[0]))
    image = lax.fori_loop(1, blocks, image_of, image_of(0, image))
    partial = jnp.concatenate(flatten(image, knots), axis=0)
    for target in range(out_ref.shape[0] // (2 * packed)):
        out_ref[target * 2 * packed : (target + 1) * 2 * packed, :] = partial
    coeffs_copy.wait()


def finish_kernel(
    ranks, spacing, arrived_ref, packs_ref, coeffs_ref, new_offset_ref, new_left_ref, new_search_ref,
):
    nodes, dets = coeffs_ref.shape
    height = packs_ref.shape[1]
    total = arrived_ref[0:height, :]
    for o in range(1, arrived_ref.shape[0] // height):
        total = total + arrived_ref[o * height : (o + 1) * height, :]
    search, left = packs_ref[0], packs_ref[1]
    image = total * (1.0 / spacing) + BASE_PRIOR * search
    norm_old = jnp.sum(left * left, keepdims=True)
    stride_factor = norm_old / jnp.sum(search * image, keepdims=True)
    fresh = left - stride_factor * image
    beta = jnp.sum(fresh * fresh, keepdims=True) / norm_old
    span, group = lax.axis_index("tm"), lax.axis_index("det")
    lines = height // 2
    knots = lines * LANES // dets
    place = (iota((8, LANES), 1) & (dets - 1)) * knots + span * nodes + (iota((8, LANES), 0) & (nodes - 1))

    def own(x):
        x = jnp.where(group == 0, x[:lines, :], x[lines:, :])
        found = jnp.zeros((8, LANES), jnp.float32)
        for p in range(lines):
            values = lane_gather(jnp.broadcast_to(x[p : p + 1, :], (8, LANES)), place & (LANES - 1))
            found = jnp.where((place >> log2(LANES)) == p, values, found)
        return found[:nodes, :dets]

    my_search = own(search)
    my_left = own(fresh)
    new_offset_ref[...] = coeffs_ref[...] + stride_factor * my_search
    new_left_ref[...] = my_left
    new_search_ref[...] = my_left + beta * my_search


def body(
    offset_coeffs,
    leftover_error,
    search_vector,
    node_lattice_offset,
    sky_cell_in_patch,
    analyser_reading_phase,
    segment_sky_patch,
):
    ranks, groups = lax.axis_size("tm"), lax.axis_size("det")
    dets, samples = analyser_reading_phase.shape
    nodes = search_vector.shape[1]
    spacing = samples // nodes
    blocks = segment_sky_patch.size
    cap = max(2, 2 * blocks // ranks)
    slots = ranks * cap
    rows = 2 * cap + 1
    height = groups * ranks * nodes * dets // LANES
    vmem = pl.BlockSpec(memory_space=pltpu.VMEM)
    hbm = pl.BlockSpec(memory_space=pltpu.HBM)
    pin = functools.partial(pltpu.with_memory_space_constraint, memory_space=pltpu.HBM)
    params = pltpu.CompilerParams(vmem_limit_bytes=VMEM_BYTES)
    inputs = (
        segment_sky_patch, node_lattice_offset.reshape(1, dets), search_vector.T, leftover_error.T,
        sky_cell_in_patch, analyser_reading_phase,
    )
    small = jax.ShapeDtypeStruct((nodes, dets), jnp.float32)

    outgoing = pl.pallas_call(
        functools.partial(send_kernel, ranks, cap),
        out_shape=jax.ShapeDtypeStruct((ranks * rows, LANES), jnp.float32),
        in_specs=[hbm] * len(inputs),
        out_specs=vmem,
        scratch_shapes=[pltpu.VMEM(x.shape, x.dtype) for x in inputs]
        + [pltpu.SemaphoreType.DMA((len(inputs),))],
        compiler_params=params,
        name="send",
    )(*[pin(x) for x in inputs])
    arrived = lax.all_to_all(
        outgoing.reshape(ranks, 1, rows * LANES), "tm", split_axis=0, concat_axis=0, tiled=True
    )
    swap = [(i, groups - 1 - i) for i in range(groups)]
    other = lax.ppermute(arrived, "det", swap)
    pages = max(1, ranks * nodes // LANES)
    f32 = jnp.float32
    room = pl.cdiv(2 * slots, BLOCK) * BLOCK + max(COLLECT, PROJECT)
    few = jax.ShapeDtypeStruct((room, LANES), f32)
    shared = (
        few, few, few, jax.ShapeDtypeStruct((pages, room, LANES), f32), few, few, few,
        jax.ShapeDtypeStruct((5, room, LANES), f32),
        jax.ShapeDtypeStruct((room * CHANNELS, LANES), f32),
    )
    arrival = [pltpu.VMEM((slots, LANES), f32)] * 3 + [pltpu.VMEM((ranks, LANES), f32)]
    sizes = (ranks, cap, dets, nodes, spacing)
    *state, packs, count = pl.pallas_call(
        functools.partial(own_kernel, *sizes),
        out_shape=shared + (
            jax.ShapeDtypeStruct((2 * height // groups, LANES), f32),
            jax.ShapeDtypeStruct((8, LANES), jnp.int32),
        ),
        in_specs=[vmem],
        out_specs=(vmem,) * 11,
        scratch_shapes=arrival,
        compiler_params=params,
        cost_estimate=pl.CostEstimate(flops=4_000_000_000, bytes_accessed=4_000_000, transcendentals=0),
        name="own",
    )(arrived.reshape(ranks * rows, LANES))
    *_, partials, packs, coeffs = pl.pallas_call(
        functools.partial(main_kernel, *sizes),
        out_shape=shared + (
            jax.ShapeDtypeStruct((ranks * groups * height, LANES), f32),
            jax.ShapeDtypeStruct((2, height, LANES), f32),
            small,
        ),
        in_specs=[vmem, hbm] + [vmem] * 11,
        out_specs=(vmem,) * 12,
        scratch_shapes=arrival + [
            pltpu.VMEM((CHANNELS, room, LANES), f32),
            pltpu.VMEM((2, 8, BLOCK), f32),
            pltpu.VMEM((pages, room, LANES), f32),
            pltpu.SemaphoreType.DMA((1,)),
        ],
        input_output_aliases={4 + k: k for k in range(9)},
        compiler_params=params,
        name="main",
    )(other.reshape(ranks * rows, LANES), pin(offset_coeffs.T), packs, count, *state)
    gathered = lax.all_to_all(
        partials.reshape(ranks * groups, 1, height * LANES),
        ("tm", "det"), split_axis=0, concat_axis=0, tiled=True,
    )
    results = pl.pallas_call(
        functools.partial(finish_kernel, ranks, spacing),
        out_shape=(small, small, small),
        in_specs=[vmem] * 3,
        out_specs=(vmem, vmem, vmem),
        compiler_params=params,
        name="finish",
    )(gathered.reshape(ranks * groups * height, LANES), packs, coeffs)
    return tuple(result.T for result in results)


def solution(mesh):
    return jax.shard_map(
        body,
        mesh=mesh,
        in_specs=(
            P("det", "tm"),
            P("det", "tm"),
            P("det", "tm"),
            P("det"),
            P("det", "tm"),
            P("det", "tm"),
            P("det", "tm"),
        ),
        out_specs=(P("det", "tm"), P("det", "tm"), P("det", "tm")),
        check_vma=False,
    )
```

```python
import functools

import jax
import jax.numpy as jnp
from jax import lax
from jax.experimental import pallas as pl
from jax.experimental.pallas import tpu as pltpu
from jax.sharding import PartitionSpec as P

PIX_OWN = 131072
MAP_PRIOR = 1.0
BASE_PRIOR = 0.1
LANES = 128
OWNER_TILES = PIX_OWN // LANES
CHANNELS = 8
COUNT = 3
BLOCK = 176
COLLECT = 32
PROJECT = 64
VMEM_BYTES = 32 * 1024 * 1024

SIN_TERMS = (1.0, -1.0 / 6, 1.0 / 120, -1.0 / 5040, 1.0 / 362880, -1.0 / 39916800, 1.0 / 6227020800)
COS_TERMS = (1.0, -0.5, 1.0 / 24, -1.0 / 720, 1.0 / 40320, -1.0 / 3628800, 1.0 / 479001600, -1.0 / 87178291200)
PI_PARTS = (3.140625, 0.0009670257568359375, 6.2771141529083252e-07)


def iota(shape, dim):
    return lax.broadcasted_iota(jnp.int32, shape, dim)


def log2(number):
    assert number & (number - 1) == 0
    return number.bit_length() - 1


def split3(x):
    high = x.astype(jnp.bfloat16)
    rest = x - high.astype(jnp.float32)
    middle = rest.astype(jnp.bfloat16)
    low = (rest - middle.astype(jnp.float32)).astype(jnp.bfloat16)
    return high, middle, low


def dot(a, b):
    return jnp.dot(a, b, preferred_element_type=jnp.float32)


def exact_dot(selector, x):
    high, middle, low = split3(x)
    width = x.shape[1]
    parts = dot(selector, jnp.concatenate([high, middle, low], axis=1))
    return (parts[:, :width] + parts[:, width : 2 * width]) + parts[:, 2 * width :]


def horner(x, terms):
    total = jnp.full_like(x, terms[-1])
    for term in terms[-2::-1]:
        total = total * x + term
    return total


def cos_sin(angle):
    turns = jnp.round(angle * (1.0 / 3.14159265358979))
    rest = angle - turns * PI_PARTS[0]
    rest = rest - turns * PI_PARTS[1]
    rest = rest - turns * PI_PARTS[2]
    half = turns * 0.5
    sign = 1.0 - 4.0 * (half - jnp.floor(half))
    square = rest * rest
    cosine = sign * horner(square, COS_TERMS)
    sine = sign * rest * horner(square, SIN_TERMS)
    return cosine, sine


def spline_weights(fraction):
    square = fraction * fraction
    cube = square * fraction
    rest = 1.0 - fraction
    first = rest * rest * rest * (1.0 / 6.0)
    second = (3.0 * cube - 6.0 * square + 4.0) * (1.0 / 6.0)
    third = (-3.0 * cube + 3.0 * square + 3.0 * fraction + 1.0) * (1.0 / 6.0)
    fourth = cube * (1.0 / 6.0)
    return (first, second, third, fourth)


def aligned(index, unit):
    return index if isinstance(index, int) else pl.multiple_of(index, unit)


def lane_gather(table, index):
    return jnp.take_along_axis(table, index, axis=1, mode="promise_in_bounds")


def send_kernel(
    ranks, cap, patch_hbm, offset_hbm, search_hbm, left_hbm, cell_hbm, phase_hbm, out_ref,
    patch_ref, offset_ref, search_ref, left_ref, cell_ref, phase_ref, sems,
):
    pairs = (
        (patch_hbm, patch_ref), (offset_hbm, offset_ref), (search_hbm, search_ref),
        (left_hbm, left_ref), (cell_hbm, cell_ref), (phase_hbm, phase_ref),
    )
    copies = [pltpu.make_async_copy(src, dst, sems.at[k]) for k, (src, dst) in enumerate(pairs)]
    for copy in copies:
        copy.start()
    copies[0].wait()
    dets, columns = patch_ref.shape
    blocks = dets * columns
    samples = phase_ref.shape[1]
    nodes = search_ref.shape[0]
    span = lax.axis_index("tm")
    rows = 2 * cap + 1
    square = (blocks, blocks)
    tiles = jnp.concatenate(
        [jnp.broadcast_to(patch_ref[:, c : c + 1], (dets, LANES)) for c in range(columns)], axis=0
    )
    owner = (tiles >> log2(OWNER_TILES)).astype(jnp.float32)
    owner_t = owner.T
    same = owner == owner_t
    here, there = iota(square, 0), iota(square, 1)
    rank_row = jnp.sum(jnp.where(same & (here < there), 1.0, 0.0), axis=0, keepdims=True)
    rank_col = jnp.sum(jnp.where(same & (there < here), 1.0, 0.0), axis=1, keepdims=True)
    slot_row = (owner_t[0:1, :] * cap + rank_row).astype(jnp.int32)
    place = (iota((ranks * cap, blocks), 0) == slot_row).astype(jnp.bfloat16)
    for copy in copies[1:]:
        copy.wait()
    cells = jnp.concatenate([cell_ref[:, c * LANES : (c + 1) * LANES] for c in range(columns)], axis=0)
    pixels = (tiles * LANES + cells).astype(jnp.float32)
    phases = jnp.concatenate([phase_ref[:, c * LANES : (c + 1) * LANES] for c in range(columns)], axis=0)
    moved = exact_dot(place, jnp.concatenate([phases, pixels], axis=1))
    slot_phase, slot_pixel = moved[:, :LANES], moved[:, LANES:]
    lane = iota(square, 1)
    small = iota((dets, LANES), 1)
    det_lane = iota((dets, LANES), 0)
    offsets = jnp.broadcast_to(offset_ref[...], (dets, dets))
    diagonal = iota((dets, dets), 0) == iota((dets, dets), 1)
    shift = jnp.sum(jnp.where(diagonal, offsets, 0).astype(jnp.float32), axis=1, keepdims=True)
    shift = jnp.broadcast_to(shift.astype(jnp.int32), (dets, LANES))
    start = jnp.concatenate([c * LANES - shift for c in range(columns)], axis=0) + span * samples
    which = (iota(square, 0) & (dets - 1)) + 1
    rank = rank_col.astype(jnp.int32)
    listing = jnp.where(lane == rank, start, 0) + jnp.where(lane == rank + cap, which, 0)
    listing = listing + jnp.where(lane == rank + 2 * cap, tiles + 1, 0)
    chosen = (iota((ranks, blocks), 0).astype(jnp.float32) == owner_t[0:1, :]).astype(jnp.bfloat16)
    info = exact_dot(chosen, listing.astype(jnp.float32))
    knots = jnp.zeros((1, LANES), jnp.float32)
    for kind, ref in enumerate((search_ref, left_ref)):
        for n in range(nodes):
            column = jnp.broadcast_to(ref[n : n + 1, :], (dets, dets))
            column = jnp.sum(jnp.where(diagonal, column, 0.0), axis=1, keepdims=True)
            at = (3 * cap + kind * dets * nodes + n) + det_lane * nodes
            knots = knots + jnp.sum(jnp.where(small == at, column, 0.0), axis=0, keepdims=True)
    info = info + knots
    for o in range(ranks):
        out_ref[o * rows : o * rows + cap, :] = slot_phase[o * cap : (o + 1) * cap, :]
        out_ref[o * rows + cap : o * rows + 2 * cap, :] = slot_pixel[o * cap : (o + 1) * cap, :]
        out_ref[o * rows + 2 * cap : (o + 1) * rows, :] = info[o : o + 1, :]


def unpack(ranks, cap, ref, phase_ref, cell_ref, info_ref, meta_ref):
    rows = 2 * cap + 1
    for o in range(ranks):
        here = o * cap
        phase_ref[here : here + cap, :] = ref[o * rows : o * rows + cap, :]
        cell_ref[here : here + cap, :] = ref[o * rows + cap : o * rows + 2 * cap, :]
        info = ref[o * rows + 2 * cap : (o + 1) * rows, :]
        info_ref[here : here + cap, :] = jnp.broadcast_to(info, (cap, LANES))
        meta_ref[o : o + 1, :] = info


def rank_slots(ranks, cap, meta_ref):
    lists = []
    spans = LANES // cap
    for k in range(ranks * cap // LANES):
        names = meta_ref[k * spans : (k + 1) * spans, :]
        lane = iota((spans, LANES), 1)
        spread = lane_gather(names, 2 * cap + (lane & (cap - 1)))
        mine = (lane >> log2(cap)) == iota((spans, LANES), 0)
        lists.append(jnp.sum(jnp.where(mine, spread, 0.0), axis=0, keepdims=True))
    names = jnp.concatenate(lists, axis=0).astype(jnp.int32)
    mine = (names > 0) & (((names - 1) & 1) == lax.axis_index("det"))
    ones = jnp.where(mine, 1.0, 0.0)
    earlier = (iota((LANES, LANES), 0) < iota((LANES, LANES), 1)).astype(jnp.bfloat16)
    rank = dot(ones.astype(jnp.bfloat16), earlier)
    sums = jnp.sum(ones, axis=1, keepdims=True)
    before = [jnp.zeros((1, 1), jnp.float32)]
    for k in range(len(lists)):
        before.append(before[-1] + sums[k : k + 1, :])
    rank = rank + jnp.concatenate(before[:-1], axis=0)
    return jnp.where(mine, rank, -1.0).astype(jnp.int32), jnp.sum(ones).astype(jnp.int32)


def flatten(pages, knots):
    dets = pages[0].shape[0]
    if knots >= LANES:
        return [page[d : d + 1, :] for d in range(dets) for page in pages]
    lane, det = iota((dets, LANES), 1), iota((dets, LANES), 0)
    spread = lane_gather(pages[0], lane & (knots - 1))
    per_row = LANES // knots
    mine = (det & (per_row - 1)) == (lane >> log2(knots))
    spread = jnp.where(mine, spread, 0.0)
    rows = []
    for first in range(0, dets, per_row):
        rows.append(jnp.sum(spread[first : first + per_row, :], axis=0, keepdims=True))
    return rows


def read_knots(ranks, cap, dets, nodes, meta_ref):
    width = dets * nodes
    knots = ranks * nodes
    per_row = LANES // width
    kinds = []
    for kind in range(2):
        lines = []
        for p in range(ranks // per_row):
            names = meta_ref[p * per_row : (p + 1) * per_row, :]
            lane = iota((per_row, LANES), 1)
            spread = lane_gather(names, (3 * cap + kind * width) + (lane & (width - 1)))
            here = (lane >> log2(width)) == iota((per_row, LANES), 0)
            lines.append(jnp.sum(jnp.where(here, spread, 0.0), axis=0, keepdims=True))
        lane = iota((dets, LANES), 1)
        tables = []
        for page in range(max(1, knots // LANES)):
            knot = lane + page * LANES
            index = ((knot >> log2(nodes)) & (per_row - 1)) * width
            index = index + iota((dets, LANES), 0) * nodes + (knot & (nodes - 1))
            table = jnp.zeros((dets, LANES), jnp.float32)
            for p, line in enumerate(lines):
                values = lane_gather(jnp.broadcast_to(line, (dets, LANES)), index)
                table = jnp.where((knot >> log2(per_row * nodes)) == p, values, table)
            tables.append(table)
        kinds.append(tables)
    return kinds


def source_of(ranks, cap, dets, total, side, phase_ref, cell_ref, info_ref):
    slots = ranks * cap
    slot = iota((slots, LANES), 0) & (cap - 1)
    lane = iota((slots, LANES), 1)
    listed = lane_gather(info_ref[...], jnp.minimum(lane, 2) * cap + slot)
    listed = listed + jnp.where(lane == 1, (side * dets).astype(jnp.float32), 0.0)
    pixel = cell_ref[...]
    cell = (pixel - jnp.floor(pixel * (1.0 / LANES)) * LANES).astype(jnp.bfloat16)
    whole = split3(listed)
    if max(total, ranks * OWNER_TILES) <= 65536:
        whole = whole[:2]
    return jnp.concatenate(split3(phase_ref[...]) + (cell,) + whole, axis=1)


def take_slots(at, rank, source, dets, side, tables):
    down = iota((BLOCK, LANES), 0) + at
    place = jnp.concatenate(
        [(down == rank[k : k + 1, :]).astype(jnp.bfloat16) for k in range(rank.shape[0])], axis=1
    )
    taken = dot(place, source)
    parts = [taken[:, k * LANES : (k + 1) * LANES] for k in range(taken.shape[1] // LANES)]
    phase = (parts[0] + parts[1]) + parts[2]
    info = sum(parts[5:], parts[4])
    lane = iota((BLOCK, LANES), 1) + (1 + side * dets)
    chosen = ((info[:, 1:2] == lane.astype(jnp.float32)) & (iota((BLOCK, LANES), 1) < dets)).astype(jnp.bfloat16)
    empty = jnp.zeros((LANES - dets, LANES), jnp.float32)
    knots = [exact_dot(chosen, jnp.concatenate([table, empty], axis=0)) for table in tables]
    return phase, parts[3], info, knots


def spline(info_ref, spacing, at, chunk):
    start = jnp.broadcast_to(info_ref[pl.ds(at, chunk), 0:1], (chunk, LANES)).astype(jnp.int32)
    time = start + iota((chunk, LANES), 1)
    interval = time >> log2(spacing)
    fraction = (time & (spacing - 1)).astype(jnp.float32) * (1.0 / spacing)
    return start >> log2(spacing), interval, spline_weights(fraction)


def five_weights(early, weights):
    padded = (0.0,) + weights + (0.0,)
    return [jnp.where(early, padded[term + 1], padded[term]) for term in range(5)]


def bin_chunks(first, last, knots, spacing, few_phase, few_cell, few_info, table_ref, cos_ref, sin_ref, stream_ref, basis_ref, bin_ref):
    pages = table_ref.shape[0]

    def prepare(step):
        at = aligned(step * COLLECT, COLLECT)
        cosine, sine = cos_sin(2.0 * few_phase[pl.ds(at, COLLECT), :])
        base, interval, weights = spline(few_info, spacing, at, COLLECT)
        for term, weight in enumerate(five_weights(interval == base, weights)):
            basis_ref[term, pl.ds(at, COLLECT), :] = weight
        stream = jnp.zeros((COLLECT, LANES), jnp.float32)
        for term in range(4):
            knot = (interval + (term - 1)) & (knots - 1)
            value = lane_gather(table_ref[0, pl.ds(at, COLLECT), :], knot & (LANES - 1))
            for page in range(1, pages):
                more = lane_gather(table_ref[page, pl.ds(at, COLLECT), :], knot & (LANES - 1))
                value = jnp.where((knot >> log2(LANES)) == page, more, value)
            stream = stream + weights[term] * value
        cos_ref[pl.ds(at, COLLECT), :] = cosine
        sin_ref[pl.ds(at, COLLECT), :] = sine
        stream_ref[pl.ds(at, COLLECT), :] = stream

    down = iota((LANES, 2 * LANES), 0).astype(jnp.float32).astype(jnp.bfloat16)
    channel = iota((CHANNELS, LANES), 0)
    zeros = jnp.zeros((2 * CHANNELS, LANES), jnp.bfloat16)

    def collect(step):
        for k in range(COLLECT // 2):
            at = step * COLLECT + 2 * k
            pieces, cells = [], []
            for slot in (at, at + 1):
                stream = jnp.broadcast_to(stream_ref[pl.ds(slot, 1), :], (CHANNELS, LANES))
                cosine = jnp.broadcast_to(cos_ref[pl.ds(slot, 1), :], (CHANNELS, LANES))
                sine = jnp.broadcast_to(sin_ref[pl.ds(slot, 1), :], (CHANNELS, LANES))
                left = jnp.where(channel < 3, stream, jnp.where(channel < 6, 1.0, cosine))
                is_one = (channel == 0) | (channel == 3)
                is_sine = (channel == 2) | (channel == 5) | (channel == 7)
                right = jnp.where(is_one, 1.0, jnp.where(is_sine, sine, cosine))
                entry = left * right
                high = entry.astype(jnp.bfloat16).astype(jnp.float32)
                rest = entry - high
                stack = jnp.concatenate([high, rest], axis=0)
                pieces.append(stack.astype(jnp.bfloat16))
                cells.append(jnp.broadcast_to(few_cell[pl.ds(slot, 1), :].astype(jnp.bfloat16), (LANES, LANES)))
            entry = jnp.concatenate(
                [
                    jnp.concatenate([pieces[0], zeros], axis=1),
                    jnp.concatenate([zeros, pieces[1]], axis=1),
                ],
                axis=0,
            )
            hits = jnp.where(jnp.concatenate(cells, axis=1) == down, jnp.int8(1), jnp.int8(0))
            sums = dot(entry, hits.T.astype(jnp.bfloat16))
            for m in range(2):
                base = 2 * CHANNELS * m
                bin_ref[pl.ds((at + m) * CHANNELS, CHANNELS), :] = (
                    sums[base : base + CHANNELS] + sums[base + CHANNELS : base + 2 * CHANNELS]
                )
    def both(step, carry):
        collect(step)
        prepare(step + 1)
        return carry


    prepare(first)
    lax.fori_loop(first, last, both, 0)


def own_kernel(
    ranks, cap, dets, nodes, spacing, own_ref,
    few_phase, few_cell, few_info, table_ref, cos_ref, sin_ref, stream_ref, basis_ref, bin_ref, packs_ref, count_ref,
    phase_ref, cell_ref, info_ref, meta_ref,
):
    knots = ranks * nodes
    side = lax.axis_index("det")
    unpack(ranks, cap, own_ref, phase_ref, cell_ref, info_ref, meta_ref)
    rank, number = rank_slots(ranks, cap, meta_ref)
    count_ref[...] = jnp.full((8, LANES), number, jnp.int32)
    tables, left = read_knots(ranks, cap, dets, nodes, meta_ref)
    packs_ref[...] = jnp.concatenate(flatten(tables, knots) + flatten(left, knots), axis=0)
    source = source_of(ranks, cap, dets, knots * spacing, side, phase_ref, cell_ref, info_ref)

    def gather_block(block, carry):
        here = pl.ds(aligned(block * BLOCK, 16), BLOCK)
        few_phase[here, :], few_cell[here, :], few_info[here, :], found = take_slots(
            block * BLOCK, rank, source, dets, side, tables
        )
        for page, rows in enumerate(found):
            table_ref[page, here, :] = rows
        return carry

    gather_block(0, 0)
    lax.fori_loop(1, block_count(number, ranks * cap), gather_block, 0)
    bin_chunks(
        0, number >> log2(COLLECT), knots, spacing, few_phase, few_cell, few_info, table_ref,
        cos_ref, sin_ref, stream_ref, basis_ref, bin_ref,
    )


def block_count(number, most):
    return sum(jnp.where(number > start, 1, 0) for start in range(0, most, BLOCK))


def main_kernel(
    ranks, cap, dets, nodes, spacing, other_ref, coeffs_hbm, packs_own, count_ref, *refs,
):
    few_phase, few_cell, few_info, table_ref, cos_ref, sin_ref, stream_ref, basis_ref, bin_ref = refs[9:18]
    out_ref, packs_ref, coeffs_ref = refs[18:21]
    phase_ref, cell_ref, info_ref, meta_ref, total_ref, turned_ref, knots_ref, sems = refs[21:]
    coeffs_copy = pltpu.make_async_copy(coeffs_hbm, coeffs_ref, sems.at[0])
    coeffs_copy.start()
    slots = ranks * cap
    knots = ranks * nodes
    packed = knots * dets // LANES
    group = lax.axis_index("det")
    side = 1 - group

    unpack(ranks, cap, other_ref, phase_ref, cell_ref, info_ref, meta_ref)
    rank, more = rank_slots(ranks, cap, meta_ref)
    ready = jnp.max(count_ref[...])
    rank = jnp.where(rank >= 0, rank + ready, -1)
    number = ready + more
    tables, left = read_knots(ranks, cap, dets, nodes, meta_ref)
    for kind, pages in enumerate((tables, left)):
        here = slice(kind * packed, (kind + 1) * packed)
        packs_ref[kind, pl.ds(group * packed, packed), :] = packs_own[here, :]
        packs_ref[kind, pl.ds(side * packed, packed), :] = jnp.concatenate(flatten(pages, knots), axis=0)
    source = source_of(ranks, cap, dets, knots * spacing, side, phase_ref, cell_ref, info_ref)
    blocks = block_count(number, 2 * slots)
    ready_blocks = block_count(ready, slots)

    def gather_block(block, carry):
        here = pl.ds(aligned(block * BLOCK, 16), BLOCK)
        def before(rows):
            return rows if isinstance(block, int) else jnp.where(block < ready_blocks, rows, 0.0)

        phase, cell, info, found = take_slots(block * BLOCK, rank, source, dets, side, tables)
        few_phase[here, :] = before(few_phase[here, :]) + phase
        few_cell[here, :] = before(few_cell[here, :]) + cell
        info = before(few_info[here, :]) + info
        few_info[here, :] = info
        turned = info.T
        turned_ref[0, pl.ds(block, 1), :] = turned[1:2, :]
        turned_ref[1, pl.ds(block, 1), :] = turned[2:3, :]
        for page, rows in enumerate(found):
            table_ref[page, here, :] = before(table_ref[page, here, :]) + rows
        return carry

    gather_block(0, 0)
    lax.fori_loop(1, blocks, gather_block, 0)

    def steps(chunk):
        return (number + (chunk - 1)) >> log2(chunk)

    bin_chunks(
        ready >> log2(COLLECT), steps(COLLECT), knots, spacing, few_phase, few_cell, few_info, table_ref,
        cos_ref, sin_ref, stream_ref, basis_ref, bin_ref,
    )

    def clear(step, carry):
        at = pl.multiple_of(step * COLLECT * CHANNELS, COLLECT * CHANNELS)
        bin_ref[pl.ds(at, COLLECT * CHANNELS), :] = jnp.zeros((COLLECT * CHANNELS, LANES), jnp.float32)
        return carry

    end = (jnp.maximum(blocks, 1) * BLOCK + (COLLECT - 1)) >> log2(COLLECT)
    lax.fori_loop(steps(COLLECT), end, clear, 0)

    def merge(block, carry):
        at = aligned(block * BLOCK, 16)
        names = few_info[pl.ds(at, BLOCK), 2:3]

        def add(other, carry):
            there = aligned(other * BLOCK, 16)
            same = (names == turned_ref[1, pl.ds(other, 1), :]).astype(jnp.bfloat16)
            for c in range(CHANNELS):
                binned = bin_ref[pl.ds(there * CHANNELS + c, BLOCK, stride=CHANNELS), :]
                high = binned.astype(jnp.bfloat16)
                if c == COUNT:
                    share = dot(same, high)
                else:
                    low = (binned - high.astype(jnp.float32)).astype(jnp.bfloat16)
                    share = dot(same, jnp.concatenate([high, low], axis=1))
                    share = share[:, :LANES] + share[:, LANES:]
                if not isinstance(other, int):
                    share = share + total_ref[c, pl.ds(at, BLOCK), :]
                total_ref[c, pl.ds(at, BLOCK), :] = share
            return carry

        add(0, 0)
        lax.fori_loop(1, blocks, add, 0)
        return carry

    merge(0, 0)
    lax.fori_loop(1, blocks, merge, 0)

    def project(at, size):
        here = pl.ds(aligned(at, 16), size)
        signal, signal_cos, signal_sin, count, cos_sum, sin_sum, cos_cos, cos_sin_sum = (
            total_ref[c, here, :] for c in range(CHANNELS)
        )
        sin_sin = count - cos_cos
        stokes_i = count + MAP_PRIOR
        stokes_q = cos_cos + MAP_PRIOR
        stokes_u = sin_sin + MAP_PRIOR
        minor_one = stokes_q * stokes_u - cos_sin_sum * cos_sin_sum
        minor_two = sin_sum * cos_sin_sum - cos_sum * stokes_u
        minor_three = cos_sum * cos_sin_sum - sin_sum * stokes_q
        minor_four = stokes_i * stokes_u - sin_sum * sin_sum
        minor_five = cos_sum * sin_sum - stokes_i * cos_sin_sum
        minor_six = stokes_i * stokes_q - cos_sum * cos_sum
        determinant = stokes_i * minor_one + cos_sum * minor_two + sin_sum * minor_three
        scale = 1.0 / determinant
        map_i = (minor_one * signal + minor_two * signal_cos + minor_three * signal_sin) * scale
        map_q = (minor_two * signal + minor_four * signal_cos + minor_five * signal_sin) * scale
        map_u = (minor_three * signal + minor_five * signal_cos + minor_six * signal_sin) * scale
        cell = few_cell[here, :].astype(jnp.int32)
        projected = (
            lane_gather(map_i, cell) + cos_ref[here, :] * lane_gather(map_q, cell)
        ) + sin_ref[here, :] * lane_gather(map_u, cell)
        cleaned = stream_ref[here, :] - projected
        valid = few_info[here, 1:2] > 0.5
        base = few_info[here, 0:1].astype(jnp.int32) >> log2(spacing)
        lane = iota((size, LANES), 1)
        pages = [jnp.zeros((size, LANES), jnp.float32) for _ in range(knots_ref.shape[0])]
        for term in range(5):
            value = basis_ref[term, here, :] * cleaned
            high = value.astype(jnp.bfloat16)
            low = (value - high.astype(jnp.float32)).astype(jnp.bfloat16)
            value = dot(jnp.concatenate([high, low], axis=1), jnp.ones((2 * LANES, LANES), jnp.bfloat16))
            knot = (base + (term - 1)) & (knots - 1)
            for page in range(len(pages)):
                pages[page] = pages[page] + jnp.where(lane + page * LANES == knot, value, 0.0)
        for page, sums in enumerate(pages):
            knots_ref[page, here, :] = jnp.where(valid, sums, 0.0)

    def image_of(block, sums):
        at = aligned(block * BLOCK, 16)
        for first in range(0, BLOCK, PROJECT):
            project(at + first, min(PROJECT, BLOCK - first))
        det = (iota((2 * dets, BLOCK), 0) + 1).astype(jnp.float32)
        chosen = (turned_ref[0, pl.ds(block, 1), :] == det).astype(jnp.bfloat16)
        return tuple(
            total + exact_dot(chosen, knots_ref[page, pl.ds(at, BLOCK), :]) for page, total in enumerate(sums)
        )

    image = tuple(jnp.zeros((2 * dets, LANES), jnp.float32) for _ in range(knots_ref.shape[0]))
    image = lax.fori_loop(1, blocks, image_of, image_of(0, image))
    partial = jnp.concatenate(flatten(image, knots), axis=0)
    for target in range(out_ref.shape[0] // (2 * packed)):
        out_ref[target * 2 * packed : (target + 1) * 2 * packed, :] = partial
    coeffs_copy.wait()


def finish_kernel(
    ranks, spacing, arrived_ref, packs_ref, coeffs_ref, new_offset_ref, new_left_ref, new_search_ref,
):
    nodes, dets = coeffs_ref.shape
    height = packs_ref.shape[1]
    total = arrived_ref[0:height, :]
    for o in range(1, arrived_ref.shape[0] // height):
        total = total + arrived_ref[o * height : (o + 1) * height, :]
    search, left = packs_ref[0], packs_ref[1]
    image = total * (1.0 / spacing) + BASE_PRIOR * search
    norm_old = jnp.sum(left * left, keepdims=True)
    stride_factor = norm_old / jnp.sum(search * image, keepdims=True)
    fresh = left - stride_factor * image
    beta = jnp.sum(fresh * fresh, keepdims=True) / norm_old
    span, group = lax.axis_index("tm"), lax.axis_index("det")
    lines = height // 2
    knots = lines * LANES // dets
    place = (iota((8, LANES), 1) & (dets - 1)) * knots + span * nodes + (iota((8, LANES), 0) & (nodes - 1))

    def own(x):
        x = jnp.where(group == 0, x[:lines, :], x[lines:, :])
        found = jnp.zeros((8, LANES), jnp.float32)
        for p in range(lines):
            values = lane_gather(jnp.broadcast_to(x[p : p + 1, :], (8, LANES)), place & (LANES - 1))
            found = jnp.where((place >> log2(LANES)) == p, values, found)
        return found[:nodes, :dets]

    my_search = own(search)
    my_left = own(fresh)
    new_offset_ref[...] = coeffs_ref[...] + stride_factor * my_search
    new_left_ref[...] = my_left
    new_search_ref[...] = my_left + beta * my_search


def body(
    offset_coeffs,
    leftover_error,
    search_vector,
    node_lattice_offset,
    sky_cell_in_patch,
    analyser_reading_phase,
    segment_sky_patch,
):
    ranks, groups = lax.axis_size("tm"), lax.axis_size("det")
    dets, samples = analyser_reading_phase.shape
    nodes = search_vector.shape[1]
    spacing = samples // nodes
    blocks = segment_sky_patch.size
    cap = max(2, 2 * blocks // ranks)
    slots = ranks * cap
    rows = 2 * cap + 1
    height = groups * ranks * nodes * dets // LANES
    vmem = pl.BlockSpec(memory_space=pltpu.VMEM)
    hbm = pl.BlockSpec(memory_space=pltpu.HBM)
    pin = functools.partial(pltpu.with_memory_space_constraint, memory_space=pltpu.HBM)
    params = pltpu.CompilerParams(vmem_limit_bytes=VMEM_BYTES)
    inputs = (
        segment_sky_patch, node_lattice_offset.reshape(1, dets), search_vector.T, leftover_error.T,
        sky_cell_in_patch, analyser_reading_phase,
    )
    small = jax.ShapeDtypeStruct((nodes, dets), jnp.float32)

    outgoing = pl.pallas_call(
        functools.partial(send_kernel, ranks, cap),
        out_shape=jax.ShapeDtypeStruct((ranks * rows, LANES), jnp.float32),
        in_specs=[hbm] * len(inputs),
        out_specs=vmem,
        scratch_shapes=[pltpu.VMEM(x.shape, x.dtype) for x in inputs]
        + [pltpu.SemaphoreType.DMA((len(inputs),))],
        compiler_params=params,
        name="send",
    )(*[pin(x) for x in inputs])
    arrived = lax.all_to_all(
        outgoing.reshape(ranks, 1, rows * LANES), "tm", split_axis=0, concat_axis=0, tiled=True
    )
    swap = [(i, groups - 1 - i) for i in range(groups)]
    other = lax.ppermute(arrived, "det", swap)
    pages = max(1, ranks * nodes // LANES)
    f32 = jnp.float32
    room = pl.cdiv(2 * slots, BLOCK) * BLOCK + max(COLLECT, PROJECT)
    few = jax.ShapeDtypeStruct((room, LANES), f32)
    shared = (
        few, few, few, jax.ShapeDtypeStruct((pages, room, LANES), f32), few, few, few,
        jax.ShapeDtypeStruct((5, room, LANES), f32),
        jax.ShapeDtypeStruct((room * CHANNELS, LANES), f32),
    )
    arrival = [pltpu.VMEM((slots, LANES), f32)] * 3 + [pltpu.VMEM((ranks, LANES), f32)]
    sizes = (ranks, cap, dets, nodes, spacing)
    *state, packs, count = pl.pallas_call(
        functools.partial(own_kernel, *sizes),
        out_shape=shared + (
            jax.ShapeDtypeStruct((2 * height // groups, LANES), f32),
            jax.ShapeDtypeStruct((8, LANES), jnp.int32),
        ),
        in_specs=[vmem],
        out_specs=(vmem,) * 11,
        scratch_shapes=arrival,
        compiler_params=params,
        cost_estimate=pl.CostEstimate(flops=4_000_000_000, bytes_accessed=4_000_000, transcendentals=0),
        name="own",
    )(arrived.reshape(ranks * rows, LANES))
    *_, partials, packs, coeffs = pl.pallas_call(
        functools.partial(main_kernel, *sizes),
        out_shape=shared + (
            jax.ShapeDtypeStruct((ranks * groups * height, LANES), f32),
            jax.ShapeDtypeStruct((2, height, LANES), f32),
            small,
        ),
        in_specs=[vmem, hbm] + [vmem] * 11,
        out_specs=(vmem,) * 12,
        scratch_shapes=arrival + [
            pltpu.VMEM((CHANNELS, room, LANES), f32),
            pltpu.VMEM((2, 8, BLOCK), f32),
            pltpu.VMEM((pages, room, LANES), f32),
            pltpu.SemaphoreType.DMA((1,)),
        ],
        input_output_aliases={4 + k: k for k in range(9)},
        compiler_params=params,
        name="main",
    )(other.reshape(ranks * rows, LANES), pin(offset_coeffs.T), packs, count, *state)
    gathered = lax.all_to_all(
        partials.reshape(ranks * groups, 1, height * LANES),
        ("tm", "det"), split_axis=0, concat_axis=0, tiled=True,
    )
    results = pl.pallas_call(
        functools.partial(finish_kernel, ranks, spacing),
        out_shape=(small, small, small),
        in_specs=[vmem] * 3,
        out_specs=(vmem, vmem, vmem),
        compiler_params=params,
        name="finish",
    )(gathered.reshape(ranks * groups * height, LANES), packs, coeffs)
    return tuple(result.T for result in results)


def solution(mesh):
    return jax.shard_map(
        body,
        mesh=mesh,
        in_specs=(
            P("det", "tm"),
            P("det", "tm"),
            P("det", "tm"),
            P("det"),
            P("det", "tm"),
            P("det", "tm"),
            P("det", "tm"),
        ),
        out_specs=(P("det", "tm"), P("det", "tm"), P("det", "tm")),
        check_vma=False,
    )
```

```python
import functools

import jax
import jax.numpy as jnp
from jax import lax
from jax.experimental import pallas as pl
from jax.experimental.pallas import tpu as pltpu
from jax.sharding import PartitionSpec as P

PIX_OWN = 131072
MAP_PRIOR = 1.0
BASE_PRIOR = 0.1
LANES = 128
OWNER_TILES = PIX_OWN // LANES
CHANNELS = 8
COUNT = 3
BLOCK = 176
COLLECT = 32
PROJECT = 64
VMEM_BYTES = 32 * 1024 * 1024

SIN_TERMS = (1.0, -1.0 / 6, 1.0 / 120, -1.0 / 5040, 1.0 / 362880, -1.0 / 39916800, 1.0 / 6227020800)
COS_TERMS = (1.0, -0.5, 1.0 / 24, -1.0 / 720, 1.0 / 40320, -1.0 / 3628800, 1.0 / 479001600, -1.0 / 87178291200)
PI_PARTS = (3.140625, 0.0009670257568359375, 6.2771141529083252e-07)


def iota(shape, dim):
    return lax.broadcasted_iota(jnp.int32, shape, dim)


def log2(number):
    assert number & (number - 1) == 0
    return number.bit_length() - 1


def split3(x):
    high = x.astype(jnp.bfloat16)
    rest = x - high.astype(jnp.float32)
    middle = rest.astype(jnp.bfloat16)
    low = (rest - middle.astype(jnp.float32)).astype(jnp.bfloat16)
    return high, middle, low


def dot(a, b):
    return jnp.dot(a, b, preferred_element_type=jnp.float32)


def exact_dot(selector, x):
    high, middle, low = split3(x)
    width = x.shape[1]
    parts = dot(selector, jnp.concatenate([high, middle, low], axis=1))
    return (parts[:, :width] + parts[:, width : 2 * width]) + parts[:, 2 * width :]


def horner(x, terms):
    total = jnp.full_like(x, terms[-1])
    for term in terms[-2::-1]:
        total = total * x + term
    return total


def cos_sin(angle):
    turns = jnp.round(angle * (1.0 / 3.14159265358979))
    rest = angle - turns * PI_PARTS[0]
    rest = rest - turns * PI_PARTS[1]
    rest = rest - turns * PI_PARTS[2]
    half = turns * 0.5
    sign = 1.0 - 4.0 * (half - jnp.floor(half))
    square = rest * rest
    cosine = sign * horner(square, COS_TERMS)
    sine = sign * rest * horner(square, SIN_TERMS)
    return cosine, sine


def spline_weights(fraction):
    square = fraction * fraction
    cube = square * fraction
    rest = 1.0 - fraction
    first = rest * rest * rest * (1.0 / 6.0)
    second = (3.0 * cube - 6.0 * square + 4.0) * (1.0 / 6.0)
    third = (-3.0 * cube + 3.0 * square + 3.0 * fraction + 1.0) * (1.0 / 6.0)
    fourth = cube * (1.0 / 6.0)
    return (first, second, third, fourth)


def aligned(index, unit):
    return index if isinstance(index, int) else pl.multiple_of(index, unit)


def lane_gather(table, index):
    return jnp.take_along_axis(table, index, axis=1, mode="promise_in_bounds")


def send_kernel(
    ranks, cap, patch_hbm, offset_hbm, search_hbm, left_hbm, cell_hbm, phase_hbm, out_ref,
    patch_ref, offset_ref, search_ref, left_ref, cell_ref, phase_ref, sems,
):
    pairs = (
        (patch_hbm, patch_ref), (offset_hbm, offset_ref), (search_hbm, search_ref),
        (left_hbm, left_ref), (cell_hbm, cell_ref), (phase_hbm, phase_ref),
    )
    copies = [pltpu.make_async_copy(src, dst, sems.at[k]) for k, (src, dst) in enumerate(pairs)]
    for copy in copies:
        copy.start()
    copies[0].wait()
    dets, columns = patch_ref.shape
    blocks = dets * columns
    samples = phase_ref.shape[1]
    nodes = search_ref.shape[0]
    span = lax.axis_index("tm")
    rows = 2 * cap + 1
    square = (blocks, blocks)
    tiles = jnp.concatenate(
        [jnp.broadcast_to(patch_ref[:, c : c + 1], (dets, LANES)) for c in range(columns)], axis=0
    )
    owner = (tiles >> log2(OWNER_TILES)).astype(jnp.float32)
    owner_t = owner.T
    same = owner == owner_t
    here, there = iota(square, 0), iota(square, 1)
    rank_row = jnp.sum(jnp.where(same & (here < there), 1.0, 0.0), axis=0, keepdims=True)
    rank_col = jnp.sum(jnp.where(same & (there < here), 1.0, 0.0), axis=1, keepdims=True)
    slot_row = (owner_t[0:1, :] * cap + rank_row).astype(jnp.int32)
    place = (iota((ranks * cap, blocks), 0) == slot_row).astype(jnp.bfloat16)
    for copy in copies[1:]:
        copy.wait()
    cells = jnp.concatenate([cell_ref[:, c * LANES : (c + 1) * LANES] for c in range(columns)], axis=0)
    pixels = (tiles * LANES + cells).astype(jnp.float32)
    phases = jnp.concatenate([phase_ref[:, c * LANES : (c + 1) * LANES] for c in range(columns)], axis=0)
    moved = exact_dot(place, jnp.concatenate([phases, pixels], axis=1))
    slot_phase, slot_pixel = moved[:, :LANES], moved[:, LANES:]
    lane = iota(square, 1)
    small = iota((dets, LANES), 1)
    det_lane = iota((dets, LANES), 0)
    offsets = jnp.broadcast_to(offset_ref[...], (dets, dets))
    diagonal = iota((dets, dets), 0) == iota((dets, dets), 1)
    shift = jnp.sum(jnp.where(diagonal, offsets, 0).astype(jnp.float32), axis=1, keepdims=True)
    shift = jnp.broadcast_to(shift.astype(jnp.int32), (dets, LANES))
    start = jnp.concatenate([c * LANES - shift for c in range(columns)], axis=0) + span * samples
    which = (iota(square, 0) & (dets - 1)) + 1
    rank = rank_col.astype(jnp.int32)
    listing = jnp.where(lane == rank, start, 0) + jnp.where(lane == rank + cap, which, 0)
    listing = listing + jnp.where(lane == rank + 2 * cap, tiles + 1, 0)
    chosen = (iota((ranks, blocks), 0).astype(jnp.float32) == owner_t[0:1, :]).astype(jnp.bfloat16)
    info = exact_dot(chosen, listing.astype(jnp.float32))
    knots = jnp.zeros((1, LANES), jnp.float32)
    for kind, ref in enumerate((search_ref, left_ref)):
        for n in range(nodes):
            column = jnp.broadcast_to(ref[n : n + 1, :], (dets, dets))
            column = jnp.sum(jnp.where(diagonal, column, 0.0), axis=1, keepdims=True)
            at = (3 * cap + kind * dets * nodes + n) + det_lane * nodes
            knots = knots + jnp.sum(jnp.where(small == at, column, 0.0), axis=0, keepdims=True)
    info = info + knots
    for o in range(ranks):
        out_ref[o * rows : o * rows + cap, :] = slot_phase[o * cap : (o + 1) * cap, :]
        out_ref[o * rows + cap : o * rows + 2 * cap, :] = slot_pixel[o * cap : (o + 1) * cap, :]
        out_ref[o * rows + 2 * cap : (o + 1) * rows, :] = info[o : o + 1, :]


def unpack(ranks, cap, ref, phase_ref, cell_ref, info_ref, meta_ref):
    rows = 2 * cap + 1
    for o in range(ranks):
        here = o * cap
        phase_ref[here : here + cap, :] = ref[o * rows : o * rows + cap, :]
        cell_ref[here : here + cap, :] = ref[o * rows + cap : o * rows + 2 * cap, :]
        info = ref[o * rows + 2 * cap : (o + 1) * rows, :]
        info_ref[here : here + cap, :] = jnp.broadcast_to(info, (cap, LANES))
        meta_ref[o : o + 1, :] = info


def rank_slots(ranks, cap, meta_ref):
    lists = []
    spans = LANES // cap
    for k in range(ranks * cap // LANES):
        names = meta_ref[k * spans : (k + 1) * spans, :]
        lane = iota((spans, LANES), 1)
        spread = lane_gather(names, 2 * cap + (lane & (cap - 1)))
        mine = (lane >> log2(cap)) == iota((spans, LANES), 0)
        lists.append(jnp.sum(jnp.where(mine, spread, 0.0), axis=0, keepdims=True))
    names = jnp.concatenate(lists, axis=0).astype(jnp.int32)
    mine = (names > 0) & (((names - 1) & 1) == lax.axis_index("det"))
    ones = jnp.where(mine, 1.0, 0.0)
    earlier = (iota((LANES, LANES), 0) < iota((LANES, LANES), 1)).astype(jnp.bfloat16)
    rank = dot(ones.astype(jnp.bfloat16), earlier)
    sums = jnp.sum(ones, axis=1, keepdims=True)
    before = [jnp.zeros((1, 1), jnp.float32)]
    for k in range(len(lists)):
        before.append(before[-1] + sums[k : k + 1, :])
    rank = rank + jnp.concatenate(before[:-1], axis=0)
    return jnp.where(mine, rank, -1.0).astype(jnp.int32), jnp.sum(ones).astype(jnp.int32)


def flatten(pages, knots):
    dets = pages[0].shape[0]
    if knots >= LANES:
        return [page[d : d + 1, :] for d in range(dets) for page in pages]
    lane, det = iota((dets, LANES), 1), iota((dets, LANES), 0)
    spread = lane_gather(pages[0], lane & (knots - 1))
    per_row = LANES // knots
    mine = (det & (per_row - 1)) == (lane >> log2(knots))
    spread = jnp.where(mine, spread, 0.0)
    rows = []
    for first in range(0, dets, per_row):
        rows.append(jnp.sum(spread[first : first + per_row, :], axis=0, keepdims=True))
    return rows


def read_knots(ranks, cap, dets, nodes, meta_ref):
    width = dets * nodes
    knots = ranks * nodes
    per_row = LANES // width
    kinds = []
    for kind in range(2):
        lines = []
        for p in range(ranks // per_row):
            names = meta_ref[p * per_row : (p + 1) * per_row, :]
            lane = iota((per_row, LANES), 1)
            spread = lane_gather(names, (3 * cap + kind * width) + (lane & (width - 1)))
            here = (lane >> log2(width)) == iota((per_row, LANES), 0)
            lines.append(jnp.sum(jnp.where(here, spread, 0.0), axis=0, keepdims=True))
        lane = iota((dets, LANES), 1)
        tables = []
        for page in range(max(1, knots // LANES)):
            knot = lane + page * LANES
            index = ((knot >> log2(nodes)) & (per_row - 1)) * width
            index = index + iota((dets, LANES), 0) * nodes + (knot & (nodes - 1))
            table = jnp.zeros((dets, LANES), jnp.float32)
            for p, line in enumerate(lines):
                values = lane_gather(jnp.broadcast_to(line, (dets, LANES)), index)
                table = jnp.where((knot >> log2(per_row * nodes)) == p, values, table)
            tables.append(table)
        kinds.append(tables)
    return kinds


def source_of(ranks, cap, dets, total, side, phase_ref, cell_ref, info_ref):
    slots = ranks * cap
    slot = iota((slots, LANES), 0) & (cap - 1)
    lane = iota((slots, LANES), 1)
    listed = lane_gather(info_ref[...], jnp.minimum(lane, 2) * cap + slot)
    listed = listed + jnp.where(lane == 1, (side * dets).astype(jnp.float32), 0.0)
    pixel = cell_ref[...]
    cell = (pixel - jnp.floor(pixel * (1.0 / LANES)) * LANES).astype(jnp.bfloat16)
    whole = split3(listed)
    if max(total, ranks * OWNER_TILES) <= 65536:
        whole = whole[:2]
    return jnp.concatenate(split3(phase_ref[...]) + (cell,) + whole, axis=1)


def take_slots(at, rank, source, dets, side, tables):
    down = iota((BLOCK, LANES), 0) + at
    place = jnp.concatenate(
        [(down == rank[k : k + 1, :]).astype(jnp.bfloat16) for k in range(rank.shape[0])], axis=1
    )
    taken = dot(place, source)
    parts = [taken[:, k * LANES : (k + 1) * LANES] for k in range(taken.shape[1] // LANES)]
    phase = (parts[0] + parts[1]) + parts[2]
    info = sum(parts[5:], parts[4])
    lane = iota((BLOCK, LANES), 1) + (1 + side * dets)
    chosen = ((info[:, 1:2] == lane.astype(jnp.float32)) & (iota((BLOCK, LANES), 1) < dets)).astype(jnp.bfloat16)
    empty = jnp.zeros((LANES - dets, LANES), jnp.float32)
    knots = [exact_dot(chosen, jnp.concatenate([table, empty], axis=0)) for table in tables]
    return phase, parts[3], info, knots


def spline(info_ref, spacing, at, chunk):
    start = jnp.broadcast_to(info_ref[pl.ds(at, chunk), 0:1], (chunk, LANES)).astype(jnp.int32)
    time = start + iota((chunk, LANES), 1)
    interval = time >> log2(spacing)
    fraction = (time & (spacing - 1)).astype(jnp.float32) * (1.0 / spacing)
    return start >> log2(spacing), interval, spline_weights(fraction)


def five_weights(early, weights):
    padded = (0.0,) + weights + (0.0,)
    return [jnp.where(early, padded[term + 1], padded[term]) for term in range(5)]


def binning(knots, spacing, few_phase, few_cell, few_info, table_ref, cos_ref, sin_ref, stream_ref, basis_ref, bin_ref):
    pages = table_ref.shape[0]

    def prepare(step):
        at = aligned(step * COLLECT, COLLECT)
        cosine, sine = cos_sin(2.0 * few_phase[pl.ds(at, COLLECT), :])
        base, interval, weights = spline(few_info, spacing, at, COLLECT)
        for term, weight in enumerate(five_weights(interval == base, weights)):
            basis_ref[term, pl.ds(at, COLLECT), :] = weight
        stream = jnp.zeros((COLLECT, LANES), jnp.float32)
        for term in range(4):
            knot = (interval + (term - 1)) & (knots - 1)
            value = lane_gather(table_ref[0, pl.ds(at, COLLECT), :], knot & (LANES - 1))
            for page in range(1, pages):
                more = lane_gather(table_ref[page, pl.ds(at, COLLECT), :], knot & (LANES - 1))
                value = jnp.where((knot >> log2(LANES)) == page, more, value)
            stream = stream + weights[term] * value
        cos_ref[pl.ds(at, COLLECT), :] = cosine
        sin_ref[pl.ds(at, COLLECT), :] = sine
        stream_ref[pl.ds(at, COLLECT), :] = stream

    down = iota((LANES, 2 * LANES), 0).astype(jnp.float32).astype(jnp.bfloat16)
    channel = iota((CHANNELS, LANES), 0)
    zeros = jnp.zeros((2 * CHANNELS, LANES), jnp.bfloat16)

    def collect(step):
        for k in range(COLLECT // 2):
            at = step * COLLECT + 2 * k
            pieces, cells = [], []
            for slot in (at, at + 1):
                stream = jnp.broadcast_to(stream_ref[pl.ds(slot, 1), :], (CHANNELS, LANES))
                cosine = jnp.broadcast_to(cos_ref[pl.ds(slot, 1), :], (CHANNELS, LANES))
                sine = jnp.broadcast_to(sin_ref[pl.ds(slot, 1), :], (CHANNELS, LANES))
                left = jnp.where(channel < 3, stream, jnp.where(channel < 6, 1.0, cosine))
                is_one = (channel == 0) | (channel == 3)
                is_sine = (channel == 2) | (channel == 5) | (channel == 7)
                right = jnp.where(is_one, 1.0, jnp.where(is_sine, sine, cosine))
                entry = left * right
                high = entry.astype(jnp.bfloat16).astype(jnp.float32)
                rest = entry - high
                stack = jnp.concatenate([high, rest], axis=0)
                pieces.append(stack.astype(jnp.bfloat16))
                cells.append(jnp.broadcast_to(few_cell[pl.ds(slot, 1), :].astype(jnp.bfloat16), (LANES, LANES)))
            entry = jnp.concatenate(
                [
                    jnp.concatenate([pieces[0], zeros], axis=1),
                    jnp.concatenate([zeros, pieces[1]], axis=1),
                ],
                axis=0,
            )
            hits = jnp.where(jnp.concatenate(cells, axis=1) == down, jnp.int8(1), jnp.int8(0))
            sums = dot(entry, hits.T.astype(jnp.bfloat16))
            for m in range(2):
                base = 2 * CHANNELS * m
                bin_ref[pl.ds((at + m) * CHANNELS, CHANNELS), :] = (
                    sums[base : base + CHANNELS] + sums[base + CHANNELS : base + 2 * CHANNELS]
                )

    def both(step, carry):
        collect(step)
        prepare(step + 1)
        return carry

    return prepare, both


def own_kernel(
    ranks, cap, dets, nodes, spacing, own_ref,
    few_phase, few_cell, few_info, table_ref, cos_ref, sin_ref, stream_ref, basis_ref, bin_ref, packs_ref, count_ref,
    phase_ref, cell_ref, info_ref, meta_ref,
):
    knots = ranks * nodes
    side = lax.axis_index("det")
    unpack(ranks, cap, own_ref, phase_ref, cell_ref, info_ref, meta_ref)
    rank, number = rank_slots(ranks, cap, meta_ref)
    count_ref[...] = jnp.full((8, LANES), number, jnp.int32)
    tables, left = read_knots(ranks, cap, dets, nodes, meta_ref)
    packs_ref[...] = jnp.concatenate(flatten(tables, knots) + flatten(left, knots), axis=0)
    source = source_of(ranks, cap, dets, knots * spacing, side, phase_ref, cell_ref, info_ref)

    def gather_block(block, carry):
        here = pl.ds(aligned(block * BLOCK, 16), BLOCK)
        few_phase[here, :], few_cell[here, :], few_info[here, :], found = take_slots(
            block * BLOCK, rank, source, dets, side, tables
        )
        for page, rows in enumerate(found):
            table_ref[page, here, :] = rows
        return carry

    prepare, both = binning(
        knots, spacing, few_phase, few_cell, few_info, table_ref,
        cos_ref, sin_ref, stream_ref, basis_ref, bin_ref,
    )
    gather_block(0, 0)
    prepare(0)
    room = pl.cdiv(BLOCK, COLLECT) * COLLECT * CHANNELS
    bin_ref[0:room, :] = jnp.zeros((room, LANES), jnp.float32)
    lax.fori_loop(1, block_count(number, ranks * cap), gather_block, 0)
    lax.fori_loop(0, number >> log2(COLLECT), both, 0)


def block_count(number, most):
    return sum(jnp.where(number > start, 1, 0) for start in range(0, most, BLOCK))


def main_kernel(
    ranks, cap, dets, nodes, spacing, other_ref, coeffs_hbm, packs_own, count_ref, *refs,
):
    few_phase, few_cell, few_info, table_ref, cos_ref, sin_ref, stream_ref, basis_ref, bin_ref = refs[9:18]
    out_ref, packs_ref, coeffs_ref = refs[18:21]
    phase_ref, cell_ref, info_ref, meta_ref, total_ref, turned_ref, knots_ref, sems = refs[21:]
    coeffs_copy = pltpu.make_async_copy(coeffs_hbm, coeffs_ref, sems.at[0])
    coeffs_copy.start()
    slots = ranks * cap
    knots = ranks * nodes
    packed = knots * dets // LANES
    group = lax.axis_index("det")
    side = 1 - group

    unpack(ranks, cap, other_ref, phase_ref, cell_ref, info_ref, meta_ref)
    rank, more = rank_slots(ranks, cap, meta_ref)
    ready = jnp.max(count_ref[...])
    rank = jnp.where(rank >= 0, rank + ready, -1)
    number = ready + more
    tables, left = read_knots(ranks, cap, dets, nodes, meta_ref)
    for kind, pages in enumerate((tables, left)):
        here = slice(kind * packed, (kind + 1) * packed)
        packs_ref[kind, pl.ds(group * packed, packed), :] = packs_own[here, :]
        packs_ref[kind, pl.ds(side * packed, packed), :] = jnp.concatenate(flatten(pages, knots), axis=0)
    source = source_of(ranks, cap, dets, knots * spacing, side, phase_ref, cell_ref, info_ref)
    blocks = block_count(number, 2 * slots)
    ready_blocks = block_count(ready, slots)

    def gather_block(block, carry):
        here = pl.ds(aligned(block * BLOCK, 16), BLOCK)
        def before(rows):
            return rows if isinstance(block, int) else jnp.where(block < ready_blocks, rows, 0.0)

        phase, cell, info, found = take_slots(block * BLOCK, rank, source, dets, side, tables)
        few_phase[here, :] = before(few_phase[here, :]) + phase
        few_cell[here, :] = before(few_cell[here, :]) + cell
        info = before(few_info[here, :]) + info
        few_info[here, :] = info
        turned = info.T
        turned_ref[0, pl.ds(block, 1), :] = turned[1:2, :]
        turned_ref[1, pl.ds(block, 1), :] = turned[2:3, :]
        for page, rows in enumerate(found):
            table_ref[page, here, :] = before(table_ref[page, here, :]) + rows
        return carry

    prepare, both = binning(
        knots, spacing, few_phase, few_cell, few_info, table_ref,
        cos_ref, sin_ref, stream_ref, basis_ref, bin_ref,
    )
    first, last = ready >> log2(COLLECT), (number + (COLLECT - 1)) >> log2(COLLECT)

    def clear(step, carry):
        at = pl.multiple_of(step * COLLECT * CHANNELS, COLLECT * CHANNELS)
        bin_ref[pl.ds(at, COLLECT * CHANNELS), :] = jnp.zeros((COLLECT * CHANNELS, LANES), jnp.float32)
        return carry

    gather_block(0, 0)
    prepare(first)

    @pl.when(blocks > 1)
    def _():
        lax.fori_loop(1, blocks, gather_block, 0)
        lax.fori_loop(last, (blocks * BLOCK + (COLLECT - 1)) >> log2(COLLECT), clear, 0)
        prepare(first)

    lax.fori_loop(first, last, both, 0)

    def merge(block, carry):
        at = aligned(block * BLOCK, 16)
        names = few_info[pl.ds(at, BLOCK), 2:3]

        def add(other, carry):
            there = aligned(other * BLOCK, 16)
            same = (names == turned_ref[1, pl.ds(other, 1), :]).astype(jnp.bfloat16)
            for c in range(CHANNELS):
                binned = bin_ref[pl.ds(there * CHANNELS + c, BLOCK, stride=CHANNELS), :]
                high = binned.astype(jnp.bfloat16)
                if c == COUNT:
                    share = dot(same, high)
                else:
                    low = (binned - high.astype(jnp.float32)).astype(jnp.bfloat16)
                    share = dot(same, jnp.concatenate([high, low], axis=1))
                    share = share[:, :LANES] + share[:, LANES:]
                if not isinstance(other, int):
                    share = share + total_ref[c, pl.ds(at, BLOCK), :]
                total_ref[c, pl.ds(at, BLOCK), :] = share
            return carry

        add(0, 0)
        if not isinstance(block, int):
            lax.fori_loop(1, blocks, add, 0)
        return carry

    def project(at, size):
        here = pl.ds(aligned(at, 16), size)
        signal, signal_cos, signal_sin, count, cos_sum, sin_sum, cos_cos, cos_sin_sum = (
            total_ref[c, here, :] for c in range(CHANNELS)
        )
        sin_sin = count - cos_cos
        stokes_i = count + MAP_PRIOR
        stokes_q = cos_cos + MAP_PRIOR
        stokes_u = sin_sin + MAP_PRIOR
        minor_one = stokes_q * stokes_u - cos_sin_sum * cos_sin_sum
        minor_two = sin_sum * cos_sin_sum - cos_sum * stokes_u
        minor_three = cos_sum * cos_sin_sum - sin_sum * stokes_q
        minor_four = stokes_i * stokes_u - sin_sum * sin_sum
        minor_five = cos_sum * sin_sum - stokes_i * cos_sin_sum
        minor_six = stokes_i * stokes_q - cos_sum * cos_sum
        determinant = stokes_i * minor_one + cos_sum * minor_two + sin_sum * minor_three
        scale = 1.0 / determinant
        map_i = (minor_one * signal + minor_two * signal_cos + minor_three * signal_sin) * scale
        map_q = (minor_two * signal + minor_four * signal_cos + minor_five * signal_sin) * scale
        map_u = (minor_three * signal + minor_five * signal_cos + minor_six * signal_sin) * scale
        cell = few_cell[here, :].astype(jnp.int32)
        projected = (
            lane_gather(map_i, cell) + cos_ref[here, :] * lane_gather(map_q, cell)
        ) + sin_ref[here, :] * lane_gather(map_u, cell)
        cleaned = stream_ref[here, :] - projected
        valid = few_info[here, 1:2] > 0.5
        base = few_info[here, 0:1].astype(jnp.int32) >> log2(spacing)
        lane = iota((size, LANES), 1)
        pages = [jnp.zeros((size, LANES), jnp.float32) for _ in range(knots_ref.shape[0])]
        for term in range(5):
            value = basis_ref[term, here, :] * cleaned
            high = value.astype(jnp.bfloat16)
            low = (value - high.astype(jnp.float32)).astype(jnp.bfloat16)
            value = dot(jnp.concatenate([high, low], axis=1), jnp.ones((2 * LANES, LANES), jnp.bfloat16))
            knot = (base + (term - 1)) & (knots - 1)
            for page in range(len(pages)):
                pages[page] = pages[page] + jnp.where(lane + page * LANES == knot, value, 0.0)
        for page, sums in enumerate(pages):
            knots_ref[page, here, :] = jnp.where(valid, sums, 0.0)

    def image_of(block, sums):
        at = aligned(block * BLOCK, 16)
        for first in range(0, BLOCK, PROJECT):
            project(at + first, min(PROJECT, BLOCK - first))
        det = (iota((2 * dets, BLOCK), 0) + 1).astype(jnp.float32)
        chosen = (turned_ref[0, pl.ds(block, 1), :] == det).astype(jnp.bfloat16)
        return tuple(
            total + exact_dot(chosen, knots_ref[page, pl.ds(at, BLOCK), :]) for page, total in enumerate(sums)
        )

    def write(image):
        partial = jnp.concatenate(flatten(image, knots), axis=0)
        for target in range(out_ref.shape[0] // (2 * packed)):
            out_ref[target * 2 * packed : (target + 1) * 2 * packed, :] = partial

    zero = tuple(jnp.zeros((2 * dets, LANES), jnp.float32) for _ in range(knots_ref.shape[0]))
    merge(0, 0)
    write(image_of(0, zero))

    @pl.when(blocks > 1)
    def _():
        lax.fori_loop(0, blocks, merge, 0)
        write(lax.fori_loop(0, blocks, image_of, zero))

    coeffs_copy.wait()


def finish_kernel(
    ranks, spacing, arrived_ref, packs_ref, coeffs_ref, new_offset_ref, new_left_ref, new_search_ref,
):
    nodes, dets = coeffs_ref.shape
    height = packs_ref.shape[1]
    total = arrived_ref[0:height, :]
    for o in range(1, arrived_ref.shape[0] // height):
        total = total + arrived_ref[o * height : (o + 1) * height, :]
    search, left = packs_ref[0], packs_ref[1]
    image = total * (1.0 / spacing) + BASE_PRIOR * search
    norm_old = jnp.sum(left * left, keepdims=True)
    stride_factor = norm_old / jnp.sum(search * image, keepdims=True)
    fresh = left - stride_factor * image
    beta = jnp.sum(fresh * fresh, keepdims=True) / norm_old
    span, group = lax.axis_index("tm"), lax.axis_index("det")
    lines = height // 2
    knots = lines * LANES // dets
    place = (iota((8, LANES), 1) & (dets - 1)) * knots + span * nodes + (iota((8, LANES), 0) & (nodes - 1))

    def own(x):
        x = jnp.where(group == 0, x[:lines, :], x[lines:, :])
        found = jnp.zeros((8, LANES), jnp.float32)
        for p in range(lines):
            values = lane_gather(jnp.broadcast_to(x[p : p + 1, :], (8, LANES)), place & (LANES - 1))
            found = jnp.where((place >> log2(LANES)) == p, values, found)
        return found[:nodes, :dets]

    my_search = own(search)
    my_left = own(fresh)
    new_offset_ref[...] = coeffs_ref[...] + stride_factor * my_search
    new_left_ref[...] = my_left
    new_search_ref[...] = my_left + beta * my_search


def body(
    offset_coeffs,
    leftover_error,
    search_vector,
    node_lattice_offset,
    sky_cell_in_patch,
    analyser_reading_phase,
    segment_sky_patch,
):
    ranks, groups = lax.axis_size("tm"), lax.axis_size("det")
    dets, samples = analyser_reading_phase.shape
    nodes = search_vector.shape[1]
    spacing = samples // nodes
    blocks = segment_sky_patch.size
    cap = max(2, 2 * blocks // ranks)
    slots = ranks * cap
    rows = 2 * cap + 1
    height = groups * ranks * nodes * dets // LANES
    vmem = pl.BlockSpec(memory_space=pltpu.VMEM)
    hbm = pl.BlockSpec(memory_space=pltpu.HBM)
    pin = functools.partial(pltpu.with_memory_space_constraint, memory_space=pltpu.HBM)
    params = pltpu.CompilerParams(vmem_limit_bytes=VMEM_BYTES)
    inputs = (
        segment_sky_patch, node_lattice_offset.reshape(1, dets), search_vector.T, leftover_error.T,
        sky_cell_in_patch, analyser_reading_phase,
    )
    small = jax.ShapeDtypeStruct((nodes, dets), jnp.float32)

    outgoing = pl.pallas_call(
        functools.partial(send_kernel, ranks, cap),
        out_shape=jax.ShapeDtypeStruct((ranks * rows, LANES), jnp.float32),
        in_specs=[hbm] * len(inputs),
        out_specs=vmem,
        scratch_shapes=[pltpu.VMEM(x.shape, x.dtype) for x in inputs]
        + [pltpu.SemaphoreType.DMA((len(inputs),))],
        compiler_params=params,
        name="send",
    )(*[pin(x) for x in inputs])
    arrived = lax.all_to_all(
        outgoing.reshape(ranks, 1, rows * LANES), "tm", split_axis=0, concat_axis=0, tiled=True
    )
    swap = [(i, groups - 1 - i) for i in range(groups)]
    other = lax.ppermute(arrived, "det", swap)
    pages = max(1, ranks * nodes // LANES)
    f32 = jnp.float32
    room = pl.cdiv(2 * slots, BLOCK) * BLOCK + max(COLLECT, PROJECT)
    few = jax.ShapeDtypeStruct((room, LANES), f32)
    shared = (
        few, few, few, jax.ShapeDtypeStruct((pages, room, LANES), f32), few, few, few,
        jax.ShapeDtypeStruct((5, room, LANES), f32),
        jax.ShapeDtypeStruct((room * CHANNELS, LANES), f32),
    )
    arrival = [pltpu.VMEM((slots, LANES), f32)] * 3 + [pltpu.VMEM((ranks, LANES), f32)]
    sizes = (ranks, cap, dets, nodes, spacing)
    *state, packs, count = pl.pallas_call(
        functools.partial(own_kernel, *sizes),
        out_shape=shared + (
            jax.ShapeDtypeStruct((2 * height // groups, LANES), f32),
            jax.ShapeDtypeStruct((8, LANES), jnp.int32),
        ),
        in_specs=[vmem],
        out_specs=(vmem,) * 11,
        scratch_shapes=arrival,
        compiler_params=params,
        cost_estimate=pl.CostEstimate(flops=4_000_000_000, bytes_accessed=4_000_000, transcendentals=0),
        name="own",
    )(arrived.reshape(ranks * rows, LANES))
    *_, partials, packs, coeffs = pl.pallas_call(
        functools.partial(main_kernel, *sizes),
        out_shape=shared + (
            jax.ShapeDtypeStruct((ranks * groups * height, LANES), f32),
            jax.ShapeDtypeStruct((2, height, LANES), f32),
            small,
        ),
        in_specs=[vmem, hbm] + [vmem] * 11,
        out_specs=(vmem,) * 12,
        scratch_shapes=arrival + [
            pltpu.VMEM((CHANNELS, room, LANES), f32),
            pltpu.VMEM((2, 8, BLOCK), f32),
            pltpu.VMEM((pages, room, LANES), f32),
            pltpu.SemaphoreType.DMA((1,)),
        ],
        input_output_aliases={4 + k: k for k in range(9)},
        compiler_params=params,
        name="main",
    )(other.reshape(ranks * rows, LANES), pin(offset_coeffs.T), packs, count, *state)
    gathered = lax.all_to_all(
        partials.reshape(ranks * groups, 1, height * LANES),
        ("tm", "det"), split_axis=0, concat_axis=0, tiled=True,
    )
    results = pl.pallas_call(
        functools.partial(finish_kernel, ranks, spacing),
        out_shape=(small, small, small),
        in_specs=[vmem] * 3,
        out_specs=(vmem, vmem, vmem),
        compiler_params=params,
        name="finish",
    )(gathered.reshape(ranks * groups * height, LANES), packs, coeffs)
    return tuple(result.T for result in results)


def solution(mesh):
    return jax.shard_map(
        body,
        mesh=mesh,
        in_specs=(
            P("det", "tm"),
            P("det", "tm"),
            P("det", "tm"),
            P("det"),
            P("det", "tm"),
            P("det", "tm"),
            P("det", "tm"),
        ),
        out_specs=(P("det", "tm"), P("det", "tm"), P("det", "tm")),
        check_vma=False,
    )
```

```python
import functools

import jax
import jax.numpy as jnp
from jax import lax
from jax.experimental import pallas as pl
from jax.experimental.pallas import tpu as pltpu
from jax.sharding import PartitionSpec as P

PIX_OWN = 131072
MAP_PRIOR = 1.0
BASE_PRIOR = 0.1
LANES = 128
OWNER_TILES = PIX_OWN // LANES
CHANNELS = 8
COUNT = 3
BLOCK = 176
COLLECT = 32
PROJECT = 64
VMEM_BYTES = 32 * 1024 * 1024

SIN_TERMS = (1.0, -1.0 / 6, 1.0 / 120, -1.0 / 5040, 1.0 / 362880, -1.0 / 39916800, 1.0 / 6227020800)
COS_TERMS = (1.0, -0.5, 1.0 / 24, -1.0 / 720, 1.0 / 40320, -1.0 / 3628800, 1.0 / 479001600, -1.0 / 87178291200)
PI_PARTS = (3.140625, 0.0009670257568359375, 6.2771141529083252e-07)


def iota(shape, dim):
    return lax.broadcasted_iota(jnp.int32, shape, dim)


def log2(number):
    assert number & (number - 1) == 0
    return number.bit_length() - 1


def split3(x):
    high = x.astype(jnp.bfloat16)
    rest = x - high.astype(jnp.float32)
    middle = rest.astype(jnp.bfloat16)
    low = (rest - middle.astype(jnp.float32)).astype(jnp.bfloat16)
    return high, middle, low


def dot(a, b):
    return jnp.dot(a, b, preferred_element_type=jnp.float32)


def exact_dot(selector, x):
    high, middle, low = split3(x)
    width = x.shape[1]
    parts = dot(selector, jnp.concatenate([high, middle, low], axis=1))
    return (parts[:, :width] + parts[:, width : 2 * width]) + parts[:, 2 * width :]


def horner(x, terms):
    total = jnp.full_like(x, terms[-1])
    for term in terms[-2::-1]:
        total = total * x + term
    return total


def cos_sin(angle):
    turns = jnp.round(angle * (1.0 / 3.14159265358979))
    rest = angle - turns * PI_PARTS[0]
    rest = rest - turns * PI_PARTS[1]
    rest = rest - turns * PI_PARTS[2]
    half = turns * 0.5
    sign = 1.0 - 4.0 * (half - jnp.floor(half))
    square = rest * rest
    cosine = sign * horner(square, COS_TERMS)
    sine = sign * rest * horner(square, SIN_TERMS)
    return cosine, sine


def spline_weights(fraction):
    square = fraction * fraction
    cube = square * fraction
    rest = 1.0 - fraction
    first = rest * rest * rest * (1.0 / 6.0)
    second = (3.0 * cube - 6.0 * square + 4.0) * (1.0 / 6.0)
    third = (-3.0 * cube + 3.0 * square + 3.0 * fraction + 1.0) * (1.0 / 6.0)
    fourth = cube * (1.0 / 6.0)
    return (first, second, third, fourth)


def aligned(index, unit):
    return index if isinstance(index, int) else pl.multiple_of(index, unit)


def lane_gather(table, index):
    return jnp.take_along_axis(table, index, axis=1, mode="promise_in_bounds")


def send_kernel(
    ranks, cap, patch_hbm, offset_hbm, search_hbm, left_hbm, cell_hbm, phase_hbm, out_ref,
    patch_ref, offset_ref, search_ref, left_ref, cell_ref, phase_ref, sems,
):
    pairs = (
        (patch_hbm, patch_ref), (offset_hbm, offset_ref), (search_hbm, search_ref),
        (left_hbm, left_ref), (cell_hbm, cell_ref), (phase_hbm, phase_ref),
    )
    copies = [pltpu.make_async_copy(src, dst, sems.at[k]) for k, (src, dst) in enumerate(pairs)]
    for copy in copies:
        copy.start()
    copies[0].wait()
    dets, columns = patch_ref.shape
    blocks = dets * columns
    samples = phase_ref.shape[1]
    nodes = search_ref.shape[0]
    span = lax.axis_index("tm")
    rows = 2 * cap + 1
    square = (blocks, blocks)
    tiles = jnp.concatenate(
        [jnp.broadcast_to(patch_ref[:, c : c + 1], (dets, LANES)) for c in range(columns)], axis=0
    )
    owner = (tiles >> log2(OWNER_TILES)).astype(jnp.float32)
    owner_t = owner.T
    same = owner == owner_t
    here, there = iota(square, 0), iota(square, 1)
    rank_row = jnp.sum(jnp.where(same & (here < there), 1.0, 0.0), axis=0, keepdims=True)
    rank_col = jnp.sum(jnp.where(same & (there < here), 1.0, 0.0), axis=1, keepdims=True)
    slot_row = (owner_t[0:1, :] * cap + rank_row).astype(jnp.int32)
    place = (iota((ranks * cap, blocks), 0) == slot_row).astype(jnp.bfloat16)
    for copy in copies[1:]:
        copy.wait()
    cells = jnp.concatenate([cell_ref[:, c * LANES : (c + 1) * LANES] for c in range(columns)], axis=0)
    pixels = (tiles * LANES + cells).astype(jnp.float32)
    phases = jnp.concatenate([phase_ref[:, c * LANES : (c + 1) * LANES] for c in range(columns)], axis=0)
    moved = exact_dot(place, jnp.concatenate([phases, pixels], axis=1))
    slot_phase, slot_pixel = moved[:, :LANES], moved[:, LANES:]
    lane = iota(square, 1)
    small = iota((dets, LANES), 1)
    det_lane = iota((dets, LANES), 0)
    offsets = jnp.broadcast_to(offset_ref[...], (dets, dets))
    diagonal = iota((dets, dets), 0) == iota((dets, dets), 1)
    shift = jnp.sum(jnp.where(diagonal, offsets, 0).astype(jnp.float32), axis=1, keepdims=True)
    shift = jnp.broadcast_to(shift.astype(jnp.int32), (dets, LANES))
    start = jnp.concatenate([c * LANES - shift for c in range(columns)], axis=0) + span * samples
    which = (iota(square, 0) & (dets - 1)) + 1
    rank = rank_col.astype(jnp.int32)
    listing = jnp.where(lane == rank, start, 0) + jnp.where(lane == rank + cap, which, 0)
    listing = listing + jnp.where(lane == rank + 2 * cap, tiles + 1, 0)
    chosen = (iota((ranks, blocks), 0).astype(jnp.float32) == owner_t[0:1, :]).astype(jnp.bfloat16)
    info = exact_dot(chosen, listing.astype(jnp.float32))
    knots = jnp.zeros((1, LANES), jnp.float32)
    for kind, ref in enumerate((search_ref, left_ref)):
        for n in range(nodes):
            column = jnp.broadcast_to(ref[n : n + 1, :], (dets, dets))
            column = jnp.sum(jnp.where(diagonal, column, 0.0), axis=1, keepdims=True)
            at = (3 * cap + kind * dets * nodes + n) + det_lane * nodes
            knots = knots + jnp.sum(jnp.where(small == at, column, 0.0), axis=0, keepdims=True)
    info = info + knots
    for o in range(ranks):
        out_ref[o * rows : o * rows + cap, :] = slot_phase[o * cap : (o + 1) * cap, :]
        out_ref[o * rows + cap : o * rows + 2 * cap, :] = slot_pixel[o * cap : (o + 1) * cap, :]
        out_ref[o * rows + 2 * cap : (o + 1) * rows, :] = info[o : o + 1, :]


def unpack(ranks, cap, ref):
    rows = 2 * cap + 1
    starts = range(0, ranks * rows, rows)
    phase = jnp.concatenate([ref[s : s + cap, :] for s in starts], axis=0)
    pixel = jnp.concatenate([ref[s + cap : s + 2 * cap, :] for s in starts], axis=0)
    lines = [ref[s + 2 * cap : s + rows, :] for s in starts]
    info = jnp.concatenate([jnp.broadcast_to(line, (cap, LANES)) for line in lines], axis=0)
    return phase, pixel, info, jnp.concatenate(lines, axis=0)


def rank_slots(ranks, cap, meta):
    lists = []
    spans = LANES // cap
    for k in range(ranks * cap // LANES):
        names = meta[k * spans : (k + 1) * spans, :]
        lane = iota((spans, LANES), 1)
        spread = lane_gather(names, 2 * cap + (lane & (cap - 1)))
        mine = (lane >> log2(cap)) == iota((spans, LANES), 0)
        lists.append(jnp.sum(jnp.where(mine, spread, 0.0), axis=0, keepdims=True))
    names = jnp.concatenate(lists, axis=0).astype(jnp.int32)
    mine = (names > 0) & (((names - 1) & 1) == lax.axis_index("det"))
    ones = jnp.where(mine, 1.0, 0.0)
    earlier = (iota((LANES, LANES), 0) < iota((LANES, LANES), 1)).astype(jnp.bfloat16)
    rank = dot(ones.astype(jnp.bfloat16), earlier)
    sums = jnp.sum(ones, axis=1, keepdims=True)
    before = [jnp.zeros((1, 1), jnp.float32)]
    for k in range(len(lists)):
        before.append(before[-1] + sums[k : k + 1, :])
    rank = rank + jnp.concatenate(before[:-1], axis=0)
    return jnp.where(mine, rank, -1.0).astype(jnp.int32), jnp.sum(ones).astype(jnp.int32)


def flatten(pages, knots):
    dets = pages[0].shape[0]
    if knots >= LANES:
        return [page[d : d + 1, :] for d in range(dets) for page in pages]
    lane, det = iota((dets, LANES), 1), iota((dets, LANES), 0)
    spread = lane_gather(pages[0], lane & (knots - 1))
    per_row = LANES // knots
    mine = (det & (per_row - 1)) == (lane >> log2(knots))
    spread = jnp.where(mine, spread, 0.0)
    rows = []
    for first in range(0, dets, per_row):
        rows.append(jnp.sum(spread[first : first + per_row, :], axis=0, keepdims=True))
    return rows


def read_knots(ranks, cap, dets, nodes, meta):
    width = dets * nodes
    knots = ranks * nodes
    per_row = LANES // width
    kinds = []
    for kind in range(2):
        lines = []
        for p in range(ranks // per_row):
            names = meta[p * per_row : (p + 1) * per_row, :]
            lane = iota((per_row, LANES), 1)
            spread = lane_gather(names, (3 * cap + kind * width) + (lane & (width - 1)))
            here = (lane >> log2(width)) == iota((per_row, LANES), 0)
            lines.append(jnp.sum(jnp.where(here, spread, 0.0), axis=0, keepdims=True))
        lane = iota((dets, LANES), 1)
        tables = []
        for page in range(max(1, knots // LANES)):
            knot = lane + page * LANES
            index = ((knot >> log2(nodes)) & (per_row - 1)) * width
            index = index + iota((dets, LANES), 0) * nodes + (knot & (nodes - 1))
            table = jnp.zeros((dets, LANES), jnp.float32)
            for p, line in enumerate(lines):
                values = lane_gather(jnp.broadcast_to(line, (dets, LANES)), index)
                table = jnp.where((knot >> log2(per_row * nodes)) == p, values, table)
            tables.append(table)
        kinds.append(tables)
    return kinds


def source_of(ranks, cap, dets, total, side, phase, pixel, info):
    slots = ranks * cap
    slot = iota((slots, LANES), 0) & (cap - 1)
    lane = iota((slots, LANES), 1)
    listed = lane_gather(info, jnp.minimum(lane, 2) * cap + slot)
    listed = listed + jnp.where(lane == 1, (side * dets).astype(jnp.float32), 0.0)
    cell = (pixel - jnp.floor(pixel * (1.0 / LANES)) * LANES).astype(jnp.bfloat16)
    whole = split3(listed)
    if max(total, ranks * OWNER_TILES) <= 65536:
        whole = whole[:2]
    return jnp.concatenate(split3(phase) + (cell,) + whole, axis=1)


def take_slots(at, rank, source, dets, side, tables):
    down = iota((BLOCK, LANES), 0) + at
    place = jnp.concatenate(
        [(down == rank[k : k + 1, :]).astype(jnp.bfloat16) for k in range(rank.shape[0])], axis=1
    )
    taken = dot(place, source)
    parts = [taken[:, k * LANES : (k + 1) * LANES] for k in range(taken.shape[1] // LANES)]
    phase = (parts[0] + parts[1]) + parts[2]
    info = sum(parts[5:], parts[4])
    lane = iota((BLOCK, LANES), 1) + (1 + side * dets)
    chosen = ((info[:, 1:2] == lane.astype(jnp.float32)) & (iota((BLOCK, LANES), 1) < dets)).astype(jnp.bfloat16)
    empty = jnp.zeros((LANES - dets, LANES), jnp.float32)
    knots = [exact_dot(chosen, jnp.concatenate([table, empty], axis=0)) for table in tables]
    return phase, parts[3], info, knots


def spline(info_ref, spacing, at, chunk):
    start = jnp.broadcast_to(info_ref[pl.ds(at, chunk), 0:1], (chunk, LANES)).astype(jnp.int32)
    time = start + iota((chunk, LANES), 1)
    interval = time >> log2(spacing)
    fraction = (time & (spacing - 1)).astype(jnp.float32) * (1.0 / spacing)
    return start >> log2(spacing), interval, spline_weights(fraction)


def five_weights(early, weights):
    padded = (0.0,) + weights + (0.0,)
    return [jnp.where(early, padded[term + 1], padded[term]) for term in range(5)]


def binning(knots, spacing, few_phase, few_cell, few_info, table_ref, cos_ref, sin_ref, stream_ref, basis_ref, bin_ref):
    pages = table_ref.shape[0]

    def prepare(step):
        at = aligned(step * COLLECT, COLLECT)
        cosine, sine = cos_sin(2.0 * few_phase[pl.ds(at, COLLECT), :])
        base, interval, weights = spline(few_info, spacing, at, COLLECT)
        for term, weight in enumerate(five_weights(interval == base, weights)):
            basis_ref[term, pl.ds(at, COLLECT), :] = weight
        stream = jnp.zeros((COLLECT, LANES), jnp.float32)
        for term in range(4):
            knot = (interval + (term - 1)) & (knots - 1)
            value = lane_gather(table_ref[0, pl.ds(at, COLLECT), :], knot & (LANES - 1))
            for page in range(1, pages):
                more = lane_gather(table_ref[page, pl.ds(at, COLLECT), :], knot & (LANES - 1))
                value = jnp.where((knot >> log2(LANES)) == page, more, value)
            stream = stream + weights[term] * value
        cos_ref[pl.ds(at, COLLECT), :] = cosine
        sin_ref[pl.ds(at, COLLECT), :] = sine
        stream_ref[pl.ds(at, COLLECT), :] = stream

    down = iota((LANES, 2 * LANES), 0).astype(jnp.float32).astype(jnp.bfloat16)
    channel = iota((CHANNELS, LANES), 0)
    zeros = jnp.zeros((2 * CHANNELS, LANES), jnp.bfloat16)

    def collect(step):
        for k in range(COLLECT // 2):
            at = step * COLLECT + 2 * k
            pieces, cells = [], []
            for slot in (at, at + 1):
                stream = jnp.broadcast_to(stream_ref[pl.ds(slot, 1), :], (CHANNELS, LANES))
                cosine = jnp.broadcast_to(cos_ref[pl.ds(slot, 1), :], (CHANNELS, LANES))
                sine = jnp.broadcast_to(sin_ref[pl.ds(slot, 1), :], (CHANNELS, LANES))
                left = jnp.where(channel < 3, stream, jnp.where(channel < 6, 1.0, cosine))
                is_one = (channel == 0) | (channel == 3)
                is_sine = (channel == 2) | (channel == 5) | (channel == 7)
                right = jnp.where(is_one, 1.0, jnp.where(is_sine, sine, cosine))
                entry = left * right
                high = entry.astype(jnp.bfloat16).astype(jnp.float32)
                rest = entry - high
                stack = jnp.concatenate([high, rest], axis=0)
                pieces.append(stack.astype(jnp.bfloat16))
                cells.append(jnp.broadcast_to(few_cell[pl.ds(slot, 1), :].astype(jnp.bfloat16), (LANES, LANES)))
            entry = jnp.concatenate(
                [
                    jnp.concatenate([pieces[0], zeros], axis=1),
                    jnp.concatenate([zeros, pieces[1]], axis=1),
                ],
                axis=0,
            )
            hits = jnp.where(jnp.concatenate(cells, axis=1) == down, jnp.int8(1), jnp.int8(0))
            sums = dot(entry, hits.T.astype(jnp.bfloat16))
            for m in range(2):
                base = 2 * CHANNELS * m
                bin_ref[pl.ds((at + m) * CHANNELS, CHANNELS), :] = (
                    sums[base : base + CHANNELS] + sums[base + CHANNELS : base + 2 * CHANNELS]
                )

    def both(step, carry):
        collect(step)
        prepare(step + 1)
        return carry

    return prepare, both


def own_kernel(
    ranks, cap, dets, nodes, spacing, own_ref,
    few_phase, few_cell, few_info, table_ref, cos_ref, sin_ref, stream_ref, basis_ref, bin_ref, packs_ref, count_ref,
):
    knots = ranks * nodes
    side = lax.axis_index("det")
    phase, pixel, info, meta = unpack(ranks, cap, own_ref)
    rank, number = rank_slots(ranks, cap, meta)
    count_ref[...] = jnp.full((8, LANES), number, jnp.int32)
    tables, left = read_knots(ranks, cap, dets, nodes, meta)
    packs_ref[...] = jnp.concatenate(flatten(tables, knots) + flatten(left, knots), axis=0)
    source = source_of(ranks, cap, dets, knots * spacing, side, phase, pixel, info)

    def gather_block(block, carry):
        here = pl.ds(aligned(block * BLOCK, 16), BLOCK)
        few_phase[here, :], few_cell[here, :], few_info[here, :], found = take_slots(
            block * BLOCK, rank, source, dets, side, tables
        )
        for page, rows in enumerate(found):
            table_ref[page, here, :] = rows
        return carry

    prepare, both = binning(
        knots, spacing, few_phase, few_cell, few_info, table_ref,
        cos_ref, sin_ref, stream_ref, basis_ref, bin_ref,
    )
    gather_block(0, 0)
    prepare(0)
    room = pl.cdiv(BLOCK, COLLECT) * COLLECT * CHANNELS
    bin_ref[0:room, :] = jnp.zeros((room, LANES), jnp.float32)
    lax.fori_loop(1, block_count(number, ranks * cap), gather_block, 0)
    lax.fori_loop(0, number >> log2(COLLECT), both, 0)


def block_count(number, most):
    return sum(jnp.where(number > start, 1, 0) for start in range(0, most, BLOCK))


def main_kernel(
    ranks, cap, dets, nodes, spacing, other_ref, coeffs_hbm, packs_own, count_ref, *refs,
):
    few_phase, few_cell, few_info, table_ref, cos_ref, sin_ref, stream_ref, basis_ref, bin_ref = refs[9:18]
    out_ref, packs_ref, coeffs_ref = refs[18:21]
    total_ref, turned_ref, knots_ref, sems = refs[21:]
    coeffs_copy = pltpu.make_async_copy(coeffs_hbm, coeffs_ref, sems.at[0])
    coeffs_copy.start()
    slots = ranks * cap
    knots = ranks * nodes
    packed = knots * dets // LANES
    group = lax.axis_index("det")
    side = 1 - group

    phase, pixel, info, meta = unpack(ranks, cap, other_ref)
    rank, more = rank_slots(ranks, cap, meta)
    ready = jnp.max(count_ref[...])
    rank = jnp.where(rank >= 0, rank + ready, -1)
    number = ready + more
    tables, left = read_knots(ranks, cap, dets, nodes, meta)
    for kind, pages in enumerate((tables, left)):
        here = slice(kind * packed, (kind + 1) * packed)
        packs_ref[kind, pl.ds(group * packed, packed), :] = packs_own[here, :]
        packs_ref[kind, pl.ds(side * packed, packed), :] = jnp.concatenate(flatten(pages, knots), axis=0)
    source = source_of(ranks, cap, dets, knots * spacing, side, phase, pixel, info)
    blocks = block_count(number, 2 * slots)
    ready_blocks = block_count(ready, slots)

    def gather_block(block, carry):
        here = pl.ds(aligned(block * BLOCK, 16), BLOCK)
        def before(rows):
            return rows if isinstance(block, int) else jnp.where(block < ready_blocks, rows, 0.0)

        phase, cell, info, found = take_slots(block * BLOCK, rank, source, dets, side, tables)
        few_phase[here, :] = before(few_phase[here, :]) + phase
        few_cell[here, :] = before(few_cell[here, :]) + cell
        info = before(few_info[here, :]) + info
        few_info[here, :] = info
        turned = info.T
        turned_ref[0, pl.ds(block, 1), :] = turned[1:2, :]
        turned_ref[1, pl.ds(block, 1), :] = turned[2:3, :]
        for page, rows in enumerate(found):
            table_ref[page, here, :] = before(table_ref[page, here, :]) + rows
        return carry

    prepare, both = binning(
        knots, spacing, few_phase, few_cell, few_info, table_ref,
        cos_ref, sin_ref, stream_ref, basis_ref, bin_ref,
    )
    first, last = ready >> log2(COLLECT), (number + (COLLECT - 1)) >> log2(COLLECT)

    def clear(step, carry):
        at = pl.multiple_of(step * COLLECT * CHANNELS, COLLECT * CHANNELS)
        bin_ref[pl.ds(at, COLLECT * CHANNELS), :] = jnp.zeros((COLLECT * CHANNELS, LANES), jnp.float32)
        return carry

    gather_block(0, 0)
    prepare(first)

    @pl.when(blocks > 1)
    def _():
        lax.fori_loop(1, blocks, gather_block, 0)
        lax.fori_loop(last, (blocks * BLOCK + (COLLECT - 1)) >> log2(COLLECT), clear, 0)
        prepare(first)

    lax.fori_loop(first, last, both, 0)

    def merge(block, carry):
        at = aligned(block * BLOCK, 16)
        names = few_info[pl.ds(at, BLOCK), 2:3]

        def add(other, carry):
            there = aligned(other * BLOCK, 16)
            same = (names == turned_ref[1, pl.ds(other, 1), :]).astype(jnp.bfloat16)
            for c in range(CHANNELS):
                binned = bin_ref[pl.ds(there * CHANNELS + c, BLOCK, stride=CHANNELS), :]
                high = binned.astype(jnp.bfloat16)
                if c == COUNT:
                    share = dot(same, high)
                else:
                    low = (binned - high.astype(jnp.float32)).astype(jnp.bfloat16)
                    share = dot(same, jnp.concatenate([high, low], axis=1))
                    share = share[:, :LANES] + share[:, LANES:]
                if not isinstance(other, int):
                    share = share + total_ref[c, pl.ds(at, BLOCK), :]
                total_ref[c, pl.ds(at, BLOCK), :] = share
            return carry

        add(0, 0)
        if not isinstance(block, int):
            lax.fori_loop(1, blocks, add, 0)
        return carry

    def project(at, size):
        here = pl.ds(aligned(at, 16), size)
        signal, signal_cos, signal_sin, count, cos_sum, sin_sum, cos_cos, cos_sin_sum = (
            total_ref[c, here, :] for c in range(CHANNELS)
        )
        sin_sin = count - cos_cos
        stokes_i = count + MAP_PRIOR
        stokes_q = cos_cos + MAP_PRIOR
        stokes_u = sin_sin + MAP_PRIOR
        minor_one = stokes_q * stokes_u - cos_sin_sum * cos_sin_sum
        minor_two = sin_sum * cos_sin_sum - cos_sum * stokes_u
        minor_three = cos_sum * cos_sin_sum - sin_sum * stokes_q
        minor_four = stokes_i * stokes_u - sin_sum * sin_sum
        minor_five = cos_sum * sin_sum - stokes_i * cos_sin_sum
        minor_six = stokes_i * stokes_q - cos_sum * cos_sum
        determinant = stokes_i * minor_one + cos_sum * minor_two + sin_sum * minor_three
        scale = 1.0 / determinant
        map_i = (minor_one * signal + minor_two * signal_cos + minor_three * signal_sin) * scale
        map_q = (minor_two * signal + minor_four * signal_cos + minor_five * signal_sin) * scale
        map_u = (minor_three * signal + minor_five * signal_cos + minor_six * signal_sin) * scale
        cell = few_cell[here, :].astype(jnp.int32)
        projected = (
            lane_gather(map_i, cell) + cos_ref[here, :] * lane_gather(map_q, cell)
        ) + sin_ref[here, :] * lane_gather(map_u, cell)
        cleaned = stream_ref[here, :] - projected
        valid = few_info[here, 1:2] > 0.5
        base = few_info[here, 0:1].astype(jnp.int32) >> log2(spacing)
        lane = iota((size, LANES), 1)
        pages = [jnp.zeros((size, LANES), jnp.float32) for _ in range(knots_ref.shape[0])]
        for term in range(5):
            value = basis_ref[term, here, :] * cleaned
            high = value.astype(jnp.bfloat16)
            low = (value - high.astype(jnp.float32)).astype(jnp.bfloat16)
            value = dot(jnp.concatenate([high, low], axis=1), jnp.ones((2 * LANES, LANES), jnp.bfloat16))
            knot = (base + (term - 1)) & (knots - 1)
            for page in range(len(pages)):
                pages[page] = pages[page] + jnp.where(lane + page * LANES == knot, value, 0.0)
        for page, sums in enumerate(pages):
            knots_ref[page, here, :] = jnp.where(valid, sums, 0.0)

    def image_of(block, sums):
        at = aligned(block * BLOCK, 16)
        for first in range(0, BLOCK, PROJECT):
            project(at + first, min(PROJECT, BLOCK - first))
        det = (iota((2 * dets, BLOCK), 0) + 1).astype(jnp.float32)
        chosen = (turned_ref[0, pl.ds(block, 1), :] == det).astype(jnp.bfloat16)
        return tuple(
            total + exact_dot(chosen, knots_ref[page, pl.ds(at, BLOCK), :]) for page, total in enumerate(sums)
        )

    def write(image):
        partial = jnp.concatenate(flatten(image, knots), axis=0)
        for target in range(out_ref.shape[0] // (2 * packed)):
            out_ref[target * 2 * packed : (target + 1) * 2 * packed, :] = partial

    zero = tuple(jnp.zeros((2 * dets, LANES), jnp.float32) for _ in range(knots_ref.shape[0]))
    merge(0, 0)
    write(image_of(0, zero))

    @pl.when(blocks > 1)
    def _():
        lax.fori_loop(0, blocks, merge, 0)
        write(lax.fori_loop(0, blocks, image_of, zero))

    coeffs_copy.wait()


def finish_kernel(
    ranks, spacing, arrived_ref, packs_ref, coeffs_ref, new_offset_ref, new_left_ref, new_search_ref,
):
    nodes, dets = coeffs_ref.shape
    height = packs_ref.shape[1]
    step = max(height, 8)
    parts = [arrived_ref[r : r + step, :] for r in range(0, arrived_ref.shape[0], step)]
    while len(parts) > 1:
        parts = [a + b for a, b in zip(parts[0::2], parts[1::2], strict=True)]
    total = sum((parts[0][r : r + height, :] for r in range(height, step, height)), parts[0][:height, :])
    search, left = packs_ref[0], packs_ref[1]
    image = total * (1.0 / spacing) + BASE_PRIOR * search
    norm_old = jnp.sum(left * left, keepdims=True)
    stride_factor = norm_old / jnp.sum(search * image, keepdims=True)
    fresh = left - stride_factor * image
    beta = jnp.sum(fresh * fresh, keepdims=True) / norm_old
    span, group = lax.axis_index("tm"), lax.axis_index("det")
    lines = height // 2
    knots = lines * LANES // dets
    place = (iota((8, LANES), 1) & (dets - 1)) * knots + span * nodes + (iota((8, LANES), 0) & (nodes - 1))

    def own(x):
        x = jnp.where(group == 0, x[:lines, :], x[lines:, :])
        found = jnp.zeros((8, LANES), jnp.float32)
        for p in range(lines):
            values = lane_gather(jnp.broadcast_to(x[p : p + 1, :], (8, LANES)), place & (LANES - 1))
            found = jnp.where((place >> log2(LANES)) == p, values, found)
        return found[:nodes, :dets]

    my_search = own(search)
    my_left = own(fresh)
    new_offset_ref[...] = coeffs_ref[...] + stride_factor * my_search
    new_left_ref[...] = my_left
    new_search_ref[...] = my_left + beta * my_search


def body(
    offset_coeffs,
    leftover_error,
    search_vector,
    node_lattice_offset,
    sky_cell_in_patch,
    analyser_reading_phase,
    segment_sky_patch,
):
    ranks, groups = lax.axis_size("tm"), lax.axis_size("det")
    dets, samples = analyser_reading_phase.shape
    nodes = search_vector.shape[1]
    spacing = samples // nodes
    blocks = segment_sky_patch.size
    cap = max(2, 2 * blocks // ranks)
    slots = ranks * cap
    rows = 2 * cap + 1
    height = groups * ranks * nodes * dets // LANES
    vmem = pl.BlockSpec(memory_space=pltpu.VMEM)
    hbm = pl.BlockSpec(memory_space=pltpu.HBM)
    pin = functools.partial(pltpu.with_memory_space_constraint, memory_space=pltpu.HBM)
    params = pltpu.CompilerParams(vmem_limit_bytes=VMEM_BYTES)
    inputs = (
        segment_sky_patch, node_lattice_offset.reshape(1, dets), search_vector.T, leftover_error.T,
        sky_cell_in_patch, analyser_reading_phase,
    )
    small = jax.ShapeDtypeStruct((nodes, dets), jnp.float32)

    outgoing = pl.pallas_call(
        functools.partial(send_kernel, ranks, cap),
        out_shape=jax.ShapeDtypeStruct((ranks * rows, LANES), jnp.float32),
        in_specs=[hbm] * len(inputs),
        out_specs=vmem,
        scratch_shapes=[pltpu.VMEM(x.shape, x.dtype) for x in inputs]
        + [pltpu.SemaphoreType.DMA((len(inputs),))],
        compiler_params=params,
        name="send",
    )(*[pin(x) for x in inputs])
    arrived = lax.all_to_all(
        outgoing.reshape(ranks, 1, rows * LANES), "tm", split_axis=0, concat_axis=0, tiled=True
    )
    swap = [(i, groups - 1 - i) for i in range(groups)]
    other = lax.ppermute(arrived, "det", swap)
    pages = max(1, ranks * nodes // LANES)
    f32 = jnp.float32
    room = pl.cdiv(2 * slots, BLOCK) * BLOCK + max(COLLECT, PROJECT)
    few = jax.ShapeDtypeStruct((room, LANES), f32)
    shared = (
        few, few, few, jax.ShapeDtypeStruct((pages, room, LANES), f32), few, few, few,
        jax.ShapeDtypeStruct((5, room, LANES), f32),
        jax.ShapeDtypeStruct((room * CHANNELS, LANES), f32),
    )
    sizes = (ranks, cap, dets, nodes, spacing)
    *state, packs, count = pl.pallas_call(
        functools.partial(own_kernel, *sizes),
        out_shape=shared + (
            jax.ShapeDtypeStruct((2 * height // groups, LANES), f32),
            jax.ShapeDtypeStruct((8, LANES), jnp.int32),
        ),
        in_specs=[vmem],
        out_specs=(vmem,) * 11,
        compiler_params=params,
        cost_estimate=pl.CostEstimate(flops=4_000_000_000, bytes_accessed=4_000_000, transcendentals=0),
        name="own",
    )(arrived.reshape(ranks * rows, LANES))
    *_, partials, packs, coeffs = pl.pallas_call(
        functools.partial(main_kernel, *sizes),
        out_shape=shared + (
            jax.ShapeDtypeStruct((ranks * groups * height, LANES), f32),
            jax.ShapeDtypeStruct((2, height, LANES), f32),
            small,
        ),
        in_specs=[vmem, hbm] + [vmem] * 11,
        out_specs=(vmem,) * 12,
        scratch_shapes=[
            pltpu.VMEM((CHANNELS, room, LANES), f32),
            pltpu.VMEM((2, 8, BLOCK), f32),
            pltpu.VMEM((pages, room, LANES), f32),
            pltpu.SemaphoreType.DMA((1,)),
        ],
        input_output_aliases={4 + k: k for k in range(9)},
        compiler_params=params,
        name="main",
    )(other.reshape(ranks * rows, LANES), pin(offset_coeffs.T), packs, count, *state)
    gathered = lax.all_to_all(
        partials.reshape(ranks * groups, 1, height * LANES),
        ("tm", "det"), split_axis=0, concat_axis=0, tiled=True,
    )
    results = pl.pallas_call(
        functools.partial(finish_kernel, ranks, spacing),
        out_shape=(small, small, small),
        in_specs=[vmem] * 3,
        out_specs=(vmem, vmem, vmem),
        compiler_params=params,
        name="finish",
    )(gathered.reshape(ranks * groups * height, LANES), packs, coeffs)
    return tuple(result.T for result in results)


def solution(mesh):
    return jax.shard_map(
        body,
        mesh=mesh,
        in_specs=(
            P("det", "tm"),
            P("det", "tm"),
            P("det", "tm"),
            P("det"),
            P("det", "tm"),
            P("det", "tm"),
            P("det", "tm"),
        ),
        out_specs=(P("det", "tm"), P("det", "tm"), P("det", "tm")),
        check_vma=False,
    )
```

```python
import functools

import jax
import jax.numpy as jnp
from jax import lax
from jax.experimental import pallas as pl
from jax.experimental.pallas import tpu as pltpu
from jax.sharding import PartitionSpec as P

PIX_OWN = 131072
MAP_PRIOR = 1.0
BASE_PRIOR = 0.1
LANES = 128
OWNER_TILES = PIX_OWN // LANES
CHANNELS = 8
COUNT = 3
BLOCK = 176
COLLECT = 32
PROJECT = 64
VMEM_BYTES = 32 * 1024 * 1024

SIN_TERMS = (1.0, -1.0 / 6, 1.0 / 120, -1.0 / 5040, 1.0 / 362880, -1.0 / 39916800, 1.0 / 6227020800)
COS_TERMS = (1.0, -0.5, 1.0 / 24, -1.0 / 720, 1.0 / 40320, -1.0 / 3628800, 1.0 / 479001600, -1.0 / 87178291200)
PI_PARTS = (3.140625, 0.0009670257568359375, 6.2771141529083252e-07)


def iota(shape, dim):
    return lax.broadcasted_iota(jnp.int32, shape, dim)


def log2(number):
    assert number & (number - 1) == 0
    return number.bit_length() - 1


def split3(x):
    high = x.astype(jnp.bfloat16)
    rest = x - high.astype(jnp.float32)
    middle = rest.astype(jnp.bfloat16)
    low = (rest - middle.astype(jnp.float32)).astype(jnp.bfloat16)
    return high, middle, low


def dot(a, b):
    return jnp.dot(a, b, preferred_element_type=jnp.float32)


def exact_dot(selector, x):
    high, middle, low = split3(x)
    width = x.shape[1]
    parts = dot(selector, jnp.concatenate([high, middle, low], axis=1))
    return (parts[:, :width] + parts[:, width : 2 * width]) + parts[:, 2 * width :]


def horner(x, terms):
    total = jnp.full_like(x, terms[-1])
    for term in terms[-2::-1]:
        total = total * x + term
    return total


def cos_sin(angle):
    turns = jnp.round(angle * (1.0 / 3.14159265358979))
    rest = angle - turns * PI_PARTS[0]
    rest = rest - turns * PI_PARTS[1]
    rest = rest - turns * PI_PARTS[2]
    half = turns * 0.5
    sign = 1.0 - 4.0 * (half - jnp.floor(half))
    square = rest * rest
    cosine = sign * horner(square, COS_TERMS)
    sine = sign * rest * horner(square, SIN_TERMS)
    return cosine, sine


def spline_weights(fraction):
    square = fraction * fraction
    cube = square * fraction
    rest = 1.0 - fraction
    first = rest * rest * rest * (1.0 / 6.0)
    second = (3.0 * cube - 6.0 * square + 4.0) * (1.0 / 6.0)
    third = (-3.0 * cube + 3.0 * square + 3.0 * fraction + 1.0) * (1.0 / 6.0)
    fourth = cube * (1.0 / 6.0)
    return (first, second, third, fourth)


def aligned(index, unit):
    return index if isinstance(index, int) else pl.multiple_of(index, unit)


def lane_gather(table, index):
    return jnp.take_along_axis(table, index, axis=1, mode="promise_in_bounds")


def send_kernel(
    ranks, cap, patch_hbm, offset_hbm, search_hbm, left_hbm, cell_hbm, phase_hbm, out_ref,
    patch_ref, offset_ref, search_ref, left_ref, cell_ref, phase_ref, sems,
):
    pairs = (
        (patch_hbm, patch_ref), (offset_hbm, offset_ref), (search_hbm, search_ref),
        (left_hbm, left_ref), (cell_hbm, cell_ref), (phase_hbm, phase_ref),
    )
    copies = [pltpu.make_async_copy(src, dst, sems.at[k]) for k, (src, dst) in enumerate(pairs)]
    for copy in copies:
        copy.start()
    copies[0].wait()
    dets, columns = patch_ref.shape
    blocks = dets * columns
    samples = phase_ref.shape[1]
    nodes = search_ref.shape[0]
    span = lax.axis_index("tm")
    rows = 2 * cap + 1
    square = (blocks, blocks)
    tiles = jnp.concatenate(
        [jnp.broadcast_to(patch_ref[:, c : c + 1], (dets, LANES)) for c in range(columns)], axis=0
    )
    owner = (tiles >> log2(OWNER_TILES)).astype(jnp.float32)
    owner_t = owner.T
    same = owner == owner_t
    here, there = iota(square, 0), iota(square, 1)
    rank_row = jnp.sum(jnp.where(same & (here < there), 1.0, 0.0), axis=0, keepdims=True)
    rank_col = jnp.sum(jnp.where(same & (there < here), 1.0, 0.0), axis=1, keepdims=True)
    slot_row = (owner_t[0:1, :] * cap + rank_row).astype(jnp.int32)
    place = (iota((ranks * cap, blocks), 0) == slot_row).astype(jnp.bfloat16)
    for copy in copies[1:]:
        copy.wait()
    cells = jnp.concatenate([cell_ref[:, c * LANES : (c + 1) * LANES] for c in range(columns)], axis=0)
    pixels = (tiles * LANES + cells).astype(jnp.float32)
    phases = jnp.concatenate([phase_ref[:, c * LANES : (c + 1) * LANES] for c in range(columns)], axis=0)
    moved = exact_dot(place, jnp.concatenate([phases, pixels], axis=1))
    slot_phase, slot_pixel = moved[:, :LANES], moved[:, LANES:]
    lane = iota(square, 1)
    small = iota((dets, LANES), 1)
    det_lane = iota((dets, LANES), 0)
    offsets = jnp.broadcast_to(offset_ref[...], (dets, dets))
    diagonal = iota((dets, dets), 0) == iota((dets, dets), 1)
    shift = jnp.sum(jnp.where(diagonal, offsets, 0).astype(jnp.float32), axis=1, keepdims=True)
    shift = jnp.broadcast_to(shift.astype(jnp.int32), (dets, LANES))
    start = jnp.concatenate([c * LANES - shift for c in range(columns)], axis=0) + span * samples
    which = (iota(square, 0) & (dets - 1)) + 1
    rank = rank_col.astype(jnp.int32)
    listing = jnp.where(lane == rank, start, 0) + jnp.where(lane == rank + cap, which, 0)
    listing = listing + jnp.where(lane == rank + 2 * cap, tiles + 1, 0)
    chosen = (iota((ranks, blocks), 0).astype(jnp.float32) == owner_t[0:1, :]).astype(jnp.bfloat16)
    info = exact_dot(chosen, listing.astype(jnp.float32))
    knots = jnp.zeros((1, LANES), jnp.float32)
    for kind, ref in enumerate((search_ref, left_ref)):
        for n in range(nodes):
            column = jnp.broadcast_to(ref[n : n + 1, :], (dets, dets))
            column = jnp.sum(jnp.where(diagonal, column, 0.0), axis=1, keepdims=True)
            at = (3 * cap + kind * dets * nodes + n) + det_lane * nodes
            knots = knots + jnp.sum(jnp.where(small == at, column, 0.0), axis=0, keepdims=True)
    info = info + knots
    for o in range(ranks):
        out_ref[o * rows : o * rows + cap, :] = slot_phase[o * cap : (o + 1) * cap, :]
        out_ref[o * rows + cap : o * rows + 2 * cap, :] = slot_pixel[o * cap : (o + 1) * cap, :]
        out_ref[o * rows + 2 * cap : (o + 1) * rows, :] = info[o : o + 1, :]


def unpack(ranks, cap, ref):
    rows = 2 * cap + 1
    starts = range(0, ranks * rows, rows)
    phase = jnp.concatenate([ref[s : s + cap, :] for s in starts], axis=0)
    pixel = jnp.concatenate([ref[s + cap : s + 2 * cap, :] for s in starts], axis=0)
    lines = [ref[s + 2 * cap : s + rows, :] for s in starts]
    info = jnp.concatenate([jnp.broadcast_to(line, (cap, LANES)) for line in lines], axis=0)
    return phase, pixel, info, jnp.concatenate(lines, axis=0)


def rank_slots(ranks, cap, meta):
    lists = []
    spans = LANES // cap
    for k in range(ranks * cap // LANES):
        names = meta[k * spans : (k + 1) * spans, :]
        lane = iota((spans, LANES), 1)
        spread = lane_gather(names, 2 * cap + (lane & (cap - 1)))
        mine = (lane >> log2(cap)) == iota((spans, LANES), 0)
        lists.append(jnp.sum(jnp.where(mine, spread, 0.0), axis=0, keepdims=True))
    names = jnp.concatenate(lists, axis=0).astype(jnp.int32)
    mine = (names > 0) & (((names - 1) & 1) == lax.axis_index("det"))
    ones = jnp.where(mine, 1.0, 0.0)
    earlier = (iota((LANES, LANES), 0) < iota((LANES, LANES), 1)).astype(jnp.bfloat16)
    rank = dot(ones.astype(jnp.bfloat16), earlier)
    sums = jnp.sum(ones, axis=1, keepdims=True)
    before = [jnp.zeros((1, 1), jnp.float32)]
    for k in range(len(lists)):
        before.append(before[-1] + sums[k : k + 1, :])
    rank = rank + jnp.concatenate(before[:-1], axis=0)
    return jnp.where(mine, rank, -1.0).astype(jnp.int32), jnp.sum(ones).astype(jnp.int32)


def flatten(pages, knots):
    dets = pages[0].shape[0]
    if knots >= LANES:
        return [page[d : d + 1, :] for d in range(dets) for page in pages]
    lane, det = iota((dets, LANES), 1), iota((dets, LANES), 0)
    spread = lane_gather(pages[0], lane & (knots - 1))
    per_row = LANES // knots
    mine = (det & (per_row - 1)) == (lane >> log2(knots))
    spread = jnp.where(mine, spread, 0.0)
    rows = []
    for first in range(0, dets, per_row):
        rows.append(jnp.sum(spread[first : first + per_row, :], axis=0, keepdims=True))
    return rows


def read_knots(ranks, cap, dets, nodes, meta):
    width = dets * nodes
    knots = ranks * nodes
    per_row = LANES // width
    kinds = []
    for kind in range(2):
        lines = []
        for p in range(ranks // per_row):
            names = meta[p * per_row : (p + 1) * per_row, :]
            lane = iota((per_row, LANES), 1)
            spread = lane_gather(names, (3 * cap + kind * width) + (lane & (width - 1)))
            here = (lane >> log2(width)) == iota((per_row, LANES), 0)
            lines.append(jnp.sum(jnp.where(here, spread, 0.0), axis=0, keepdims=True))
        lane = iota((dets, LANES), 1)
        tables = []
        for page in range(max(1, knots // LANES)):
            knot = lane + page * LANES
            index = ((knot >> log2(nodes)) & (per_row - 1)) * width
            index = index + iota((dets, LANES), 0) * nodes + (knot & (nodes - 1))
            table = jnp.zeros((dets, LANES), jnp.float32)
            for p, line in enumerate(lines):
                values = lane_gather(jnp.broadcast_to(line, (dets, LANES)), index)
                table = jnp.where((knot >> log2(per_row * nodes)) == p, values, table)
            tables.append(table)
        kinds.append(tables)
    return kinds


def source_of(ranks, cap, dets, total, side, phase, pixel, info):
    slots = ranks * cap
    slot = iota((slots, LANES), 0) & (cap - 1)
    lane = iota((slots, LANES), 1)
    listed = lane_gather(info, jnp.minimum(lane, 2) * cap + slot)
    listed = listed + jnp.where(lane == 1, (side * dets).astype(jnp.float32), 0.0)
    cell = (pixel - jnp.floor(pixel * (1.0 / LANES)) * LANES).astype(jnp.bfloat16)
    whole = split3(listed)
    if max(total, ranks * OWNER_TILES) <= 65536:
        whole = whole[:2]
    return jnp.concatenate(split3(phase) + (cell,) + whole, axis=1)


def take_slots(at, rank, source, dets, side, tables):
    down = iota((BLOCK, LANES), 0) + at
    place = jnp.concatenate(
        [(down == rank[k : k + 1, :]).astype(jnp.bfloat16) for k in range(rank.shape[0])], axis=1
    )
    taken = dot(place, source)
    parts = [taken[:, k * LANES : (k + 1) * LANES] for k in range(taken.shape[1] // LANES)]
    phase = (parts[0] + parts[1]) + parts[2]
    info = sum(parts[5:], parts[4])
    lane = iota((BLOCK, LANES), 1) + (1 + side * dets)
    chosen = ((info[:, 1:2] == lane.astype(jnp.float32)) & (iota((BLOCK, LANES), 1) < dets)).astype(jnp.bfloat16)
    empty = jnp.zeros((LANES - dets, LANES), jnp.float32)
    knots = [exact_dot(chosen, jnp.concatenate([table, empty], axis=0)) for table in tables]
    return phase, parts[3], info, knots


def spline(info_ref, spacing, at, chunk):
    start = jnp.broadcast_to(info_ref[pl.ds(at, chunk), 0:1], (chunk, LANES)).astype(jnp.int32)
    time = start + iota((chunk, LANES), 1)
    interval = time >> log2(spacing)
    fraction = (time & (spacing - 1)).astype(jnp.float32) * (1.0 / spacing)
    return start >> log2(spacing), interval, spline_weights(fraction)


def five_weights(early, weights):
    padded = (0.0,) + weights + (0.0,)
    return [jnp.where(early, padded[term + 1], padded[term]) for term in range(5)]


def binning(knots, spacing, few_phase, few_cell, few_info, table_ref, cos_ref, sin_ref, stream_ref, basis_ref, bin_ref):
    pages = table_ref.shape[0]

    def prepare(step):
        at = aligned(step * COLLECT, COLLECT)
        cosine, sine = cos_sin(2.0 * few_phase[pl.ds(at, COLLECT), :])
        base, interval, weights = spline(few_info, spacing, at, COLLECT)
        for term, weight in enumerate(five_weights(interval == base, weights)):
            basis_ref[term, pl.ds(at, COLLECT), :] = weight
        stream = jnp.zeros((COLLECT, LANES), jnp.float32)
        for term in range(4):
            knot = (interval + (term - 1)) & (knots - 1)
            value = lane_gather(table_ref[0, pl.ds(at, COLLECT), :], knot & (LANES - 1))
            for page in range(1, pages):
                more = lane_gather(table_ref[page, pl.ds(at, COLLECT), :], knot & (LANES - 1))
                value = jnp.where((knot >> log2(LANES)) == page, more, value)
            stream = stream + weights[term] * value
        cos_ref[pl.ds(at, COLLECT), :] = cosine
        sin_ref[pl.ds(at, COLLECT), :] = sine
        stream_ref[pl.ds(at, COLLECT), :] = stream

    down = iota((LANES, LANES), 0).astype(jnp.float32).astype(jnp.bfloat16)
    channel = iota((CHANNELS, LANES), 0)

    def collect(step):
        for k in range(COLLECT // 2):
            at = step * COLLECT + 2 * k
            pieces, cells = [], []
            for slot in (at, at + 1):
                stream = jnp.broadcast_to(stream_ref[pl.ds(slot, 1), :], (CHANNELS, LANES))
                cosine = jnp.broadcast_to(cos_ref[pl.ds(slot, 1), :], (CHANNELS, LANES))
                sine = jnp.broadcast_to(sin_ref[pl.ds(slot, 1), :], (CHANNELS, LANES))
                left = jnp.where(channel < 3, stream, jnp.where(channel < 6, 1.0, cosine))
                is_one = (channel == 0) | (channel == 3)
                is_sine = (channel == 2) | (channel == 5) | (channel == 7)
                right = jnp.where(is_one, 1.0, jnp.where(is_sine, sine, cosine))
                entry = left * right
                high = entry.astype(jnp.bfloat16).astype(jnp.float32)
                rest = entry - high
                stack = jnp.concatenate([high, rest], axis=0)
                pieces.append(stack.astype(jnp.bfloat16))
                cells.append(jnp.broadcast_to(few_cell[pl.ds(slot, 1), :].astype(jnp.bfloat16), (LANES, LANES)))
            hits = [jnp.where(cell == down, jnp.int8(1), jnp.int8(0)).T.astype(jnp.bfloat16) for cell in cells]
            sums = dot(jnp.concatenate(pieces, axis=0), jnp.concatenate(hits, axis=1))
            for m in range(2):
                base = 2 * CHANNELS * m
                mine = sums[base : base + 2 * CHANNELS, m * LANES : (m + 1) * LANES]
                bin_ref[pl.ds((at + m) * CHANNELS, CHANNELS), :] = mine[:CHANNELS] + mine[CHANNELS:]

    def both(step, carry):
        collect(step)
        prepare(step + 1)
        return carry

    return prepare, both


def own_kernel(
    ranks, cap, dets, nodes, spacing, own_ref,
    few_phase, few_cell, few_info, table_ref, cos_ref, sin_ref, stream_ref, basis_ref, bin_ref, packs_ref, count_ref,
):
    knots = ranks * nodes
    side = lax.axis_index("det")
    phase, pixel, info, meta = unpack(ranks, cap, own_ref)
    rank, number = rank_slots(ranks, cap, meta)
    count_ref[...] = jnp.full((8, LANES), number, jnp.int32)
    tables, left = read_knots(ranks, cap, dets, nodes, meta)
    packs_ref[...] = jnp.concatenate(flatten(tables, knots) + flatten(left, knots), axis=0)
    source = source_of(ranks, cap, dets, knots * spacing, side, phase, pixel, info)

    def gather_block(block, carry):
        here = pl.ds(aligned(block * BLOCK, 16), BLOCK)
        few_phase[here, :], few_cell[here, :], few_info[here, :], found = take_slots(
            block * BLOCK, rank, source, dets, side, tables
        )
        for page, rows in enumerate(found):
            table_ref[page, here, :] = rows
        return carry

    prepare, both = binning(
        knots, spacing, few_phase, few_cell, few_info, table_ref,
        cos_ref, sin_ref, stream_ref, basis_ref, bin_ref,
    )
    gather_block(0, 0)
    prepare(0)
    room = pl.cdiv(BLOCK, COLLECT) * COLLECT * CHANNELS
    bin_ref[0:room, :] = jnp.zeros((room, LANES), jnp.float32)
    lax.fori_loop(1, block_count(number, ranks * cap), gather_block, 0)
    lax.fori_loop(0, number >> log2(COLLECT), both, 0)


def block_count(number, most):
    return sum(jnp.where(number > start, 1, 0) for start in range(0, most, BLOCK))


def main_kernel(
    ranks, cap, dets, nodes, spacing, other_ref, coeffs_hbm, packs_own, count_ref, *refs,
):
    few_phase, few_cell, few_info, table_ref, cos_ref, sin_ref, stream_ref, basis_ref, bin_ref = refs[9:18]
    out_ref, packs_ref, coeffs_ref = refs[18:21]
    total_ref, turned_ref, knots_ref, sems = refs[21:]
    coeffs_copy = pltpu.make_async_copy(coeffs_hbm, coeffs_ref, sems.at[0])
    coeffs_copy.start()
    slots = ranks * cap
    knots = ranks * nodes
    packed = knots * dets // LANES
    group = lax.axis_index("det")
    side = 1 - group

    phase, pixel, info, meta = unpack(ranks, cap, other_ref)
    rank, more = rank_slots(ranks, cap, meta)
    ready = jnp.max(count_ref[...])
    rank = jnp.where(rank >= 0, rank + ready, -1)
    number = ready + more
    tables, left = read_knots(ranks, cap, dets, nodes, meta)
    for kind, pages in enumerate((tables, left)):
        here = slice(kind * packed, (kind + 1) * packed)
        packs_ref[kind, pl.ds(group * packed, packed), :] = packs_own[here, :]
        packs_ref[kind, pl.ds(side * packed, packed), :] = jnp.concatenate(flatten(pages, knots), axis=0)
    source = source_of(ranks, cap, dets, knots * spacing, side, phase, pixel, info)
    blocks = block_count(number, 2 * slots)
    ready_blocks = block_count(ready, slots)

    def gather_block(block, carry):
        here = pl.ds(aligned(block * BLOCK, 16), BLOCK)
        def before(rows):
            return rows if isinstance(block, int) else jnp.where(block < ready_blocks, rows, 0.0)

        phase, cell, info, found = take_slots(block * BLOCK, rank, source, dets, side, tables)
        few_phase[here, :] = before(few_phase[here, :]) + phase
        few_cell[here, :] = before(few_cell[here, :]) + cell
        info = before(few_info[here, :]) + info
        few_info[here, :] = info
        turned = info.T
        turned_ref[0, pl.ds(block, 1), :] = turned[1:2, :]
        turned_ref[1, pl.ds(block, 1), :] = turned[2:3, :]
        for page, rows in enumerate(found):
            table_ref[page, here, :] = before(table_ref[page, here, :]) + rows
        return carry

    prepare, both = binning(
        knots, spacing, few_phase, few_cell, few_info, table_ref,
        cos_ref, sin_ref, stream_ref, basis_ref, bin_ref,
    )
    first, last = ready >> log2(COLLECT), (number + (COLLECT - 1)) >> log2(COLLECT)

    def clear(step, carry):
        at = pl.multiple_of(step * COLLECT * CHANNELS, COLLECT * CHANNELS)
        bin_ref[pl.ds(at, COLLECT * CHANNELS), :] = jnp.zeros((COLLECT * CHANNELS, LANES), jnp.float32)
        return carry

    gather_block(0, 0)
    prepare(first)

    @pl.when(blocks > 1)
    def _():
        lax.fori_loop(1, blocks, gather_block, 0)
        lax.fori_loop(last, (blocks * BLOCK + (COLLECT - 1)) >> log2(COLLECT), clear, 0)
        prepare(first)

    lax.fori_loop(first, last, both, 0)

    def merge(block, carry):
        at = aligned(block * BLOCK, 16)
        names = few_info[pl.ds(at, BLOCK), 2:3]

        def add(other, carry):
            there = aligned(other * BLOCK, 16)
            same = (names == turned_ref[1, pl.ds(other, 1), :]).astype(jnp.bfloat16)
            for c in range(CHANNELS):
                binned = bin_ref[pl.ds(there * CHANNELS + c, BLOCK, stride=CHANNELS), :]
                high = binned.astype(jnp.bfloat16)
                if c == COUNT:
                    share = dot(same, high)
                else:
                    low = (binned - high.astype(jnp.float32)).astype(jnp.bfloat16)
                    share = dot(same, jnp.concatenate([high, low], axis=1))
                    share = share[:, :LANES] + share[:, LANES:]
                if not isinstance(other, int):
                    share = share + total_ref[c, pl.ds(at, BLOCK), :]
                total_ref[c, pl.ds(at, BLOCK), :] = share
            return carry

        add(0, 0)
        if not isinstance(block, int):
            lax.fori_loop(1, blocks, add, 0)
        return carry

    def project(at, size):
        here = pl.ds(aligned(at, 16), size)
        signal, signal_cos, signal_sin, count, cos_sum, sin_sum, cos_cos, cos_sin_sum = (
            total_ref[c, here, :] for c in range(CHANNELS)
        )
        sin_sin = count - cos_cos
        stokes_i = count + MAP_PRIOR
        stokes_q = cos_cos + MAP_PRIOR
        stokes_u = sin_sin + MAP_PRIOR
        minor_one = stokes_q * stokes_u - cos_sin_sum * cos_sin_sum
        minor_two = sin_sum * cos_sin_sum - cos_sum * stokes_u
        minor_three = cos_sum * cos_sin_sum - sin_sum * stokes_q
        minor_four = stokes_i * stokes_u - sin_sum * sin_sum
        minor_five = cos_sum * sin_sum - stokes_i * cos_sin_sum
        minor_six = stokes_i * stokes_q - cos_sum * cos_sum
        determinant = stokes_i * minor_one + cos_sum * minor_two + sin_sum * minor_three
        scale = 1.0 / determinant
        map_i = (minor_one * signal + minor_two * signal_cos + minor_three * signal_sin) * scale
        map_q = (minor_two * signal + minor_four * signal_cos + minor_five * signal_sin) * scale
        map_u = (minor_three * signal + minor_five * signal_cos + minor_six * signal_sin) * scale
        cell = few_cell[here, :].astype(jnp.int32)
        projected = (
            lane_gather(map_i, cell) + cos_ref[here, :] * lane_gather(map_q, cell)
        ) + sin_ref[here, :] * lane_gather(map_u, cell)
        cleaned = stream_ref[here, :] - projected
        valid = few_info[here, 1:2] > 0.5
        base = few_info[here, 0:1].astype(jnp.int32) >> log2(spacing)
        lane = iota((size, LANES), 1)
        pages = [jnp.zeros((size, LANES), jnp.float32) for _ in range(knots_ref.shape[0])]
        for term in range(5):
            value = basis_ref[term, here, :] * cleaned
            high = value.astype(jnp.bfloat16)
            low = (value - high.astype(jnp.float32)).astype(jnp.bfloat16)
            value = dot(jnp.concatenate([high, low], axis=1), jnp.ones((2 * LANES, LANES), jnp.bfloat16))
            knot = (base + (term - 1)) & (knots - 1)
            for page in range(len(pages)):
                pages[page] = pages[page] + jnp.where(lane + page * LANES == knot, value, 0.0)
        for page, sums in enumerate(pages):
            knots_ref[page, here, :] = jnp.where(valid, sums, 0.0)

    def image_of(block, sums):
        at = aligned(block * BLOCK, 16)
        for first in range(0, BLOCK, PROJECT):
            project(at + first, min(PROJECT, BLOCK - first))
        det = (iota((2 * dets, BLOCK), 0) + 1).astype(jnp.float32)
        chosen = (turned_ref[0, pl.ds(block, 1), :] == det).astype(jnp.bfloat16)
        return tuple(
            total + exact_dot(chosen, knots_ref[page, pl.ds(at, BLOCK), :]) for page, total in enumerate(sums)
        )

    def write(image):
        partial = jnp.concatenate(flatten(image, knots), axis=0)
        for target in range(out_ref.shape[0] // (2 * packed)):
            out_ref[target * 2 * packed : (target + 1) * 2 * packed, :] = partial

    zero = tuple(jnp.zeros((2 * dets, LANES), jnp.float32) for _ in range(knots_ref.shape[0]))
    merge(0, 0)
    write(image_of(0, zero))

    @pl.when(blocks > 1)
    def _():
        lax.fori_loop(0, blocks, merge, 0)
        write(lax.fori_loop(0, blocks, image_of, zero))

    coeffs_copy.wait()


def finish_kernel(
    ranks, spacing, arrived_ref, packs_ref, coeffs_ref, new_offset_ref, new_left_ref, new_search_ref,
):
    nodes, dets = coeffs_ref.shape
    height = packs_ref.shape[1]
    step = max(height, 8)
    parts = [arrived_ref[r : r + step, :] for r in range(0, arrived_ref.shape[0], step)]
    while len(parts) > 1:
        parts = [a + b for a, b in zip(parts[0::2], parts[1::2], strict=True)]
    total = sum((parts[0][r : r + height, :] for r in range(height, step, height)), parts[0][:height, :])
    search, left = packs_ref[0], packs_ref[1]
    image = total * (1.0 / spacing) + BASE_PRIOR * search
    norm_old = jnp.sum(left * left, keepdims=True)
    stride_factor = norm_old / jnp.sum(search * image, keepdims=True)
    fresh = left - stride_factor * image
    beta = jnp.sum(fresh * fresh, keepdims=True) / norm_old
    span, group = lax.axis_index("tm"), lax.axis_index("det")
    lines = height // 2
    knots = lines * LANES // dets
    place = (iota((8, LANES), 1) & (dets - 1)) * knots + span * nodes + (iota((8, LANES), 0) & (nodes - 1))

    def own(x):
        x = jnp.where(group == 0, x[:lines, :], x[lines:, :])
        found = jnp.zeros((8, LANES), jnp.float32)
        for p in range(lines):
            values = lane_gather(jnp.broadcast_to(x[p : p + 1, :], (8, LANES)), place & (LANES - 1))
            found = jnp.where((place >> log2(LANES)) == p, values, found)
        return found[:nodes, :dets]

    my_search = own(search)
    my_left = own(fresh)
    new_offset_ref[...] = coeffs_ref[...] + stride_factor * my_search
    new_left_ref[...] = my_left
    new_search_ref[...] = my_left + beta * my_search


def body(
    offset_coeffs,
    leftover_error,
    search_vector,
    node_lattice_offset,
    sky_cell_in_patch,
    analyser_reading_phase,
    segment_sky_patch,
):
    ranks, groups = lax.axis_size("tm"), lax.axis_size("det")
    dets, samples = analyser_reading_phase.shape
    nodes = search_vector.shape[1]
    spacing = samples // nodes
    blocks = segment_sky_patch.size
    cap = max(2, 2 * blocks // ranks)
    slots = ranks * cap
    rows = 2 * cap + 1
    height = groups * ranks * nodes * dets // LANES
    vmem = pl.BlockSpec(memory_space=pltpu.VMEM)
    hbm = pl.BlockSpec(memory_space=pltpu.HBM)
    pin = functools.partial(pltpu.with_memory_space_constraint, memory_space=pltpu.HBM)
    params = pltpu.CompilerParams(vmem_limit_bytes=VMEM_BYTES)
    inputs = (
        segment_sky_patch, node_lattice_offset.reshape(1, dets), search_vector.T, leftover_error.T,
        sky_cell_in_patch, analyser_reading_phase,
    )
    small = jax.ShapeDtypeStruct((nodes, dets), jnp.float32)

    outgoing = pl.pallas_call(
        functools.partial(send_kernel, ranks, cap),
        out_shape=jax.ShapeDtypeStruct((ranks * rows, LANES), jnp.float32),
        in_specs=[hbm] * len(inputs),
        out_specs=vmem,
        scratch_shapes=[pltpu.VMEM(x.shape, x.dtype) for x in inputs]
        + [pltpu.SemaphoreType.DMA((len(inputs),))],
        compiler_params=params,
        name="send",
    )(*[pin(x) for x in inputs])
    arrived = lax.all_to_all(
        outgoing.reshape(ranks, 1, rows * LANES), "tm", split_axis=0, concat_axis=0, tiled=True
    )
    swap = [(i, groups - 1 - i) for i in range(groups)]
    other = lax.ppermute(arrived, "det", swap)
    pages = max(1, ranks * nodes // LANES)
    f32 = jnp.float32
    room = pl.cdiv(2 * slots, BLOCK) * BLOCK + max(COLLECT, PROJECT)
    few = jax.ShapeDtypeStruct((room, LANES), f32)
    shared = (
        few, few, few, jax.ShapeDtypeStruct((pages, room, LANES), f32), few, few, few,
        jax.ShapeDtypeStruct((5, room, LANES), f32),
        jax.ShapeDtypeStruct((room * CHANNELS, LANES), f32),
    )
    sizes = (ranks, cap, dets, nodes, spacing)
    *state, packs, count = pl.pallas_call(
        functools.partial(own_kernel, *sizes),
        out_shape=shared + (
            jax.ShapeDtypeStruct((2 * height // groups, LANES), f32),
            jax.ShapeDtypeStruct((8, LANES), jnp.int32),
        ),
        in_specs=[vmem],
        out_specs=(vmem,) * 11,
        compiler_params=params,
        cost_estimate=pl.CostEstimate(flops=4_000_000_000, bytes_accessed=4_000_000, transcendentals=0),
        name="own",
    )(arrived.reshape(ranks * rows, LANES))
    *_, partials, packs, coeffs = pl.pallas_call(
        functools.partial(main_kernel, *sizes),
        out_shape=shared + (
            jax.ShapeDtypeStruct((ranks * groups * height, LANES), f32),
            jax.ShapeDtypeStruct((2, height, LANES), f32),
            small,
        ),
        in_specs=[vmem, hbm] + [vmem] * 11,
        out_specs=(vmem,) * 12,
        scratch_shapes=[
            pltpu.VMEM((CHANNELS, room, LANES), f32),
            pltpu.VMEM((2, 8, BLOCK), f32),
            pltpu.VMEM((pages, room, LANES), f32),
            pltpu.SemaphoreType.DMA((1,)),
        ],
        input_output_aliases={4 + k: k for k in range(9)},
        compiler_params=params,
        name="main",
    )(other.reshape(ranks * rows, LANES), pin(offset_coeffs.T), packs, count, *state)
    gathered = lax.all_to_all(
        partials.reshape(ranks * groups, 1, height * LANES),
        ("tm", "det"), split_axis=0, concat_axis=0, tiled=True,
    )
    results = pl.pallas_call(
        functools.partial(finish_kernel, ranks, spacing),
        out_shape=(small, small, small),
        in_specs=[vmem] * 3,
        out_specs=(vmem, vmem, vmem),
        compiler_params=params,
        name="finish",
    )(gathered.reshape(ranks * groups * height, LANES), packs, coeffs)
    return tuple(result.T for result in results)


def solution(mesh):
    return jax.shard_map(
        body,
        mesh=mesh,
        in_specs=(
            P("det", "tm"),
            P("det", "tm"),
            P("det", "tm"),
            P("det"),
            P("det", "tm"),
            P("det", "tm"),
            P("det", "tm"),
        ),
        out_specs=(P("det", "tm"), P("det", "tm"), P("det", "tm")),
        check_vma=False,
    )
```

```python
import functools

import jax
import jax.numpy as jnp
from jax import lax
from jax.experimental import pallas as pl
from jax.experimental.pallas import tpu as pltpu
from jax.sharding import PartitionSpec as P

PIX_OWN = 131072
MAP_PRIOR = 1.0
BASE_PRIOR = 0.1
LANES = 128
OWNER_TILES = PIX_OWN // LANES
CHANNELS = 8
COUNT = 3
BLOCK = 176
COLLECT = 32
PROJECT = 64
VMEM_BYTES = 32 * 1024 * 1024

SIN_TERMS = (1.0, -1.0 / 6, 1.0 / 120, -1.0 / 5040, 1.0 / 362880, -1.0 / 39916800, 1.0 / 6227020800)
COS_TERMS = (1.0, -0.5, 1.0 / 24, -1.0 / 720, 1.0 / 40320, -1.0 / 3628800, 1.0 / 479001600, -1.0 / 87178291200)
PI_PARTS = (3.140625, 0.0009670257568359375, 6.2771141529083252e-07)


def iota(shape, dim):
    return lax.broadcasted_iota(jnp.int32, shape, dim)


def log2(number):
    assert number & (number - 1) == 0
    return number.bit_length() - 1


def split3(x):
    high = x.astype(jnp.bfloat16)
    rest = x - high.astype(jnp.float32)
    middle = rest.astype(jnp.bfloat16)
    low = (rest - middle.astype(jnp.float32)).astype(jnp.bfloat16)
    return high, middle, low


def dot(a, b):
    return jnp.dot(a, b, preferred_element_type=jnp.float32)


def exact_dot(selector, x):
    high, middle, low = split3(x)
    width = x.shape[1]
    parts = dot(selector, jnp.concatenate([high, middle, low], axis=1))
    return (parts[:, :width] + parts[:, width : 2 * width]) + parts[:, 2 * width :]


def horner(x, terms):
    total = jnp.full_like(x, terms[-1])
    for term in terms[-2::-1]:
        total = total * x + term
    return total


def cos_sin(angle):
    turns = jnp.round(angle * (1.0 / 3.14159265358979))
    rest = angle - turns * PI_PARTS[0]
    rest = rest - turns * PI_PARTS[1]
    rest = rest - turns * PI_PARTS[2]
    half = turns * 0.5
    sign = 1.0 - 4.0 * (half - jnp.floor(half))
    square = rest * rest
    cosine = sign * horner(square, COS_TERMS)
    sine = sign * rest * horner(square, SIN_TERMS)
    return cosine, sine


def spline_weights(fraction):
    square = fraction * fraction
    cube = square * fraction
    rest = 1.0 - fraction
    first = rest * rest * rest * (1.0 / 6.0)
    second = (3.0 * cube - 6.0 * square + 4.0) * (1.0 / 6.0)
    third = (-3.0 * cube + 3.0 * square + 3.0 * fraction + 1.0) * (1.0 / 6.0)
    fourth = cube * (1.0 / 6.0)
    return (first, second, third, fourth)


def aligned(index, unit):
    return index if isinstance(index, int) else pl.multiple_of(index, unit)


def lane_gather(table, index):
    return jnp.take_along_axis(table, index, axis=1, mode="promise_in_bounds")


def send_kernel(
    ranks, cap, patch_hbm, offset_hbm, search_hbm, left_hbm, cell_hbm, phase_hbm, out_ref,
    patch_ref, offset_ref, search_ref, left_ref, cell_ref, phase_ref, sems,
):
    pairs = (
        (patch_hbm, patch_ref), (offset_hbm, offset_ref), (search_hbm, search_ref),
        (left_hbm, left_ref), (cell_hbm, cell_ref), (phase_hbm, phase_ref),
    )
    copies = [pltpu.make_async_copy(src, dst, sems.at[k]) for k, (src, dst) in enumerate(pairs)]
    for copy in copies:
        copy.start()
    copies[0].wait()
    dets, columns = patch_ref.shape
    blocks = dets * columns
    samples = phase_ref.shape[1]
    nodes = search_ref.shape[0]
    span = lax.axis_index("tm")
    rows = 2 * cap + 1
    square = (blocks, blocks)
    tiles = jnp.concatenate(
        [jnp.broadcast_to(patch_ref[:, c : c + 1], (dets, LANES)) for c in range(columns)], axis=0
    )
    owner = (tiles >> log2(OWNER_TILES)).astype(jnp.float32)
    owner_t = owner.T
    same = owner == owner_t
    here, there = iota(square, 0), iota(square, 1)
    rank_row = jnp.sum(jnp.where(same & (here < there), 1.0, 0.0), axis=0, keepdims=True)
    rank_col = jnp.sum(jnp.where(same & (there < here), 1.0, 0.0), axis=1, keepdims=True)
    slot_row = (owner_t[0:1, :] * cap + rank_row).astype(jnp.int32)
    place = (iota((ranks * cap, blocks), 0) == slot_row).astype(jnp.bfloat16)
    for copy in copies[1:]:
        copy.wait()
    cells = jnp.concatenate([cell_ref[:, c * LANES : (c + 1) * LANES] for c in range(columns)], axis=0)
    pixels = (tiles * LANES + cells).astype(jnp.float32)
    phases = jnp.concatenate([phase_ref[:, c * LANES : (c + 1) * LANES] for c in range(columns)], axis=0)
    moved = exact_dot(place, jnp.concatenate([phases, pixels], axis=1))
    slot_phase, slot_pixel = moved[:, :LANES], moved[:, LANES:]
    lane = iota(square, 1)
    small = iota((dets, LANES), 1)
    det_lane = iota((dets, LANES), 0)
    offsets = jnp.broadcast_to(offset_ref[...], (dets, dets))
    diagonal = iota((dets, dets), 0) == iota((dets, dets), 1)
    shift = jnp.sum(jnp.where(diagonal, offsets, 0).astype(jnp.float32), axis=1, keepdims=True)
    shift = jnp.broadcast_to(shift.astype(jnp.int32), (dets, LANES))
    start = jnp.concatenate([c * LANES - shift for c in range(columns)], axis=0) + span * samples
    which = (iota(square, 0) & (dets - 1)) + 1
    rank = rank_col.astype(jnp.int32)
    listing = jnp.where(lane == rank, start, 0) + jnp.where(lane == rank + cap, which, 0)
    listing = listing + jnp.where(lane == rank + 2 * cap, tiles + 1, 0)
    chosen = (iota((ranks, blocks), 0).astype(jnp.float32) == owner_t[0:1, :]).astype(jnp.bfloat16)
    info = exact_dot(chosen, listing.astype(jnp.float32))
    knots = jnp.zeros((1, LANES), jnp.float32)
    for kind, ref in enumerate((search_ref, left_ref)):
        for n in range(nodes):
            column = jnp.broadcast_to(ref[n : n + 1, :], (dets, dets))
            column = jnp.sum(jnp.where(diagonal, column, 0.0), axis=1, keepdims=True)
            at = (3 * cap + kind * dets * nodes + n) + det_lane * nodes
            knots = knots + jnp.sum(jnp.where(small == at, column, 0.0), axis=0, keepdims=True)
    info = info + knots
    for o in range(ranks):
        out_ref[o * rows : o * rows + cap, :] = slot_phase[o * cap : (o + 1) * cap, :]
        out_ref[o * rows + cap : o * rows + 2 * cap, :] = slot_pixel[o * cap : (o + 1) * cap, :]
        out_ref[o * rows + 2 * cap : (o + 1) * rows, :] = info[o : o + 1, :]


def unpack(ranks, cap, ref, phase_ref, cell_ref, info_ref, meta_ref):
    rows = 2 * cap + 1
    for o in range(ranks):
        here = o * cap
        phase_ref[here : here + cap, :] = ref[o * rows : o * rows + cap, :]
        cell_ref[here : here + cap, :] = ref[o * rows + cap : o * rows + 2 * cap, :]
        info = ref[o * rows + 2 * cap : (o + 1) * rows, :]
        info_ref[here : here + cap, :] = jnp.broadcast_to(info, (cap, LANES))
        meta_ref[o : o + 1, :] = info


def rank_slots(ranks, cap, meta_ref):
    lists = []
    spans = LANES // cap
    for k in range(ranks * cap // LANES):
        names = meta_ref[k * spans : (k + 1) * spans, :]
        lane = iota((spans, LANES), 1)
        spread = lane_gather(names, 2 * cap + (lane & (cap - 1)))
        mine = (lane >> log2(cap)) == iota((spans, LANES), 0)
        lists.append(jnp.sum(jnp.where(mine, spread, 0.0), axis=0, keepdims=True))
    names = jnp.concatenate(lists, axis=0).astype(jnp.int32)
    mine = (names > 0) & (((names - 1) & 1) == lax.axis_index("det"))
    ones = jnp.where(mine, 1.0, 0.0)
    earlier = (iota((LANES, LANES), 0) < iota((LANES, LANES), 1)).astype(jnp.bfloat16)
    rank = dot(ones.astype(jnp.bfloat16), earlier)
    sums = jnp.sum(ones, axis=1, keepdims=True)
    before = [jnp.zeros((1, 1), jnp.float32)]
    for k in range(len(lists)):
        before.append(before[-1] + sums[k : k + 1, :])
    rank = rank + jnp.concatenate(before[:-1], axis=0)
    return jnp.where(mine, rank, -1.0).astype(jnp.int32), jnp.sum(ones).astype(jnp.int32)


def flatten(pages, knots):
    dets = pages[0].shape[0]
    if knots >= LANES:
        return [page[d : d + 1, :] for d in range(dets) for page in pages]
    lane, det = iota((dets, LANES), 1), iota((dets, LANES), 0)
    spread = lane_gather(pages[0], lane & (knots - 1))
    per_row = LANES // knots
    mine = (det & (per_row - 1)) == (lane >> log2(knots))
    spread = jnp.where(mine, spread, 0.0)
    rows = []
    for first in range(0, dets, per_row):
        rows.append(jnp.sum(spread[first : first + per_row, :], axis=0, keepdims=True))
    return rows


def read_knots(ranks, cap, dets, nodes, meta_ref):
    width = dets * nodes
    knots = ranks * nodes
    per_row = LANES // width
    kinds = []
    for kind in range(2):
        lines = []
        for p in range(ranks // per_row):
            names = meta_ref[p * per_row : (p + 1) * per_row, :]
            lane = iota((per_row, LANES), 1)
            spread = lane_gather(names, (3 * cap + kind * width) + (lane & (width - 1)))
            here = (lane >> log2(width)) == iota((per_row, LANES), 0)
            lines.append(jnp.sum(jnp.where(here, spread, 0.0), axis=0, keepdims=True))
        lane = iota((dets, LANES), 1)
        tables = []
        for page in range(max(1, knots // LANES)):
            knot = lane + page * LANES
            index = ((knot >> log2(nodes)) & (per_row - 1)) * width
            index = index + iota((dets, LANES), 0) * nodes + (knot & (nodes - 1))
            table = jnp.zeros((dets, LANES), jnp.float32)
            for p, line in enumerate(lines):
                values = lane_gather(jnp.broadcast_to(line, (dets, LANES)), index)
                table = jnp.where((knot >> log2(per_row * nodes)) == p, values, table)
            tables.append(table)
        kinds.append(tables)
    return kinds


def source_of(ranks, cap, dets, total, side, phase_ref, cell_ref, info_ref):
    slots = ranks * cap
    slot = iota((slots, LANES), 0) & (cap - 1)
    lane = iota((slots, LANES), 1)
    listed = lane_gather(info_ref[...], jnp.minimum(lane, 2) * cap + slot)
    listed = listed + jnp.where(lane == 1, (side * dets).astype(jnp.float32), 0.0)
    pixel = cell_ref[...]
    cell = (pixel - jnp.floor(pixel * (1.0 / LANES)) * LANES).astype(jnp.bfloat16)
    whole = split3(listed)
    if max(total, ranks * OWNER_TILES) <= 65536:
        whole = whole[:2]
    return jnp.concatenate(split3(phase_ref[...]) + (cell,) + whole, axis=1)


def take_slots(at, rank, source, dets, side, tables):
    down = iota((BLOCK, LANES), 0) + at
    place = jnp.concatenate(
        [(down == rank[k : k + 1, :]).astype(jnp.bfloat16) for k in range(rank.shape[0])], axis=1
    )
    taken = dot(place, source)
    parts = [taken[:, k * LANES : (k + 1) * LANES] for k in range(taken.shape[1] // LANES)]
    phase = (parts[0] + parts[1]) + parts[2]
    info = sum(parts[5:], parts[4])
    lane = iota((BLOCK, LANES), 1) + (1 + side * dets)
    chosen = ((info[:, 1:2] == lane.astype(jnp.float32)) & (iota((BLOCK, LANES), 1) < dets)).astype(jnp.bfloat16)
    empty = jnp.zeros((LANES - dets, LANES), jnp.float32)
    knots = [exact_dot(chosen, jnp.concatenate([table, empty], axis=0)) for table in tables]
    return phase, parts[3], info, knots


def spline(info_ref, spacing, at, chunk):
    start = jnp.broadcast_to(info_ref[pl.ds(at, chunk), 0:1], (chunk, LANES)).astype(jnp.int32)
    time = start + iota((chunk, LANES), 1)
    interval = time >> log2(spacing)
    fraction = (time & (spacing - 1)).astype(jnp.float32) * (1.0 / spacing)
    return start >> log2(spacing), interval, spline_weights(fraction)


def five_weights(early, weights):
    padded = (0.0,) + weights + (0.0,)
    return [jnp.where(early, padded[term + 1], padded[term]) for term in range(5)]


def binning(knots, spacing, few_phase, few_cell, few_info, table_ref, cos_ref, sin_ref, stream_ref, basis_ref, bin_ref):
    pages = table_ref.shape[0]

    def prepare(step):
        at = aligned(step * COLLECT, COLLECT)
        cosine, sine = cos_sin(2.0 * few_phase[pl.ds(at, COLLECT), :])
        base, interval, weights = spline(few_info, spacing, at, COLLECT)
        for term, weight in enumerate(five_weights(interval == base, weights)):
            basis_ref[term, pl.ds(at, COLLECT), :] = weight
        stream = jnp.zeros((COLLECT, LANES), jnp.float32)
        for term in range(4):
            knot = (interval + (term - 1)) & (knots - 1)
            value = lane_gather(table_ref[0, pl.ds(at, COLLECT), :], knot & (LANES - 1))
            for page in range(1, pages):
                more = lane_gather(table_ref[page, pl.ds(at, COLLECT), :], knot & (LANES - 1))
                value = jnp.where((knot >> log2(LANES)) == page, more, value)
            stream = stream + weights[term] * value
        cos_ref[pl.ds(at, COLLECT), :] = cosine
        sin_ref[pl.ds(at, COLLECT), :] = sine
        stream_ref[pl.ds(at, COLLECT), :] = stream

    down = iota((LANES, 2 * LANES), 0).astype(jnp.int8)
    channel = iota((CHANNELS, LANES), 0)
    zeros = jnp.zeros((2 * CHANNELS, LANES), jnp.bfloat16)

    def collect(step):
        for k in range(COLLECT // 2):
            at = step * COLLECT + 2 * k
            pieces, cells = [], []
            for slot in (at, at + 1):
                stream = jnp.broadcast_to(stream_ref[pl.ds(slot, 1), :], (CHANNELS, LANES))
                cosine = jnp.broadcast_to(cos_ref[pl.ds(slot, 1), :], (CHANNELS, LANES))
                sine = jnp.broadcast_to(sin_ref[pl.ds(slot, 1), :], (CHANNELS, LANES))
                left = jnp.where(channel < 3, stream, jnp.where(channel < 6, 1.0, cosine))
                is_one = (channel == 0) | (channel == 3)
                is_sine = (channel == 2) | (channel == 5) | (channel == 7)
                right = jnp.where(is_one, 1.0, jnp.where(is_sine, sine, cosine))
                entry = left * right
                high = entry.astype(jnp.bfloat16).astype(jnp.float32)
                rest = entry - high
                stack = jnp.concatenate([high, rest], axis=0)
                pieces.append(stack.astype(jnp.bfloat16))
                cells.append(jnp.broadcast_to(few_cell[pl.ds(slot, 1), :].astype(jnp.int32).astype(jnp.int8), (LANES, LANES)))
            entry = jnp.concatenate(
                [
                    jnp.concatenate([pieces[0], zeros], axis=1),
                    jnp.concatenate([zeros, pieces[1]], axis=1),
                ],
                axis=0,
            )
            hits = jnp.where(jnp.concatenate(cells, axis=1) == down, jnp.int8(1), jnp.int8(0))
            sums = dot(entry, hits.T.astype(jnp.bfloat16))
            for m in range(2):
                base = 2 * CHANNELS * m
                bin_ref[pl.ds((at + m) * CHANNELS, CHANNELS), :] = (
                    sums[base : base + CHANNELS] + sums[base + CHANNELS : base + 2 * CHANNELS]
                )

    def both(step, carry):
        collect(step)
        prepare(step + 1)
        return carry

    return prepare, both


def own_kernel(
    ranks, cap, dets, nodes, spacing, own_ref,
    few_phase, few_cell, few_info, table_ref, cos_ref, sin_ref, stream_ref, basis_ref, bin_ref, packs_ref, count_ref,
    phase_ref, cell_ref, info_ref, meta_ref,
):
    knots = ranks * nodes
    side = lax.axis_index("det")
    unpack(ranks, cap, own_ref, phase_ref, cell_ref, info_ref, meta_ref)
    rank, number = rank_slots(ranks, cap, meta_ref)
    count_ref[...] = jnp.full((8, LANES), number, jnp.int32)
    tables, left = read_knots(ranks, cap, dets, nodes, meta_ref)
    packs_ref[...] = jnp.concatenate(flatten(tables, knots) + flatten(left, knots), axis=0)
    source = source_of(ranks, cap, dets, knots * spacing, side, phase_ref, cell_ref, info_ref)

    def gather_block(block, carry):
        here = pl.ds(aligned(block * BLOCK, 16), BLOCK)
        few_phase[here, :], few_cell[here, :], few_info[here, :], found = take_slots(
            block * BLOCK, rank, source, dets, side, tables
        )
        for page, rows in enumerate(found):
            table_ref[page, here, :] = rows
        return carry

    prepare, both = binning(
        knots, spacing, few_phase, few_cell, few_info, table_ref,
        cos_ref, sin_ref, stream_ref, basis_ref, bin_ref,
    )
    gather_block(0, 0)
    prepare(0)
    room = pl.cdiv(BLOCK, COLLECT) * COLLECT * CHANNELS
    bin_ref[0:room, :] = jnp.zeros((room, LANES), jnp.float32)
    lax.fori_loop(1, block_count(number, ranks * cap), gather_block, 0)
    lax.fori_loop(0, number >> log2(COLLECT), both, 0)


def block_count(number, most):
    return sum(jnp.where(number > start, 1, 0) for start in range(0, most, BLOCK))


def main_kernel(
    ranks, cap, dets, nodes, spacing, other_ref, coeffs_hbm, packs_own, count_ref, *refs,
):
    few_phase, few_cell, few_info, table_ref, cos_ref, sin_ref, stream_ref, basis_ref, bin_ref = refs[9:18]
    out_ref, packs_ref, coeffs_ref = refs[18:21]
    phase_ref, cell_ref, info_ref, meta_ref, total_ref, turned_ref, knots_ref, sems = refs[21:]
    coeffs_copy = pltpu.make_async_copy(coeffs_hbm, coeffs_ref, sems.at[0])
    coeffs_copy.start()
    slots = ranks * cap
    knots = ranks * nodes
    packed = knots * dets // LANES
    group = lax.axis_index("det")
    side = 1 - group

    unpack(ranks, cap, other_ref, phase_ref, cell_ref, info_ref, meta_ref)
    rank, more = rank_slots(ranks, cap, meta_ref)
    ready = jnp.max(count_ref[...])
    rank = jnp.where(rank >= 0, rank + ready, -1)
    number = ready + more
    tables, left = read_knots(ranks, cap, dets, nodes, meta_ref)
    for kind, pages in enumerate((tables, left)):
        here = slice(kind * packed, (kind + 1) * packed)
        packs_ref[kind, pl.ds(group * packed, packed), :] = packs_own[here, :]
        packs_ref[kind, pl.ds(side * packed, packed), :] = jnp.concatenate(flatten(pages, knots), axis=0)
    source = source_of(ranks, cap, dets, knots * spacing, side, phase_ref, cell_ref, info_ref)
    blocks = block_count(number, 2 * slots)
    ready_blocks = block_count(ready, slots)

    def gather_block(block, carry):
        here = pl.ds(aligned(block * BLOCK, 16), BLOCK)
        def before(rows):
            return rows if isinstance(block, int) else jnp.where(block < ready_blocks, rows, 0.0)

        phase, cell, info, found = take_slots(block * BLOCK, rank, source, dets, side, tables)
        few_phase[here, :] = before(few_phase[here, :]) + phase
        few_cell[here, :] = before(few_cell[here, :]) + cell
        info = before(few_info[here, :]) + info
        few_info[here, :] = info
        turned = info.T
        turned_ref[0, pl.ds(block, 1), :] = turned[1:2, :]
        turned_ref[1, pl.ds(block, 1), :] = turned[2:3, :]
        for page, rows in enumerate(found):
            table_ref[page, here, :] = before(table_ref[page, here, :]) + rows
        return carry

    prepare, both = binning(
        knots, spacing, few_phase, few_cell, few_info, table_ref,
        cos_ref, sin_ref, stream_ref, basis_ref, bin_ref,
    )
    first, last = ready >> log2(COLLECT), (number + (COLLECT - 1)) >> log2(COLLECT)

    def clear(step, carry):
        at = pl.multiple_of(step * COLLECT * CHANNELS, COLLECT * CHANNELS)
        bin_ref[pl.ds(at, COLLECT * CHANNELS), :] = jnp.zeros((COLLECT * CHANNELS, LANES), jnp.float32)
        return carry

    gather_block(0, 0)
    prepare(first)

    @pl.when(blocks > 1)
    def _():
        lax.fori_loop(1, blocks, gather_block, 0)
        lax.fori_loop(last, (blocks * BLOCK + (COLLECT - 1)) >> log2(COLLECT), clear, 0)
        prepare(first)

    lax.fori_loop(first, last, both, 0)

    def merge(block, carry):
        at = aligned(block * BLOCK, 16)
        names = few_info[pl.ds(at, BLOCK), 2:3]

        def add(other, carry):
            there = aligned(other * BLOCK, 16)
            same = (names == turned_ref[1, pl.ds(other, 1), :]).astype(jnp.bfloat16)
            for c in range(CHANNELS):
                binned = bin_ref[pl.ds(there * CHANNELS + c, BLOCK, stride=CHANNELS), :]
                high = binned.astype(jnp.bfloat16)
                if c == COUNT:
                    share = dot(same, high)
                else:
                    low = (binned - high.astype(jnp.float32)).astype(jnp.bfloat16)
                    share = dot(same, jnp.concatenate([high, low], axis=1))
                    share = share[:, :LANES] + share[:, LANES:]
                if not isinstance(other, int):
                    share = share + total_ref[c, pl.ds(at, BLOCK), :]
                total_ref[c, pl.ds(at, BLOCK), :] = share
            return carry

        add(0, 0)
        if not isinstance(block, int):
            lax.fori_loop(1, blocks, add, 0)
        return carry

    def project(at, size):
        here = pl.ds(aligned(at, 16), size)
        signal, signal_cos, signal_sin, count, cos_sum, sin_sum, cos_cos, cos_sin_sum = (
            total_ref[c, here, :] for c in range(CHANNELS)
        )
        sin_sin = count - cos_cos
        stokes_i = count + MAP_PRIOR
        stokes_q = cos_cos + MAP_PRIOR
        stokes_u = sin_sin + MAP_PRIOR
        minor_one = stokes_q * stokes_u - cos_sin_sum * cos_sin_sum
        minor_two = sin_sum * cos_sin_sum - cos_sum * stokes_u
        minor_three = cos_sum * cos_sin_sum - sin_sum * stokes_q
        minor_four = stokes_i * stokes_u - sin_sum * sin_sum
        minor_five = cos_sum * sin_sum - stokes_i * cos_sin_sum
        minor_six = stokes_i * stokes_q - cos_sum * cos_sum
        determinant = stokes_i * minor_one + cos_sum * minor_two + sin_sum * minor_three
        scale = 1.0 / determinant
        map_i = (minor_one * signal + minor_two * signal_cos + minor_three * signal_sin) * scale
        map_q = (minor_two * signal + minor_four * signal_cos + minor_five * signal_sin) * scale
        map_u = (minor_three * signal + minor_five * signal_cos + minor_six * signal_sin) * scale
        cell = few_cell[here, :].astype(jnp.int32)
        projected = (
            lane_gather(map_i, cell) + cos_ref[here, :] * lane_gather(map_q, cell)
        ) + sin_ref[here, :] * lane_gather(map_u, cell)
        cleaned = stream_ref[here, :] - projected
        valid = few_info[here, 1:2] > 0.5
        base = few_info[here, 0:1].astype(jnp.int32) >> log2(spacing)
        lane = iota((size, LANES), 1)
        pages = [jnp.zeros((size, LANES), jnp.float32) for _ in range(knots_ref.shape[0])]
        for term in range(5):
            value = basis_ref[term, here, :] * cleaned
            high = value.astype(jnp.bfloat16)
            low = (value - high.astype(jnp.float32)).astype(jnp.bfloat16)
            value = dot(jnp.concatenate([high, low], axis=1), jnp.ones((2 * LANES, LANES), jnp.bfloat16))
            knot = (base + (term - 1)) & (knots - 1)
            for page in range(len(pages)):
                pages[page] = pages[page] + jnp.where(lane + page * LANES == knot, value, 0.0)
        for page, sums in enumerate(pages):
            knots_ref[page, here, :] = jnp.where(valid, sums, 0.0)

    def image_of(block, sums):
        at = aligned(block * BLOCK, 16)
        for first in range(0, BLOCK, PROJECT):
            project(at + first, min(PROJECT, BLOCK - first))
        det = (iota((2 * dets, BLOCK), 0) + 1).astype(jnp.float32)
        chosen = (turned_ref[0, pl.ds(block, 1), :] == det).astype(jnp.bfloat16)
        return tuple(
            total + exact_dot(chosen, knots_ref[page, pl.ds(at, BLOCK), :]) for page, total in enumerate(sums)
        )

    def write(image):
        partial = jnp.concatenate(flatten(image, knots), axis=0)
        for target in range(out_ref.shape[0] // (2 * packed)):
            out_ref[target * 2 * packed : (target + 1) * 2 * packed, :] = partial

    zero = tuple(jnp.zeros((2 * dets, LANES), jnp.float32) for _ in range(knots_ref.shape[0]))
    merge(0, 0)
    write(image_of(0, zero))

    @pl.when(blocks > 1)
    def _():
        lax.fori_loop(0, blocks, merge, 0)
        write(lax.fori_loop(0, blocks, image_of, zero))

    coeffs_copy.wait()


def finish_kernel(
    ranks, spacing, arrived_ref, packs_ref, coeffs_ref, new_offset_ref, new_left_ref, new_search_ref,
):
    nodes, dets = coeffs_ref.shape
    height = packs_ref.shape[1]
    total = arrived_ref[0:height, :]
    for o in range(1, arrived_ref.shape[0] // height):
        total = total + arrived_ref[o * height : (o + 1) * height, :]
    search, left = packs_ref[0], packs_ref[1]
    image = total * (1.0 / spacing) + BASE_PRIOR * search
    norm_old = jnp.sum(left * left, keepdims=True)
    stride_factor = norm_old / jnp.sum(search * image, keepdims=True)
    fresh = left - stride_factor * image
    beta = jnp.sum(fresh * fresh, keepdims=True) / norm_old
    span, group = lax.axis_index("tm"), lax.axis_index("det")
    lines = height // 2
    knots = lines * LANES // dets
    place = (iota((8, LANES), 1) & (dets - 1)) * knots + span * nodes + (iota((8, LANES), 0) & (nodes - 1))

    def own(x):
        x = jnp.where(group == 0, x[:lines, :], x[lines:, :])
        found = jnp.zeros((8, LANES), jnp.float32)
        for p in range(lines):
            values = lane_gather(jnp.broadcast_to(x[p : p + 1, :], (8, LANES)), place & (LANES - 1))
            found = jnp.where((place >> log2(LANES)) == p, values, found)
        return found[:nodes, :dets]

    my_search = own(search)
    my_left = own(fresh)
    new_offset_ref[...] = coeffs_ref[...] + stride_factor * my_search
    new_left_ref[...] = my_left
    new_search_ref[...] = my_left + beta * my_search


def body(
    offset_coeffs,
    leftover_error,
    search_vector,
    node_lattice_offset,
    sky_cell_in_patch,
    analyser_reading_phase,
    segment_sky_patch,
):
    ranks, groups = lax.axis_size("tm"), lax.axis_size("det")
    dets, samples = analyser_reading_phase.shape
    nodes = search_vector.shape[1]
    spacing = samples // nodes
    blocks = segment_sky_patch.size
    cap = max(2, 2 * blocks // ranks)
    slots = ranks * cap
    rows = 2 * cap + 1
    height = groups * ranks * nodes * dets // LANES
    vmem = pl.BlockSpec(memory_space=pltpu.VMEM)
    hbm = pl.BlockSpec(memory_space=pltpu.HBM)
    pin = functools.partial(pltpu.with_memory_space_constraint, memory_space=pltpu.HBM)
    params = pltpu.CompilerParams(vmem_limit_bytes=VMEM_BYTES)
    inputs = (
        segment_sky_patch, node_lattice_offset.reshape(1, dets), search_vector.T, leftover_error.T,
        sky_cell_in_patch, analyser_reading_phase,
    )
    small = jax.ShapeDtypeStruct((nodes, dets), jnp.float32)

    outgoing = pl.pallas_call(
        functools.partial(send_kernel, ranks, cap),
        out_shape=jax.ShapeDtypeStruct((ranks * rows, LANES), jnp.float32),
        in_specs=[hbm] * len(inputs),
        out_specs=vmem,
        scratch_shapes=[pltpu.VMEM(x.shape, x.dtype) for x in inputs]
        + [pltpu.SemaphoreType.DMA((len(inputs),))],
        compiler_params=params,
        name="send",
    )(*[pin(x) for x in inputs])
    arrived = lax.all_to_all(
        outgoing.reshape(ranks, 1, rows * LANES), "tm", split_axis=0, concat_axis=0, tiled=True
    )
    swap = [(i, groups - 1 - i) for i in range(groups)]
    other = lax.ppermute(arrived, "det", swap)
    pages = max(1, ranks * nodes // LANES)
    f32 = jnp.float32
    room = pl.cdiv(2 * slots, BLOCK) * BLOCK + max(COLLECT, PROJECT)
    few = jax.ShapeDtypeStruct((room, LANES), f32)
    shared = (
        few, few, few, jax.ShapeDtypeStruct((pages, room, LANES), f32), few, few, few,
        jax.ShapeDtypeStruct((5, room, LANES), f32),
        jax.ShapeDtypeStruct((room * CHANNELS, LANES), f32),
    )
    arrival = [pltpu.VMEM((slots, LANES), f32)] * 3 + [pltpu.VMEM((ranks, LANES), f32)]
    sizes = (ranks, cap, dets, nodes, spacing)
    *state, packs, count = pl.pallas_call(
        functools.partial(own_kernel, *sizes),
        out_shape=shared + (
            jax.ShapeDtypeStruct((2 * height // groups, LANES), f32),
            jax.ShapeDtypeStruct((8, LANES), jnp.int32),
        ),
        in_specs=[vmem],
        out_specs=(vmem,) * 11,
        scratch_shapes=arrival,
        compiler_params=params,
        cost_estimate=pl.CostEstimate(flops=4_000_000_000, bytes_accessed=4_000_000, transcendentals=0),
        name="own",
    )(arrived.reshape(ranks * rows, LANES))
    *_, partials, packs, coeffs = pl.pallas_call(
        functools.partial(main_kernel, *sizes),
        out_shape=shared + (
            jax.ShapeDtypeStruct((ranks * groups * height, LANES), f32),
            jax.ShapeDtypeStruct((2, height, LANES), f32),
            small,
        ),
        in_specs=[vmem, hbm] + [vmem] * 11,
        out_specs=(vmem,) * 12,
        scratch_shapes=arrival + [
            pltpu.VMEM((CHANNELS, room, LANES), f32),
            pltpu.VMEM((2, 8, BLOCK), f32),
            pltpu.VMEM((pages, room, LANES), f32),
            pltpu.SemaphoreType.DMA((1,)),
        ],
        input_output_aliases={4 + k: k for k in range(9)},
        compiler_params=params,
        name="main",
    )(other.reshape(ranks * rows, LANES), pin(offset_coeffs.T), packs, count, *state)
    gathered = lax.all_to_all(
        partials.reshape(ranks * groups, 1, height * LANES),
        ("tm", "det"), split_axis=0, concat_axis=0, tiled=True,
    )
    results = pl.pallas_call(
        functools.partial(finish_kernel, ranks, spacing),
        out_shape=(small, small, small),
        in_specs=[vmem] * 3,
        out_specs=(vmem, vmem, vmem),
        compiler_params=params,
        name="finish",
    )(gathered.reshape(ranks * groups * height, LANES), packs, coeffs)
    return tuple(result.T for result in results)


def solution(mesh):
    return jax.shard_map(
        body,
        mesh=mesh,
        in_specs=(
            P("det", "tm"),
            P("det", "tm"),
            P("det", "tm"),
            P("det"),
            P("det", "tm"),
            P("det", "tm"),
            P("det", "tm"),
        ),
        out_specs=(P("det", "tm"), P("det", "tm"), P("det", "tm")),
        check_vma=False,
    )
```
